128 devices in a mesh: pts: 16 (over x, y), cams: 8 (over z, core).
Axes of the slice: x: 4, y: 4, z: 4, core: 2. Of those that a mesh axis runs over, the one named last changes fastest.
Arguments:
- cam_jac: float32 [2, 4, 9, 32768], P(None, None, None, 'pts'), may hold values from -0.375 to 0.375
- pt_jac: float32 [2, 4, 3, 32768], P(None, None, None, 'pts'), may hold values from -6 to 6
- resid: float32 [2, 4, 32768], P(None, None, 'pts'), may hold values from -6 to 6
- point_damping: float32 [32768], P('pts'), may hold values from 0.2 to 2
- obs_camera: int32 [4, 32768], P(None, 'pts'), may hold values from 0 to 1023, as said below
- members: int32 [16, 8, 512], P('pts', 'cams'), may hold values from 0 to 2047, as said below
- partners: int32 [8, 2], replicated, may hold values from 0 to 7, as said below
- camera_damping: float32 [8, 1152], P('cams', 'pts'), may hold values from 0.5 to 4
Outputs:
- slab: float32 [8, 1152, 3456], P('cams', 'pts')
- solution: float32 [8, 1152], P('cams', 'pts')
- residual: float32 [8, 1152], P('cams', 'pts')
The draws below stay inside these ranges and needn't reach their ends.
Inputs may be any that keep to these rules, and one draw needn't show every extreme that they name: `obs_camera`: camera id = cluster * 128 + camera within the cluster. The first 2 observations of a point lie in one cluster and the others in a partner of it; the point is listed in members for exactly those two clusters. members[b, c] holds 512 distinct numbers of points within block b (0 to 2047); each point of a block is listed for exactly two clusters, which are partners of each other. The clusters form one cycle: partners[c] are the two clusters next to c on it, in either order, distinct and other than c, so c is named in the rows of both.
All inputs are finite; a program needn't handle non-finite values.
Results may differ from the reference program's by a relative error of at most 0.0003.
Values sent between devices are 32-bit elements; how exact they have to be, the bound alone decides.
No kernel may reach another device: no remote copies, remote signals or barrier semaphores. Data moves between devices by JAX's collectives and lax.ppermute only.
A program may use at most 576 MiB of HBM per device.

```python
import math
import jax
import jax.numpy as jnp
from jax import lax

CP = 9
CAMS_CL = 128
K = 4
MEM = 512
ITERS = 2
W = 1152
NCL = 8
SHARDS = 16
P_SH = 2048
NPTS = 32768


def layout(key):
    order = jax.random.permutation(jax.random.fold_in(key, 101), NCL).astype(jnp.int32)
    shard_keys = jax.random.split(jax.random.fold_in(key, 102), SHARDS)
    placing = jax.vmap(lambda sub: jax.random.permutation(sub, P_SH))(shard_keys).astype(jnp.int32)
    return (order, placing)


def draw_partners(key, part):
    order, placing = layout(key)
    where = jnp.argsort(order, stable=True).astype(jnp.int32)
    before = order[(where - 1) % NCL]
    after = order[(where + 1) % NCL]
    flips = jax.random.randint(jax.random.fold_in(key, 103), (NCL,), 0, 2) == 1
    first = jnp.where(flips, after, before)
    second = jnp.where(flips, before, after)
    return jnp.stack([first, second], axis=1).astype(jnp.int32)


def draw_members(key, part):
    order, placing = layout(key)
    where = jnp.argsort(order, stable=True).astype(jnp.int32)
    half = MEM // 2
    steps = jnp.arange(half, dtype=jnp.int32)[None, :]
    lower = ((where - 1) % NCL)[:, None] * half + steps
    upper = where[:, None] * half + steps
    slots = jnp.concatenate([lower, upper], axis=1)
    return placing[:, slots].astype(jnp.int32)


def draw_obs_camera(key, part):
    order, placing = layout(key)
    key = jax.random.fold_in(key, 7)
    half = MEM // 2
    numbers = jax.vmap(lambda row: jnp.argsort(row, stable=True))(placing).astype(jnp.int32)
    edge = numbers // half
    home = order[edge]
    other = order[(edge + 1) % NCL]
    which = jnp.arange(K, dtype=jnp.int32)[:, None, None] < K // 2
    cluster = jnp.where(which, home[None], other[None])
    picks = jax.random.randint(key, (K, SHARDS, P_SH), 0, CAMS_CL)
    return (cluster * CAMS_CL + picks).reshape(K, NPTS).astype(jnp.int32)


def shard_levels(key, dims, cuts, smallest, largest):
    level, own = 1.0, jax.random.fold_in(key, 6)
    for position, shards_of in cuts:
        heights = jnp.exp(jax.random.uniform(jax.random.fold_in(own, position), (shards_of,), jnp.float32, smallest / len(cuts), largest / len(cuts)))
        level = level * jnp.repeat(heights, dims[position] // shards_of).reshape([-1 if axis == position else 1 for axis in range(len(dims))])
    return level


def bell_draw(key, shape, scale, limit, cuts=(), held_as=jnp.bfloat16):
    gain = shard_levels(key, shape, cuts, -0.22, 0.18) if cuts else 1.0
    values = jax.random.normal(key, shape, jnp.float32) * scale * gain
    return jnp.minimum(jnp.maximum(values, -limit), limit).astype(held_as)


def setup_inputs(seed: int = 0) -> dict:
    seeds = jax.random.split(jax.random.key(seed), 9)
    cam_jac = bell_draw(seeds[0], (2, K, CP, NPTS), (MEM * K * SHARDS // CAMS_CL) ** -0.5, 0.375, ((3, 16),), jnp.float32)
    pt_jac = bell_draw(seeds[1], (2, K, 3, NPTS), 1.0, 6.0, ((3, 16),), jnp.float32)
    resid = bell_draw(seeds[2], (2, K, NPTS), 1.0, 6.0, ((2, 16),), jnp.float32)
    point_damping = jnp.clip(jnp.exp(math.log(2.0) - 2.3025851 * jax.random.uniform(seeds[3], (NPTS,), jnp.float32) ** shard_levels(seeds[3], (NPTS,), ((0, 16),), -0.2, 0.2)), 0.2, 2.0)
    obs_camera = draw_obs_camera(jax.random.fold_in(seeds[8], 71), 0)
    members = draw_members(jax.random.fold_in(seeds[8], 71), 0)
    partners = draw_partners(jax.random.fold_in(seeds[8], 71), 0)
    camera_damping = jnp.clip(jnp.exp(math.log(4.0) - 2.0794415 * jax.random.uniform(seeds[7], (NCL, W), jnp.float32) ** shard_levels(seeds[7], (NCL, W), ((0, 8), (1, 16)), -0.2, 0.2)), 0.5, 4.0)
    return dict(cam_jac=cam_jac, pt_jac=pt_jac, resid=resid, point_damping=point_damping, obs_camera=obs_camera, members=members, partners=partners, camera_damping=camera_damping)


HIGH = lax.Precision.HIGHEST

def member_terms(cam_jac, pt_jac, resid, damping, cameras, blocks):
    count = cam_jac.shape[3]
    cluster = cameras // CAMS_CL
    place = jnp.where(cluster == blocks[0], 0, jnp.where(cluster == blocks[1], 1, 2))
    column = (place * CAMS_CL + cameras % CAMS_CL).astype(jnp.int32)
    onehot = (column[:, :, None] == jnp.arange(3 * CAMS_CL, dtype=jnp.int32)[None, None, :]).astype(jnp.float32)
    cross = jnp.einsum('akim,akem->kiem', pt_jac, cam_jac, precision=HIGH)
    coupled = jnp.einsum('kmc,kiem->imce', onehot, cross, precision=HIGH).reshape(3, count, 3 * CAMS_CL * CP)
    normal = jnp.einsum('akim,akjm->ijm', pt_jac, pt_jac, precision=HIGH)
    pulled = jnp.einsum('akim,akm->im', pt_jac, resid, precision=HIGH)
    l00 = jnp.sqrt(normal[0, 0] + damping)
    l10 = normal[1, 0] / l00
    l20 = normal[2, 0] / l00
    l11 = jnp.sqrt(normal[1, 1] + damping - l10 * l10)
    l21 = (normal[2, 1] - l20 * l10) / l11
    l22 = jnp.sqrt(normal[2, 2] + damping - l20 * l20 - l21 * l21)
    first = coupled[0] / l00[:, None]
    second = (coupled[1] - l10[:, None] * first) / l11[:, None]
    third = (coupled[2] - l20[:, None] * first - l21[:, None] * second) / l22[:, None]
    reduced = jnp.concatenate([first, second, third], axis=0)
    wfirst = pulled[0] / l00
    wsecond = (pulled[1] - l10 * wfirst) / l11
    wthird = (pulled[2] - l20 * wfirst - l21 * wsecond) / l22
    weights = jnp.concatenate([wfirst, wsecond, wthird], axis=0)
    home = onehot[:, :, :CAMS_CL]
    outer = jnp.einsum('akem,akfm->kmef', cam_jac, cam_jac, precision=HIGH)
    camera_sum = jnp.einsum('kmc,kmef->cef', home, outer, precision=HIGH).reshape(CAMS_CL, CP * CP)
    pulled_cam = jnp.einsum('akem,akm->kme', cam_jac, resid, precision=HIGH)
    camera_pull = jnp.einsum('kmc,kme->ce', home, pulled_cam, precision=HIGH).reshape(CAMS_CL * CP)
    return (reduced, weights, camera_sum, camera_pull)

def reference(cam_jac, pt_jac, resid, point_damping, obs_camera, members, partners, camera_damping):
    width = CP * CAMS_CL

    def one_cluster(cluster):
        blocks = jnp.concatenate([cluster[None], partners[cluster]]).astype(jnp.int32)

        def one_shard(totals, shard):
            index = (shard * P_SH + members[shard, cluster]).astype(jnp.int32)
            reduced, weights, camera_sum, camera_pull = member_terms(cam_jac[..., index], pt_jac[..., index], resid[..., index], point_damping[index], obs_camera[:, index], blocks)
            left = reduced[:, :width]
            coupling = totals[0] - jnp.dot(left.T, reduced, precision=HIGH, preferred_element_type=jnp.float32)
            pull = camera_pull - jnp.dot(weights, left, precision=HIGH, preferred_element_type=jnp.float32)
            return ((coupling, totals[1] + camera_sum, totals[2] + pull), None)
        init = (jnp.zeros((width, 3 * width), jnp.float32), jnp.zeros((CAMS_CL, CP * CP), jnp.float32), jnp.zeros((width,), jnp.float32))
        (coupling, camera_sum, rhs), _ = lax.scan(one_shard, init, jnp.arange(SHARDS, dtype=jnp.int32))
        placed = jnp.einsum('cef,cd->cedf', camera_sum.reshape(CAMS_CL, CP, CP), jnp.eye(CAMS_CL, dtype=jnp.float32), precision=HIGH).reshape(width, width)
        square = coupling[:, :width] + (placed + jnp.diag(camera_damping[cluster]))
        return (jnp.concatenate([square, coupling[:, width:]], axis=1), rhs)
    slab, rhs = lax.map(one_cluster, jnp.arange(NCL, dtype=jnp.int32))
    dinv = jnp.diagonal(slab[:, :, :width], axis1=1, axis2=2)

    def apply(vector):
        picked = jnp.concatenate([vector[:, None, :], vector[partners]], axis=1).reshape(NCL, 3 * width)
        return jnp.einsum('cij,cj->ci', slab, picked, precision=HIGH)
    solution = jnp.zeros((NCL, width), jnp.float32)
    residual = rhs
    precond = residual / dinv
    direction = precond
    norm_now = jnp.sum(residual * precond)
    for step in range(ITERS):
        image = apply(direction)
        alpha = norm_now / jnp.sum(direction * image)
        solution = solution + alpha * direction
        residual = residual - alpha * image
        precond = residual / dinv
        norm_next = jnp.sum(residual * precond)
        direction = precond + norm_next / norm_now * direction
        norm_now = norm_next
    return (slab, solution, residual)
```

```python
import functools

import jax
import jax.numpy as jnp
from jax import lax
from jax.experimental import pallas as pl
from jax.experimental.pallas import tpu as pltpu
from jax.sharding import PartitionSpec as P

CP = 9
CAMS_CL = 128
NCL = 8
SHARDS = 16
P_SH = 2048
MEM = 512
ROWS = 72
GROUP = 8
WIDTH = CP * CAMS_CL
SLOTS = 128
FEAT = 112
PAYLOAD = 176
CHUNK = 256

HIGH = lax.Precision.HIGHEST
BF16 = jnp.bfloat16
F32 = jnp.float32
PARAMS = pltpu.CompilerParams(vmem_limit_bytes=48 * 1024 * 1024)
NN = (((1,), (0,)), ((), ()))
NT = (((1,), (1,)), ((), ()))


def iota(shape, axis):
    return lax.broadcasted_iota(jnp.int32, shape, axis)


def ninth(value):
    return (value * 57) >> 9


def split2(value):
    high = value.astype(BF16).astype(F32)
    return jnp.concatenate([high, value - high], axis=0).astype(BF16)


def dot(a, b, dims):
    return lax.dot_general(a, b, dims, preferred_element_type=F32)


def dot_high(a, b):
    return lax.dot_general(a, b, NN, precision=HIGH, preferred_element_type=F32)


def prepare_kernel(
    partners_ref, cam_ref, pt_ref, resid_ref, damp_ref, ids_ref, members_ref,
    y_ref, part_ref, camsum_ref, p_s, x_s, a_s, f_s,
):
    cluster = lax.axis_index("cams")
    blocks = [cluster, partners_ref[cluster, 0], partners_ref[cluster, 1]]
    for a in range(2):
        for k in range(4):
            for i in range(3):
                p_s[i, a * 4 + k : a * 4 + k + 1, :] = pt_ref[a, k, i : i + 1, :]
        p_s[3, a * 4 : a * 4 + 4, :] = resid_ref[a]
    x_s[148:160, :] = jnp.zeros((12, P_SH), F32)
    a_s[:, 48:64, :] = jnp.zeros((4, 16, P_SH), F32)

    def chunk(step, carry):
        at = pl.ds(pl.multiple_of(step * CHUNK, CHUNK), CHUNK)
        p0, p1, p2, res = (p_s[i, :, at] for i in range(4))
        damp = damp_ref[:, at]

        def total(x):
            return jnp.sum(x, axis=0, keepdims=True)

        i00 = 1.0 / jnp.sqrt(total(p0 * p0) + damp)
        l10 = total(p0 * p1) * i00
        l20 = total(p0 * p2) * i00
        i11 = 1.0 / jnp.sqrt(total(p1 * p1) + damp - l10 * l10)
        l21 = (total(p1 * p2) - l20 * l10) * i11
        i22 = 1.0 / jnp.sqrt(total(p2 * p2) + damp - l20 * l20 - l21 * l21)
        b0 = p0 * i00
        b1 = (p1 - l10 * b0) * i11
        b2 = (p2 - l20 * b0 - l21 * b1) * i22
        b = [b0, b1, b2]
        w = [total(x * res) for x in b]
        jac = [[cam_ref[a, k, :, at] for k in range(4)] for a in range(2)]
        red = [
            [b[i][k : k + 1] * jac[0][k] + b[i][4 + k : 5 + k] * jac[1][k] for k in range(4)]
            for i in range(3)
        ]
        ids = [ids_ref[k : k + 1, at] for k in range(4)]
        homes = [jnp.broadcast_to(ids[k] >> 7, (CP, CHUNK)) for k in (0, 2)]
        same = [
            jnp.broadcast_to(ids[k], (CP, CHUNK)) == jnp.broadcast_to(ids[k + 1], (CP, CHUNK))
            for k in (0, 2)
        ]
        for pair in range(2):
            ka, kb = 2 * pair, 2 * pair + 1
            both = red[0][ka] * red[0][kb] + red[1][ka] * red[1][kb] + red[2][ka] * red[2][kb]
            both = jnp.where(same[pair], both, 0.0)
            for k in (ka, kb):
                j0, j1 = jac[0][k], jac[1][k]
                r0, r1, r2 = red[0][k], red[1][k], red[2][k]
                rhs = j0 * res[k : k + 1] + j1 * res[4 + k : 5 + k] - (r0 * w[0] + r1 * w[1] + r2 * w[2])
                diag = j0 * j0 + j1 * j1 - (r0 * r0 + r1 * r1 + r2 * r2) - both
                for s in range(3):
                    here = homes[pair] == blocks[s]
                    a_s[k, 18 * s : 18 * s + 9, at] = jnp.where(here, rhs, 0.0)
                    a_s[k, 18 * s + 9 : 18 * s + 18, at] = jnp.where(here, diag, 0.0)
        swap = homes[0] != cluster
        for q in range(2):
            for i in range(3):
                row = 9 * (2 * i + q)
                x_s[row : row + 9, at] = jnp.where(swap, red[i][2 + q], red[i][q])
                x_s[54 + row : 63 + row, at] = jnp.where(swap, red[i][q], red[i][2 + q])
            for a in range(2):
                row = 112 + 9 * (2 * a + q)
                x_s[row : row + 9, at] = jnp.where(swap, jac[a][2 + q], jac[a][q])
            swap1 = (ids[0] >> 7) != cluster
            own = jnp.where(swap1, ids[2 + q], ids[q])
            other = jnp.where(swap1, ids[q], ids[2 + q])
            x_s[108 + q : 109 + q, at] = (own & 127).astype(F32)
            place = jnp.where((other >> 7) == blocks[1], 0, CAMS_CL)
            x_s[110 + q : 111 + q, at] = ((other & 127) + place).astype(F32)
        return carry

    lax.fori_loop(0, P_SH // CHUNK, chunk, 0)

    picked = (iota((P_SH, MEM), 0) == members_ref[0]).astype(F32).astype(BF16)
    y = dot(split2(x_s[...]), picked, NN)
    y_ref[...] = y[:160] + y[160:]

    part = jnp.zeros((128, CAMS_CL), F32)
    for k in range(4):
        cams = ids_ref[k : k + 1, :] & 127
        onehot = (iota((CAMS_CL, P_SH), 0) == cams).astype(F32).astype(BF16)
        part = part + dot(split2(a_s[k]), onehot, NT)
    part_ref[...] = part[:64] + part[64:]

    f_s[...] = jnp.zeros((128, MEM), F32)
    camsum = jnp.zeros((CAMS_CL, 128), F32)
    for q in range(2):
        j0 = y_ref[112 + 9 * q : 121 + 9 * q, :]
        j1 = y_ref[130 + 9 * q : 139 + 9 * q, :]
        for e in range(CP):
            f_s[9 * e : 9 * e + 9, :] = j0[e : e + 1] * j0 + j1[e : e + 1] * j1
        onehot = (iota((CAMS_CL, MEM), 0).astype(F32) == y_ref[108 + q : 109 + q, :]).astype(F32).astype(BF16)
        feats = f_s[...]
        high = feats.astype(BF16)
        low = (feats - high.astype(F32)).astype(BF16)
        camsum = camsum + dot(onehot, high, NT) + dot(onehot, low, NT)
    camsum_ref[...] = camsum


def pack_kernel(round_ref, partners_ref, y_ref, part_ref, camsum_ref, damp_ref, out_ref):
    cluster = lax.axis_index("cams")
    block = lax.axis_index("pts")
    groups = [y_ref[108 + q : 109 + q, :].astype(jnp.int32) >> 3 for q in range(2)]
    lanes = iota((SHARDS, MEM), 0)
    wanted = (lanes == groups[0]) | (lanes == groups[1])
    upto = (iota((MEM, MEM), 0) <= iota((MEM, MEM), 1)).astype(F32).astype(BF16)
    count = dot(wanted.astype(F32).astype(BF16), upto, NN)
    offset = round_ref[0] * SLOTS + 1
    slot = jnp.where(wanted, count.astype(jnp.int32) - offset, -1)
    feats = split2(y_ref[0:FEAT, :])
    part = part_ref[0:56, :]
    lane = iota((128, CAMS_CL), 0)
    spread = ((iota((128, CAMS_CL), 1) == block * GROUP + ninth(lane)) & (lane < ROWS)).astype(F32)
    row = iota((56, 128), 0)
    entry = iota((56, 128), 1)
    entry = entry - 9 * ninth(entry)
    for s in range(3):
        place = cluster if s == 0 else partners_ref[cluster, s - 1]
        place = (place - (cluster >> 1) * 2 + NCL) & (NCL - 1)
        damp = damp_ref[pl.ds(place, 1), :]
        part = part + dot_high(jnp.where(row - (18 * s + 9) == entry, damp, 0.0), spread)
    most = jnp.max(count, axis=1, keepdims=True)
    most = jnp.max(most, axis=0, keepdims=True)
    part = jnp.where(row == 54, most, part)
    for j in range(0, SHARDS, 2):
        wants = jnp.concatenate(
            [jnp.broadcast_to(slot[j + h : j + h + 1], (SLOTS, MEM)) for h in range(2)], axis=0
        )
        onehot = ((iota((2 * SLOTS, MEM), 0) & (SLOTS - 1)) == wants).astype(F32).astype(BF16)
        sent = dot(feats, onehot, NT)
        sent = sent[:FEAT] + sent[FEAT:]
        for h in range(2):
            out_ref[j + h, 0:FEAT, :] = sent[:, h * SLOTS : (h + 1) * SLOTS]
            out_ref[j + h, FEAT : FEAT + 8, :] = camsum_ref[(j + h) * GROUP : (j + h + 1) * GROUP, :]
            out_ref[j + h, FEAT + 8 : PAYLOAD, :] = part


def rows_kernel(first, *refs):
    if first:
        recv_ref, damp_ref, slab_ref, msg_ref, own_s, other_s, tot_s, turn_s = refs
    else:
        recv_ref, damp_ref, before_ref, before_msg_ref, slab_ref, msg_ref, own_s, other_s, tot_s, turn_s = refs
    group = lax.axis_index("pts")
    own_s[...] = jnp.zeros(own_s.shape, F32)
    other_s[...] = jnp.zeros(other_s.shape, F32)

    def chunk(step, carry):
        def load(row, count):
            return jnp.concatenate(
                [recv_ref[2 * step + h, row : row + count, :] for h in range(2)], axis=1
            )

        cams = [load(108 + q, 1).astype(jnp.int32) for q in range(2)]
        cols = [load(110 + q, 1).astype(jnp.int32) for q in range(2)]
        masks = [(iota((GROUP, CHUNK), 0) == cams[q] - group * GROUP).astype(F32) for q in range(2)]
        left = []
        for i in range(3):
            ra, rb = load(18 * i, 9), load(18 * i + 9, 9)
            left.append(
                jnp.concatenate(
                    [masks[0] * ra[e : e + 1] + masks[1] * rb[e : e + 1] for e in range(CP)], axis=0
                )
            )
        for which, (base, size, spots, acc) in enumerate(
            ((0, CAMS_CL, cams, own_s), (54, 2 * CAMS_CL, cols, other_s))
        ):
            sides = []
            hots = []
            for q in range(2):
                right = [load(base + 9 * (2 * i + q), 9) for i in range(3)]
                terms = [
                    left[0] * right[0][e : e + 1]
                    + left[1] * right[1][e : e + 1]
                    + left[2] * right[2][e : e + 1]
                    for e in range(CP)
                ]
                sides.append(split2(jnp.concatenate(terms, axis=0)))
                hots.append((iota((size, CHUNK), 0) == spots[q]).astype(F32).astype(BF16))
            got = dot(jnp.concatenate(sides, axis=1), jnp.concatenate(hots, axis=1), NT)
            acc[...] -= got[: CP * ROWS] + got[CP * ROWS :]
        return carry

    lax.fori_loop(0, SHARDS // 2, chunk, 0)

    tot = recv_ref[0, FEAT:PAYLOAD, :]
    most = recv_ref[0, FEAT + 62 : FEAT + 63, :]
    for b in range(1, SHARDS):
        tot = tot + recv_ref[b, FEAT:PAYLOAD, :]
        most = jnp.maximum(most, recv_ref[b, FEAT + 62 : FEAT + 63, :])
    tot_s[...] = tot

    lane = iota((GROUP, 128), 1)
    if first:
        where = ninth(lane)
        spread = (iota((ROWS, 128), 0) - 9 * ninth(iota((ROWS, 128), 0)) == iota((ROWS, 128), 1)).astype(F32)
        lane72 = iota((GROUP, ROWS), 1)
        damp = dot_high(jnp.where(ninth(lane72) == iota((GROUP, ROWS), 0), damp_ref[...], 0.0), spread)
        here = (lane == group * GROUP + iota((GROUP, 128), 0)).astype(F32)
        sums = tot_s[0:GROUP, :]
        for f in range(CP):
            for e in range(CP):
                term = sums[:, 9 * e + f : 9 * e + f + 1]
                if e == f:
                    term = term + damp[:, e : e + 1]
                row = f * ROWS + e * GROUP
                own_s[row : row + GROUP, :] += term * here

    rhs = [tot_s[8 + 18 * s : 17 + 18 * s, :] for s in range(3)]
    diag = [tot_s[17 + 18 * s : 26 + 18 * s, :] for s in range(3)]
    start = [rhs[s] / diag[s] for s in range(3)]
    image = jnp.zeros((ROWS, 128), F32)
    for f in range(CP):
        rows = slice(f * ROWS, (f + 1) * ROWS)
        image = image + own_s[rows, :] * start[0][f : f + 1]
        image = image + other_s[rows, 0:128] * start[1][f : f + 1]
        image = image + other_s[rows, 128:256] * start[2][f : f + 1]
    image = jnp.sum(image, axis=1, keepdims=True)
    order = (iota((ROWS, 128), 1) == 9 * (iota((ROWS, 128), 0) & 7) + (iota((ROWS, 128), 0) >> 3)).astype(F32)
    image = jnp.sum(image * order, axis=0, keepdims=True)

    lane = iota((CAMS_CL, 128), 1)
    spread = ((iota((CAMS_CL, 128), 0) == group * GROUP + ninth(lane)) & (lane < ROWS)).astype(F32)
    lane = iota((CP, 128), 1)
    entry = lane - 9 * ninth(lane) == iota((CP, 128), 0)

    def share(x):
        return jnp.sum(jnp.where(entry, dot_high(x, spread), 0.0), axis=0, keepdims=True)

    pad = (iota((1, 128), 1) >= ROWS).astype(F32)
    if not first:
        image = image + before_msg_ref[0:1, 256:384]
    msg = jnp.concatenate([share(rhs[0]), share(diag[0]) + pad, image, most], axis=1)
    msg_ref[...] = jnp.broadcast_to(msg, msg_ref.shape)

    row = iota((WIDTH, WIDTH), 0)
    shuffle = ((row & 127) * 9 + (row >> 7) == iota((WIDTH, WIDTH), 1)).astype(F32).astype(BF16)
    for s in range(3):
        if s == 0:
            parts = [own_s[f * ROWS : (f + 1) * ROWS, :] for f in range(CP)]
        else:
            parts = [
                other_s[f * ROWS : (f + 1) * ROWS, (s - 1) * 128 : s * 128] for f in range(CP)
            ]
        whole = jnp.concatenate(parts, axis=1)
        high = whole.astype(BF16).astype(F32)
        rest = whole - high
        middle = rest.astype(BF16).astype(F32)
        low = rest - middle
        stack = jnp.concatenate([high, middle, low, jnp.zeros((8, WIDTH), F32)], axis=0).astype(BF16)
        got = dot(stack, shuffle, NN)
        got = got[:ROWS] + got[ROWS : 2 * ROWS] + got[2 * ROWS : 3 * ROWS]
        for t in range(CP):
            for e in range(CP):
                turn_s[t, pl.ds(e, GROUP, stride=CP), :] = got[
                    e * GROUP : (e + 1) * GROUP, t * 128 : (t + 1) * 128
                ]
            lanes = slice(s * WIDTH + t * 128, s * WIDTH + (t + 1) * 128)
            if first:
                slab_ref[:, lanes] = turn_s[t]
            else:
                slab_ref[:, lanes] = before_ref[:, lanes] + turn_s[t]


def step_kernel(partners_ref, all_ref, slab_ref, msg_ref, vec_ref, d_s):
    cluster = lax.axis_index("cams")
    mine = lax.axis_index("pts") * NCL + cluster
    residual = all_ref[:, 0:128]
    dinv = all_ref[:, 128:256]
    image = all_ref[:, 256:384]

    def total(x):
        return jnp.sum(jnp.sum(x, axis=0, keepdims=True), axis=1, keepdims=True)

    direction = residual / dinv
    norm = total(residual * direction)
    alpha = norm / total(direction * image)
    step = alpha * direction
    residual = residual - alpha * image
    precond = residual / dinv
    norm_next = total(residual * precond)
    d_s[0] = precond + norm_next / norm * direction
    d_s[1] = step
    d_s[2] = residual
    blocks = [cluster, partners_ref[cluster, 0], partners_ref[cluster, 1]]
    picked = [d_s[0, pl.ds(blocks[s], SHARDS, stride=NCL), :] for s in range(3)]
    column = iota((128, WIDTH), 1)
    owner = (iota((SHARDS, WIDTH), 1) * 911) >> 16
    tile = (column - 72 * ((column * 911) >> 16) == iota((128, WIDTH), 0)).astype(F32)
    spread = dot_high(jnp.concatenate(picked, axis=0), tile)
    acc = jnp.zeros((ROWS, 128), F32)
    for s in range(3):
        part = jnp.where(owner == iota((SHARDS, WIDTH), 0), spread[s * SHARDS : (s + 1) * SHARDS], 0.0)
        line = jnp.sum(part, axis=0, keepdims=True)
        for t in range(CP):
            lanes = slice(s * WIDTH + t * 128, s * WIDTH + (t + 1) * 128)
            acc = acc + slab_ref[:, lanes] * line[:, t * 128 : (t + 1) * 128]
    acc = jnp.sum(acc, axis=1, keepdims=True)
    eye = (iota((ROWS, 128), 0) == iota((ROWS, 128), 1)).astype(F32)
    acc = jnp.sum(acc * eye, axis=0, keepdims=True)
    own = d_s[0, pl.ds(mine, 1), :]
    msg_ref[...] = jnp.broadcast_to(total(own * acc), msg_ref.shape)
    vec_ref[0:1, :] = d_s[1, pl.ds(mine, 1), :]
    vec_ref[1:2, :] = own
    vec_ref[2:3, :] = d_s[2, pl.ds(mine, 1), :]
    vec_ref[3:4, :] = acc
    vec_ref[4:5, :] = jnp.broadcast_to(norm_next, (1, 128))
    vec_ref[5:8, :] = jnp.zeros((3, 128), F32)


def finish_kernel(all_ref, vec_ref, solution_ref, residual_ref):
    alpha = vec_ref[4:5, :] / jnp.sum(all_ref[...], axis=0, keepdims=True)
    solution_ref[...] = (vec_ref[0:1, :] + alpha * vec_ref[1:2, :])[:, :ROWS]
    residual_ref[...] = (vec_ref[2:3, :] - alpha * vec_ref[3:4, :])[:, :ROWS]


SMEM = pl.BlockSpec(memory_space=pltpu.SMEM)
VMEM = pl.BlockSpec(memory_space=pltpu.VMEM)


def call(kernel, n_smem, args, outs, scratch=()):
    specs = [SMEM] * n_smem + [VMEM] * (len(args) - n_smem)
    return pl.pallas_call(
        kernel,
        out_shape=[jax.ShapeDtypeStruct(shape, F32) for shape in outs],
        in_specs=specs,
        out_specs=[VMEM] * len(outs),
        scratch_shapes=list(scratch),
        compiler_params=PARAMS,
    )(*args)


def exchange(x, axes):
    return lax.all_to_all(x, axes, 0, 0, tiled=True)


def form_rows(recv, damp, before=None):
    scratch = (
        pltpu.VMEM((CP * ROWS, CAMS_CL), F32),
        pltpu.VMEM((CP * ROWS, 2 * CAMS_CL), F32),
        pltpu.VMEM((PAYLOAD - FEAT, 128), F32),
        pltpu.VMEM((CP, ROWS, 128), F32),
    )
    outs = [(ROWS, 3 * WIDTH), (SHARDS * NCL, 512)]
    args = (recv, damp) + (before or ())
    return call(functools.partial(rows_kernel, before is None), 0, args, outs, scratch)


def gather_damping(damp):
    core = lax.axis_index("cams") % 2
    other = lax.ppermute(damp, "cams", [(i, i ^ 1) for i in range(NCL)])
    pair = jnp.where(core == 0, jnp.concatenate([damp, other]), jnp.concatenate([other, damp]))
    parts = [pair]
    for s in range(1, 4):
        parts.append(lax.ppermute(pair, "cams", [((i + 2 * s) % NCL, i) for i in range(NCL)]))
    return jnp.concatenate(parts, axis=0)


def body(cam_jac, pt_jac, resid, point_damping, obs_camera, members, partners, camera_damping):
    damp_all = jnp.pad(gather_damping(camera_damping), ((0, 0), (0, 128 - ROWS)))
    y, part, camsum = call(
        prepare_kernel,
        1,
        (partners, cam_jac, pt_jac, resid, point_damping[None], obs_camera, members[0]),
        [(160, MEM), (64, CAMS_CL), (CAMS_CL, 128)],
        (
            pltpu.VMEM((4, 8, P_SH), F32),
            pltpu.VMEM((160, P_SH), F32),
            pltpu.VMEM((4, 64, P_SH), F32),
            pltpu.VMEM((128, MEM), F32),
        ),
    )

    def send(turn):
        packed = call(
            pack_kernel,
            2,
            (turn, partners, y, part, camsum, damp_all),
            [(SHARDS, PAYLOAD, SLOTS)],
        )[0]
        return exchange(packed, "pts")

    slab, msg = form_rows(send(jnp.zeros((1,), jnp.int32)), camera_damping)
    everyone = exchange(msg, ("pts", "cams"))
    most = jnp.max(everyone[:, 384]).astype(jnp.int32)

    def more(slab, msg, everyone):
        def again(state):
            turn, slab, msg = state
            slab, msg = form_rows(send(turn[None]), camera_damping, (slab, msg[0:8]))
            return (turn + 1, slab, msg)

        _, slab, msg = lax.while_loop(lambda state: state[0] * SLOTS < most, again, (jnp.int32(1), slab, msg))
        return slab, exchange(msg, ("pts", "cams"))

    slab, everyone = lax.cond(
        most > SLOTS, more, lambda slab, msg, everyone: (slab, everyone), slab, msg, everyone
    )
    msg, vec = call(
        step_kernel,
        1,
        (partners, everyone, slab),
        [(SHARDS * NCL, 128), (8, 128)],
        (pltpu.VMEM((3, SHARDS * NCL, 128), F32),),
    )
    solution, residual = call(
        finish_kernel, 0, (exchange(msg, ("pts", "cams")), vec), [(1, ROWS), (1, ROWS)]
    )
    return (slab[None], solution, residual)


def solution(mesh):
    in_specs = (
        P(None, None, None, "pts"),
        P(None, None, None, "pts"),
        P(None, None, "pts"),
        P("pts"),
        P(None, "pts"),
        P("pts", "cams", None),
        P(),
        P("cams", "pts"),
    )
    out_specs = (P("cams", "pts", None), P("cams", "pts"), P("cams", "pts"))
    return jax.shard_map(body, mesh=mesh, in_specs=in_specs, out_specs=out_specs, check_vma=False)
```

```python
import functools

import jax
import jax.numpy as jnp
from jax import lax
from jax.experimental import pallas as pl
from jax.experimental.pallas import tpu as pltpu
from jax.sharding import PartitionSpec as P

CP = 9
CAMS_CL = 128
NCL = 8
SHARDS = 16
P_SH = 2048
MEM = 512
ROWS = 72
GROUP = 8
WIDTH = CP * CAMS_CL
SLOTS = 128
SENT = 100
FEAT = 112
PAYLOAD = 128
CHUNK = 256
PAIRS = [(e, f) for e in range(CP) for f in range(e, CP)]

HIGH = lax.Precision.HIGHEST
BF16 = jnp.bfloat16
F32 = jnp.float32
PARAMS = pltpu.CompilerParams(vmem_limit_bytes=48 * 1024 * 1024)
NN = (((1,), (0,)), ((), ()))
NT = (((1,), (1,)), ((), ()))


def iota(shape, axis):
    return lax.broadcasted_iota(jnp.int32, shape, axis)


def ninth(value):
    return (value * 7282) >> 16


def split2(value):
    high = value.astype(BF16).astype(F32)
    return jnp.concatenate([high, value - high], axis=0).astype(BF16)


def dot(a, b, dims):
    return lax.dot_general(a, b, dims, preferred_element_type=F32)


def dot_high(a, b):
    return lax.dot_general(a, b, NN, precision=HIGH, preferred_element_type=F32)


def hot(condition):
    return condition.astype(F32).astype(BF16)


def total(x):
    return jnp.sum(x, axis=0, keepdims=True)


def pack_kernel(
    round_ref, partners_ref, cam_ref, pt_ref, resid_ref, damp_ref, ids_ref, members_ref, cam_damp_ref,
    out_ref, x_s, y_s, f_s, g_s, t_s,
):
    cluster = lax.axis_index("cams")
    block = lax.axis_index("pts")
    first_partner = partners_ref[0, cluster]

    def chunk(step, carry):
        at = pl.ds(pl.multiple_of(step * CHUNK, CHUNK), CHUNK)
        p0, p1, p2 = (jnp.concatenate([pt_ref[0, i, :, at], pt_ref[1, i, :, at]], axis=0) for i in range(3))
        res = jnp.concatenate([resid_ref[0, :, at], resid_ref[1, :, at]], axis=0)
        damp = damp_ref[:, at]
        i00 = 1.0 / jnp.sqrt(total(p0 * p0) + damp)
        l10 = total(p0 * p1) * i00
        l20 = total(p0 * p2) * i00
        i11 = 1.0 / jnp.sqrt(total(p1 * p1) + damp - l10 * l10)
        l21 = (total(p1 * p2) - l20 * l10) * i11
        i22 = 1.0 / jnp.sqrt(total(p2 * p2) + damp - l20 * l20 - l21 * l21)
        b0 = p0 * i00
        b1 = (p1 - l10 * b0) * i11
        b2 = (p2 - l20 * b0 - l21 * b1) * i22
        ids = ids_ref[:, at]
        swap = jnp.broadcast_to(ids[0:1] >> 7, (4, CHUNK)) != cluster

        def turn(x):
            return jnp.where(swap, jnp.concatenate([x[2:4], x[0:2]], axis=0), x)

        for a in range(2):
            for e in range(CP):
                row = (a * CP + e) * 4
                x_s[row : row + 4, at] = turn(cam_ref[a, e, :, at])
        for i, b in enumerate((b0, b1, b2)):
            for a in range(2):
                row = 72 + (2 * i + a) * 4
                x_s[row : row + 4, at] = turn(b[4 * a : 4 * a + 4])
        ids = turn(ids)
        far = (iota((4, CHUNK), 0) >= 2) & ((ids >> 7) != first_partner)
        x_s[96:100, at] = ((ids & 127) + jnp.where(far, CAMS_CL, 0)).astype(F32)
        for a in range(2):
            x_s[100 + 4 * a : 104 + 4 * a, at] = turn(res[4 * a : 4 * a + 4])
        w = [total(b * res) for b in (b0, b1, b2)]
        x_s[108:112, at] = jnp.concatenate(w + [jnp.zeros((1, CHUNK), F32)], axis=0)
        return carry

    lax.fori_loop(0, P_SH // CHUNK, chunk, 0)

    y = dot(split2(x_s[...]), hot(iota((P_SH, MEM), 0) == members_ref[...]), NN)
    y_s[...] = y[:FEAT] + y[FEAT:]

    def pair(row):
        return y_s[row : row + 2, :]

    jac = [[pair((a * CP + e) * 4) for e in range(CP)] for a in range(2)]
    scaled = [[pair(72 + (2 * i + a) * 4) for a in range(2)] for i in range(3)]
    res = [pair(100 + 4 * a) for a in range(2)]
    w = [y_s[108 + i : 109 + i, :] for i in range(3)]
    same = (y_s[96:97, :] == y_s[97:98, :]).astype(F32)
    f_s[90:128, :] = jnp.zeros((38, MEM), F32)
    g_s[36:40, :] = jnp.zeros((4, MEM), F32)
    for e in range(CP):
        j0, j1 = jac[0][e], jac[1][e]
        red = [scaled[i][0] * j0 + scaled[i][1] * j1 for i in range(3)]
        both = sum(r[0:1] * r[1:2] for r in red) * same
        g_s[2 * e : 2 * e + 2, :] = j0 * res[0] + j1 * res[1] - sum(red[i] * w[i] for i in range(3))
        g_s[18 + 2 * e : 20 + 2 * e, :] = j0 * j0 + j1 * j1 - sum(r * r for r in red) - both
    for n, (e, f) in enumerate(PAIRS):
        f_s[2 * n : 2 * n + 2, :] = jac[0][e] * jac[0][f] + jac[1][e] * jac[1][f]
    feats = f_s[...]
    high = feats.astype(BF16)
    low = (feats - high.astype(F32)).astype(BF16)
    sums = split2(g_s[...])
    hots = [hot(iota((CAMS_CL, MEM), 0).astype(F32) == y_s[96 + q : 97 + q, :]) for q in range(2)]
    camsum = [dot(hots[q], high, NT) + dot(hots[q], low, NT) for q in range(2)]
    camsum = jnp.where((iota((CAMS_CL, 128), 1) & 1) == 0, camsum[0], camsum[1])
    sums = [dot(sums, hots[q], NT) for q in range(2)]
    sums = [x[:40] + x[40:] for x in sums]
    t_s[...] = jnp.where((iota((40, CAMS_CL), 0) & 1) == 0, sums[0], sums[1])
    part = t_s[pl.ds(0, 18, stride=2), :] + t_s[pl.ds(1, 18, stride=2), :]
    lane = iota((ROWS, CAMS_CL), 0)
    spread = (iota((ROWS, CAMS_CL), 1) == block * GROUP + ninth(lane)).astype(F32)
    lane = iota((18, ROWS), 1)
    damp = jnp.where(iota((18, ROWS), 0) - 9 == lane - 9 * ninth(lane), cam_damp_ref[...], 0.0)
    part = part + dot_high(damp, spread)

    groups = [y_s[96 + q : 97 + q, :].astype(jnp.int32) >> 3 for q in range(2)]
    lanes = iota((SHARDS, MEM), 0)
    wanted = (lanes == groups[0]) | (lanes == groups[1])
    count = dot(hot(wanted), hot(iota((MEM, MEM), 0) <= iota((MEM, MEM), 1)), NN)
    offset = round_ref[0] * SLOTS
    slot = jnp.where(wanted, count.astype(jnp.int32) - (offset + 1), -1)
    most = jnp.max(count, axis=1, keepdims=True)
    here = jnp.minimum(jnp.maximum(most - offset.astype(F32), 0.0), float(SLOTS))
    most = jnp.broadcast_to(jnp.max(most, axis=0, keepdims=True), (1, SLOTS))
    feats = split2(y_s[...])
    for j in range(0, SHARDS, 2):
        wants = jnp.concatenate(
            [jnp.broadcast_to(slot[j + h : j + h + 1], (SLOTS, MEM)) for h in range(2)], axis=0
        )
        sent = dot(feats, hot((iota((2 * SLOTS, MEM), 0) & (SLOTS - 1)) == wants), NT)
        sent = sent[:FEAT] + sent[FEAT:]
        for h in range(2):
            to = j + h
            out_ref[to, 0:SENT, :] = sent[:SENT, h * SLOTS : (h + 1) * SLOTS]
            out_ref[to, SENT : SENT + 8, :] = camsum[to * GROUP : (to + 1) * GROUP]
            out_ref[to, SENT + 8 : SENT + 26, :] = part
            out_ref[to, 126:127, :] = most
            out_ref[to, 127:128, :] = jnp.broadcast_to(here[to : to + 1], (1, SLOTS))


def sums_kernel(recv_ref, out_ref):
    group = lax.axis_index("pts")
    tot = recv_ref[0, 104:128, :]
    most = recv_ref[0, 126:127, :]
    for b in range(1, SHARDS):
        tot = tot + recv_ref[b, 104:128, :]
        most = jnp.maximum(most, recv_ref[b, 126:127, :])
    rhs, diag = tot[4:13], tot[13:22]
    column = iota((CAMS_CL, WIDTH), 1)
    spread = (ninth(column) == iota((CAMS_CL, WIDTH), 0)).astype(F32)
    column = iota((CP, WIDTH), 1)
    entry = column - 9 * ninth(column) == iota((CP, WIDTH), 0)
    line = total(jnp.where(entry, dot_high(rhs / diag, spread), 0.0))
    for t in range(CP):
        out_ref[t : t + 1, :] = line[:, t * 128 : (t + 1) * 128]

    def share(x, shift):
        lane = iota((CAMS_CL, 256), 1) - shift
        cam = jnp.where((lane >= 0) & (lane < ROWS), group * GROUP + ninth(jnp.maximum(lane, 0)), -1)
        lane = jnp.maximum(iota((CP, 256), 1) - shift, 0)
        entry = lane - 9 * ninth(lane) == iota((CP, 256), 0)
        return total(jnp.where(entry, dot_high(x, (cam == iota((CAMS_CL, 256), 0)).astype(F32)), 0.0))

    msg = share(rhs, 0) + share(diag, ROWS)
    out_ref[9:10, :] = msg[:, :128]
    out_ref[10:11, :] = msg[:, 128:]
    out_ref[11:12, :] = most
    out_ref[12:16, :] = jnp.zeros((4, 128), F32)


def rows_kernel(first, recv_ref, *refs):
    if first:
        damp_ref, slab_ref, own_s, other_s, turn_s, buf_s = refs
    else:
        before_ref, slab_ref, own_s, other_s, turn_s, buf_s = refs
    group = lax.axis_index("pts")
    own_s[...] = jnp.zeros(own_s.shape, F32)
    other_s[...] = jnp.zeros(other_s.shape, F32)

    counts = [recv_ref[b, 127, 0].astype(jnp.int32) for b in range(SHARDS)]
    lane = iota((SENT, 128), 1)
    buf_s[0] = jnp.zeros((SENT, 128), F32)
    at = jnp.int32(0)
    for b in range(SHARDS):
        shift = at & 127
        tile = at >> 7
        moved = pltpu.roll(recv_ref[b, 0:SENT, :], shift, 1)
        buf_s[tile] += jnp.where(lane >= shift, moved, 0.0)
        buf_s[tile + 1] = jnp.where(lane >= shift, 0.0, moved)
        at = at + counts[b]
    buf_s[(at >> 7) + 1] = jnp.zeros((SENT, 128), F32)

    def chunk(step, carry):
        def load(row, count):
            return jnp.concatenate([buf_s[2 * step + h, row : row + count, :] for h in range(2)], axis=1)

        numbers = load(96, 4).astype(jnp.int32)
        spots = [numbers[q : q + 1] for q in range(4)]
        masks = [(iota((GROUP, CHUNK), 0) == spots[q] - group * GROUP).astype(F32) for q in range(2)]
        scaled = [[load(72 + (2 * i + a) * 4, 4) for a in range(2)] for i in range(3)]
        red = [[] for i in range(3)]
        for e in range(CP):
            j0, j1 = load(e * 4, 4), load((CP + e) * 4, 4)
            for i in range(3):
                red[i].append(scaled[i][0] * j0 + scaled[i][1] * j1)
        left = [
            jnp.concatenate([masks[0] * red[i][e][0:1] + masks[1] * red[i][e][1:2] for e in range(CP)], axis=0)
            for i in range(3)
        ]
        for base, size, acc in ((0, CAMS_CL, own_s), (2, 2 * CAMS_CL, other_s)):
            sides = []
            hots = []
            for q in (base, base + 1):
                terms = [sum(left[i] * red[i][e][q : q + 1] for i in range(3)) for e in range(CP)]
                sides.append(split2(jnp.concatenate(terms, axis=0)))
                spot = (spots[q] & 128) + ((spots[q] * CP) & 127)
                hots.append(hot(iota((size, CHUNK), 0) == spot))
            got = dot(jnp.concatenate(sides, axis=1), jnp.concatenate(hots, axis=1), NT)
            acc[...] -= got[: CP * ROWS] + got[CP * ROWS :]
        return carry

    lax.fori_loop(0, (at + CHUNK - 1) // CHUNK, chunk, 0)

    if first:
        lane = iota((ROWS, 128), 0)
        spread = (lane - 9 * ninth(lane) == iota((ROWS, 128), 1)).astype(F32)
        damp = jnp.where(ninth(iota((GROUP, ROWS), 1)) == iota((GROUP, ROWS), 0), damp_ref[...], 0.0)
        damp = dot_high(damp, spread)
        here = (group * GROUP + iota((GROUP, 128), 0)) * CP
        here = (iota((GROUP, 128), 1) == (here & 127)).astype(F32)
        sums = recv_ref[0, SENT : SENT + 8, :]
        for b in range(1, SHARDS):
            sums = sums + recv_ref[b, SENT : SENT + 8, :]
        for n, (e, f) in enumerate(PAIRS):
            term = sums[:, 2 * n : 2 * n + 1] + sums[:, 2 * n + 1 : 2 * n + 2]
            if e == f:
                term = term + damp[:, e : e + 1]
            term = term * here
            for row in {f * ROWS + e * GROUP: 0, e * ROWS + f * GROUP: 0}:
                own_s[row : row + GROUP, :] += term

    column = iota((ROWS, 128), 1)
    for s in range(3):
        parts = []
        for f in range(CP):
            rows = slice(f * ROWS, (f + 1) * ROWS)
            part = own_s[rows, :] if s == 0 else other_s[rows, (s - 1) * 128 : s * 128]
            parts.append(pltpu.roll(part, f, 1))
        for t in range(CP):
            entry = column + t * 128
            entry = entry - 9 * ninth(entry)
            got = parts[0]
            for f in range(1, CP):
                got = jnp.where(entry == f, parts[f], got)
            for e in range(CP):
                turn_s[t, pl.ds(e, GROUP, stride=CP), :] = got[e * GROUP : (e + 1) * GROUP]
            lanes = slice(s * WIDTH + t * 128, s * WIDTH + (t + 1) * 128)
            if first:
                slab_ref[:, lanes] = turn_s[t]
            else:
                slab_ref[:, lanes] = before_ref[:, lanes] + turn_s[t]


def times_rows(slab_ref, line):
    acc = jnp.zeros((ROWS, 128), F32)
    for s in range(3):
        for t in range(CP):
            lanes = slice(s * WIDTH + t * 128, s * WIDTH + (t + 1) * 128)
            acc = acc + slab_ref[:, lanes] * line(s, t)
    return jnp.sum(acc, axis=1, keepdims=True)


def image_kernel(partners_ref, slab_ref, pair_ref, z1_ref, z2_ref, z3_ref, msg_ref, most_ref, v_s):
    cluster = lax.axis_index("cams")
    most = pair_ref[11:12, :]
    for s, ref in enumerate((pair_ref, z1_ref, z2_ref, z3_ref)):
        for h in range(2):
            v_s[2 * s + h] = ref[16 * h : 16 * h + 16, :]
            most = jnp.maximum(most, ref[16 * h + 11 : 16 * h + 12, :])
    places = [0]
    for s in range(2):
        other = partners_ref[s, cluster]
        places.append(2 * (((other >> 1) - (cluster >> 1)) & 3) + ((other ^ cluster) & 1))
    image = times_rows(slab_ref, lambda s, t: v_s[places[s], t : t + 1, :])
    image = total(image * (iota((ROWS, 256), 1) - 2 * ROWS == iota((ROWS, 256), 0)).astype(F32))
    msg = image + jnp.concatenate([v_s[0, 9:10, :], v_s[0, 10:11, :]], axis=1)
    msg_ref[...] = jnp.broadcast_to(msg, msg_ref.shape)
    most_ref[0] = jnp.max(most).astype(jnp.int32)


def step_kernel(partners_ref, all_ref, slab_ref, msg_ref, vec_ref, d_s):
    cluster = lax.axis_index("cams")
    mine = lax.axis_index("pts") * NCL + cluster
    residual = all_ref[:, 0:ROWS]
    dinv = all_ref[:, ROWS : 2 * ROWS]
    image = all_ref[:, 2 * ROWS : 3 * ROWS]

    def whole(x):
        return jnp.sum(total(x), axis=1, keepdims=True)

    direction = residual / dinv
    norm = whole(residual * direction)
    alpha = norm / whole(direction * image)
    step = alpha * direction
    residual = residual - alpha * image
    precond = residual / dinv
    norm_next = whole(residual * precond)
    d_s[...] = jnp.zeros(d_s.shape, F32)
    d_s[0, :, 0:ROWS] = precond + norm_next / norm * direction
    d_s[1, :, 0:ROWS] = step
    d_s[2, :, 0:ROWS] = residual
    blocks = [cluster, partners_ref[0, cluster], partners_ref[1, cluster]]
    picked = [d_s[0, pl.ds(blocks[s], SHARDS, stride=NCL), :] for s in range(3)]
    column = iota((128, WIDTH), 1)
    owner = (iota((SHARDS, WIDTH), 1) * 911) >> 16
    tile = (column - 72 * ((column * 911) >> 16) == iota((128, WIDTH), 0)).astype(F32)
    spread = dot_high(jnp.concatenate(picked, axis=0), tile)
    lines = [
        total(jnp.where(owner == iota((SHARDS, WIDTH), 0), spread[s * SHARDS : (s + 1) * SHARDS], 0.0))
        for s in range(3)
    ]
    acc = times_rows(slab_ref, lambda s, t: lines[s][:, t * 128 : (t + 1) * 128])
    acc = total(acc * (iota((ROWS, 128), 0) == iota((ROWS, 128), 1)).astype(F32))
    own = d_s[0, pl.ds(mine, 1), :]
    msg_ref[...] = jnp.broadcast_to(whole(own * acc), msg_ref.shape)
    vec_ref[0:1, :] = d_s[1, pl.ds(mine, 1), :]
    vec_ref[1:2, :] = own
    vec_ref[2:3, :] = d_s[2, pl.ds(mine, 1), :]
    vec_ref[3:4, :] = acc
    vec_ref[4:5, :] = jnp.broadcast_to(norm_next, (1, 128))
    vec_ref[5:8, :] = jnp.zeros((3, 128), F32)


def finish_kernel(all_ref, vec_ref, solution_ref, residual_ref):
    alpha = vec_ref[4:5, :] / total(all_ref[...])
    solution_ref[...] = (vec_ref[0:1, :] + alpha * vec_ref[1:2, :])[:, :ROWS]
    residual_ref[...] = (vec_ref[2:3, :] - alpha * vec_ref[3:4, :])[:, :ROWS]


SMEM = pl.BlockSpec(memory_space=pltpu.SMEM)
VMEM = pl.BlockSpec(memory_space=pltpu.VMEM)


def call(kernel, n_smem, args, outs, scratch=(), cost=None):
    return pl.pallas_call(
        kernel,
        out_shape=[jax.ShapeDtypeStruct(x, jnp.int32 if len(x) == 1 else F32) for x in outs],
        in_specs=[SMEM] * n_smem + [VMEM] * (len(args) - n_smem),
        out_specs=[SMEM if len(x) == 1 else VMEM for x in outs],
        scratch_shapes=[pltpu.VMEM(x, F32) for x in scratch],
        compiler_params=PARAMS,
        cost_estimate=cost,
    )(*args)


def exchange(x, axes):
    return lax.all_to_all(x, axes, 0, 0, tiled=True)


def form_rows(recv, other):
    first = other.shape == (1, ROWS)
    scratch = ((CP * ROWS, CAMS_CL), (CP * ROWS, 2 * CAMS_CL), (CP, ROWS, 128), (SHARDS + 2, SENT, 128))
    return call(
        functools.partial(rows_kernel, first),
        0,
        (recv, other),
        [(ROWS, 3 * WIDTH)],
        scratch,
        pl.CostEstimate(flops=8 * 10**9, bytes_accessed=4 * 10**6, transcendentals=0),
    )[0]


def share_vectors(own):
    other = lax.ppermute(own, "cams", [(i, i ^ 1) for i in range(NCL)])
    pair = jnp.concatenate([own, other], axis=0)
    moves = [[((i + 2 * s) % NCL, i) for i in range(NCL)] for s in range(1, 4)]
    return [pair] + [lax.ppermute(pair, "cams", move) for move in moves]


def body(cam_jac, pt_jac, resid, point_damping, obs_camera, members, partners, camera_damping):
    partners = partners.T
    points = (
        partners,
        jnp.transpose(cam_jac, (0, 2, 1, 3)),
        jnp.transpose(pt_jac, (0, 2, 1, 3)),
        resid,
        point_damping[None],
        obs_camera,
        members[0],
        camera_damping,
    )

    def send(turn):
        scratch = ((FEAT, P_SH), (FEAT, MEM), (128, MEM), (40, MEM), (40, 128))
        packed = call(pack_kernel, 2, (turn,) + points, [(SHARDS, PAYLOAD, SLOTS)], scratch)[0]
        return exchange(packed, "pts")

    def first_image(slab, vectors):
        outs = [(SHARDS * NCL, 256), (1,)]
        return call(image_kernel, 1, (partners, slab, *vectors), outs, ((8, 16, 128),))

    recv = send(jnp.zeros((1,), jnp.int32))
    vectors = share_vectors(call(sums_kernel, 0, (recv,), [(16, 128)])[0])
    slab = form_rows(recv, camera_damping)
    msg, most = first_image(slab, vectors)
    most = most[0]

    def more(slab, msg):
        def again(state):
            turn, slab = state
            return (turn + 1, form_rows(send(turn[None]), slab))

        slab = lax.while_loop(lambda state: state[0] * SLOTS < most, again, (jnp.int32(1), slab))[1]
        return slab, first_image(slab, vectors)[0]

    slab, msg = lax.cond(most > SLOTS, more, lambda slab, msg: (slab, msg), slab, msg)
    msg, vec = call(
        step_kernel,
        1,
        (partners, exchange(msg, ("pts", "cams")), slab),
        [(SHARDS * NCL, 128), (8, 128)],
        ((3, SHARDS * NCL, 128),),
    )
    outs = [(1, ROWS), (1, ROWS)]
    solution, residual = call(finish_kernel, 0, (exchange(msg, ("pts", "cams")), vec), outs)
    return (slab[None], solution, residual)


def solution(mesh):
    in_specs = (
        P(None, None, None, "pts"),
        P(None, None, None, "pts"),
        P(None, None, "pts"),
        P("pts"),
        P(None, "pts"),
        P("pts", "cams", None),
        P(),
        P("cams", "pts"),
    )
    out_specs = (P("cams", "pts", None), P("cams", "pts"), P("cams", "pts"))
    return jax.shard_map(body, mesh=mesh, in_specs=in_specs, out_specs=out_specs, check_vma=False)
```

```python
import functools

import jax
import jax.numpy as jnp
from jax import lax
from jax.experimental import pallas as pl
from jax.experimental.pallas import tpu as pltpu
from jax.sharding import PartitionSpec as P

CP = 9
CAMS_CL = 128
NCL = 8
SHARDS = 16
P_SH = 2048
MEM = 512
ROWS = 72
GROUP = 8
WIDTH = CP * CAMS_CL
SLOTS = 96
SENT = 100
FEAT = 112
JROWS = 72
PAYLOAD = 104
CHUNK = 256
PAIRS = [(e, f) for e in range(CP) for f in range(e, CP)]

BF16 = jnp.bfloat16
F32 = jnp.float32
PARAMS = pltpu.CompilerParams(vmem_limit_bytes=48 * 1024 * 1024)
NN = (((1,), (0,)), ((), ()))
NT = (((1,), (1,)), ((), ()))


def iota(shape, axis):
    return lax.broadcasted_iota(jnp.int32, shape, axis)


def ninth(value):
    return (value * 7282) >> 16


def split2(value):
    high = value.astype(BF16).astype(F32)
    return jnp.concatenate([high, value - high], axis=0).astype(BF16)


def dot(a, b, dims):
    return lax.dot_general(a, b, dims, preferred_element_type=F32)


def dot_exact(a, onehot):
    high = a.astype(BF16)
    rest = a - high.astype(F32)
    middle = rest.astype(BF16)
    low = (rest - middle.astype(F32)).astype(BF16)
    return dot(high, onehot, NN) + dot(middle, onehot, NN) + dot(low, onehot, NN)


def hot(condition):
    return condition.astype(F32).astype(BF16)


def total(x):
    return jnp.sum(x, axis=0, keepdims=True)


def pack_kernel(
    round_ref, partners_ref, cam_ref, pt_ref, resid_ref, damp_ref, ids_ref, members_ref, cam_damp_ref,
    out_ref, x_s, y_s, f_s, g_s, t_s,
):
    cluster = lax.axis_index("cams")
    block = lax.axis_index("pts")
    first_partner = partners_ref[0, cluster]

    def chunk(step, carry):
        at = pl.ds(pl.multiple_of(step * CHUNK, CHUNK), CHUNK)
        p0, p1, p2 = (jnp.concatenate([pt_ref[0, i, :, at], pt_ref[1, i, :, at]], axis=0) for i in range(3))
        res = jnp.concatenate([resid_ref[0, :, at], resid_ref[1, :, at]], axis=0)
        damp = damp_ref[:, at]
        i00 = 1.0 / jnp.sqrt(total(p0 * p0) + damp)
        l10 = total(p0 * p1) * i00
        l20 = total(p0 * p2) * i00
        i11 = 1.0 / jnp.sqrt(total(p1 * p1) + damp - l10 * l10)
        l21 = (total(p1 * p2) - l20 * l10) * i11
        i22 = 1.0 / jnp.sqrt(total(p2 * p2) + damp - l20 * l20 - l21 * l21)
        b0 = p0 * i00
        b1 = (p1 - l10 * b0) * i11
        b2 = (p2 - l20 * b0 - l21 * b1) * i22
        ids = ids_ref[:, at]
        swap = jnp.broadcast_to(ids[0:1] >> 7, (4, CHUNK)) != cluster

        def turn(x):
            return jnp.where(swap, jnp.concatenate([x[2:4], x[0:2]], axis=0), x)

        for a in range(2):
            for e in range(CP):
                row = (a * CP + e) * 4
                x_s[row : row + 4, at] = turn(cam_ref[a, e, :, at])
        for i, b in enumerate((b0, b1, b2)):
            for a in range(2):
                row = 72 + (2 * i + a) * 4
                x_s[row : row + 4, at] = turn(b[4 * a : 4 * a + 4])
        ids = turn(ids)
        far = (iota((4, CHUNK), 0) >= 2) & ((ids >> 7) != first_partner)
        x_s[96:100, at] = ((ids & 127) + jnp.where(far, CAMS_CL, 0)).astype(F32)
        for a in range(2):
            x_s[100 + 4 * a : 104 + 4 * a, at] = turn(res[4 * a : 4 * a + 4])
        w = [total(b * res) for b in (b0, b1, b2)]
        x_s[108:112, at] = jnp.concatenate(w + [jnp.zeros((1, CHUNK), F32)], axis=0)
        return carry

    lax.fori_loop(0, P_SH // CHUNK, chunk, 0)

    y = dot(split2(x_s[...]), hot(iota((P_SH, MEM), 0) == members_ref[...]), NN)
    y_s[...] = y[:FEAT] + y[FEAT:]

    def pair(row):
        return y_s[row : row + 2, :]

    jac = [[pair((a * CP + e) * 4) for e in range(CP)] for a in range(2)]
    scaled = [[pair(72 + (2 * i + a) * 4) for a in range(2)] for i in range(3)]
    res = [pair(100 + 4 * a) for a in range(2)]
    w = [y_s[108 + i : 109 + i, :] for i in range(3)]
    same = (y_s[96:97, :] == y_s[97:98, :]).astype(F32)
    f_s[90:128, :] = jnp.zeros((38, MEM), F32)
    g_s[36:40, :] = jnp.zeros((4, MEM), F32)
    for e in range(CP):
        j0, j1 = jac[0][e], jac[1][e]
        red = [scaled[i][0] * j0 + scaled[i][1] * j1 for i in range(3)]
        both = sum(r[0:1] * r[1:2] for r in red) * same
        g_s[2 * e : 2 * e + 2, :] = j0 * res[0] + j1 * res[1] - sum(red[i] * w[i] for i in range(3))
        g_s[18 + 2 * e : 20 + 2 * e, :] = j0 * j0 + j1 * j1 - sum(r * r for r in red) - both
    for n, (e, f) in enumerate(PAIRS):
        f_s[2 * n : 2 * n + 2, :] = jac[0][e] * jac[0][f] + jac[1][e] * jac[1][f]
    feats = f_s[...]
    high = feats.astype(BF16)
    low = (feats - high.astype(F32)).astype(BF16)
    sums = split2(g_s[...])
    hots = [hot(iota((CAMS_CL, MEM), 0).astype(F32) == y_s[96 + q : 97 + q, :]) for q in range(2)]
    camsum = [dot(hots[q], high, NT) + dot(hots[q], low, NT) for q in range(2)]
    camsum = jnp.where((iota((CAMS_CL, 128), 1) & 1) == 0, camsum[0], camsum[1])
    sums = [dot(sums, hots[q], NT) for q in range(2)]
    sums = [x[:40] + x[40:] for x in sums]
    t_s[...] = jnp.where((iota((40, CAMS_CL), 0) & 1) == 0, sums[0], sums[1])
    part = t_s[pl.ds(0, 18, stride=2), :] + t_s[pl.ds(1, 18, stride=2), :]
    lane = iota((ROWS, CAMS_CL), 0)
    spread = hot(iota((ROWS, CAMS_CL), 1) == block * GROUP + ninth(lane))
    lane = iota((18, ROWS), 1)
    damp = jnp.where(iota((18, ROWS), 0) - 9 == lane - 9 * ninth(lane), cam_damp_ref[...], 0.0)
    part = part + dot_exact(damp, spread)

    offset = round_ref[0] * SLOTS
    groups = [y_s[96 + q : 97 + q, :].astype(jnp.int32) >> 3 for q in range(2)]
    lanes = iota((SHARDS, MEM), 0)
    wanted = (lanes == groups[0]) | (lanes == groups[1])
    count = dot(hot(wanted), hot(iota((MEM, MEM), 0) <= iota((MEM, MEM), 1)), NN).astype(jnp.int32)
    slot = count - (offset + 1)
    slot = jnp.where(wanted & (slot < SLOTS), slot, -1)
    most = jnp.max(count, axis=1, keepdims=True)
    here = jnp.minimum(jnp.maximum(most - offset, 0), SLOTS).astype(F32)
    most = jnp.broadcast_to(jnp.max(most, axis=0, keepdims=True).astype(F32), (1, 128))
    feats = split2(y_s[...])
    lane = iota((24, 128), 1)
    for j in range(0, SHARDS, 2):
        wants = jnp.concatenate(
            [jnp.broadcast_to(slot[j + h : j + h + 1], (128, MEM)) for h in range(2)], axis=0
        )
        sent = dot(feats, hot((iota((256, MEM), 0) & 127) == wants), NT)
        sent = sent[:FEAT] + sent[FEAT:]
        for h in range(2):
            to = j + h
            own = sent[:, h * 128 : (h + 1) * 128]
            scaled = own[JROWS : JROWS + 24]
            for third in range(3):
                rows = slice(24 * third, 24 * third + 24)
                out_ref[to, rows, :] = jnp.where(lane < SLOTS, own[rows], pltpu.roll(scaled, SLOTS - 32 * third, 1))
            out_ref[to, 72:76, :] = own[96:100]
            out_ref[to, 76:94, :] = part
            out_ref[to, 94:95, :] = most
            out_ref[to, 95:96, :] = jnp.broadcast_to(here[to : to + 1], (1, 128))
            out_ref[to, 96:104, :] = camsum[to * GROUP : (to + 1) * GROUP]


def sums_kernel(recv_ref, out_ref):
    group = lax.axis_index("pts")
    tot = recv_ref[0, 72:96, :]
    most = tot
    for b in range(1, SHARDS):
        one = recv_ref[b, 72:96, :]
        tot = tot + one
        most = jnp.maximum(most, one)
    tot, most = tot[4:22], most[22:23]
    column = iota((CAMS_CL, WIDTH), 1)
    spread = hot(ninth(column) == iota((CAMS_CL, WIDTH), 0))
    column = iota((CP, WIDTH), 1)
    entry = column - 9 * ninth(column) == iota((CP, WIDTH), 0)
    lines = dot_exact(tot, spread)
    lane = iota((CAMS_CL, 128), 1)
    share = hot((iota((CAMS_CL, 128), 0) == group * GROUP + ninth(lane)) & (lane < ROWS))
    lane = iota((CP, 128), 1)
    entry_share = lane - 9 * ninth(lane) == iota((CP, 128), 0)
    share = dot_exact(tot, share)
    for k in range(2):
        line = total(jnp.where(entry, lines[CP * k : CP * (k + 1)], 0.0))
        for t in range(CP):
            out_ref[CP * k + t : CP * k + t + 1, :] = line[:, t * 128 : (t + 1) * 128]
        out_ref[18 + k : 19 + k, :] = total(jnp.where(entry_share, share[CP * k : CP * (k + 1)], 0.0))
    out_ref[20:21, :] = most
    out_ref[21:24, :] = jnp.zeros((3, 128), F32)


def rows_kernel(first, recv_ref, *refs):
    if first:
        damp_ref, slab_ref, own_s, other_s, turn_s, buf_s = refs
    else:
        before_ref, slab_ref, own_s, other_s, turn_s, buf_s = refs
    group = lax.axis_index("pts")
    own_s[...] = jnp.zeros(own_s.shape, F32)
    other_s[...] = jnp.zeros(other_s.shape, F32)

    counts = [recv_ref[b, 95, 0].astype(jnp.int32) for b in range(SHARDS)]
    lane = iota((1, 128), 1)
    third = iota((24, 128), 1) >> 5
    buf_s[0] = jnp.zeros((SENT, 128), F32)
    at = jnp.int32(0)
    for b in range(SHARDS):
        shift = at & 127
        tile = at >> 7
        jac = recv_ref[b, 0:JROWS, :]
        scaled = [pltpu.roll(jac[24 * h : 24 * h + 24], 128 - SLOTS + 32 * h, 1) for h in range(3)]
        scaled = jnp.where(third == 0, scaled[0], jnp.where(third == 1, scaled[1], scaled[2]))
        here = ((lane >= shift) & (lane < shift + SLOTS)).astype(F32)
        beyond = (lane < shift + (SLOTS - 128)).astype(F32)
        for row, rows, values in ((0, JROWS, jac), (72, 24, scaled), (96, 4, recv_ref[b, JROWS : JROWS + 4, :])):
            moved = pltpu.roll(values, shift, 1)
            buf_s[tile, row : row + rows, :] += moved * here
            buf_s[tile + 1, row : row + rows, :] = moved * beyond
        at = at + counts[b]

    def chunk(tile, tiles):
        lanes = 128 * tiles

        def load(row, count):
            return jnp.concatenate([buf_s[tile + h, row : row + count, :] for h in range(tiles)], axis=1)

        numbers = load(96, 4).astype(jnp.int32)
        spots = [numbers[q : q + 1] for q in range(4)]
        masks = [(iota((GROUP, lanes), 0) == spots[q] - group * GROUP).astype(F32) for q in range(2)]
        scaled = [[load(72 + (2 * i + a) * 4, 4) for a in range(2)] for i in range(3)]
        red = [[] for i in range(3)]
        for e in range(CP):
            j0, j1 = load(e * 4, 4), load((CP + e) * 4, 4)
            for i in range(3):
                red[i].append(scaled[i][0] * j0 + scaled[i][1] * j1)
        left = [
            jnp.concatenate([masks[0] * red[i][e][0:1] + masks[1] * red[i][e][1:2] for e in range(CP)], axis=0)
            for i in range(3)
        ]
        for base, size, acc in ((0, CAMS_CL, own_s), (2, 2 * CAMS_CL, other_s)):
            sides = []
            hots = []
            for q in (base, base + 1):
                terms = [sum(left[i] * red[i][e][q : q + 1] for i in range(3)) for e in range(CP)]
                sides.append(split2(jnp.concatenate(terms, axis=0)))
                spot = (spots[q] & 128) + ((spots[q] * CP) & 127)
                hots.append(hot(iota((size, lanes), 0) == spot))
            got = dot(jnp.concatenate(sides, axis=1), jnp.concatenate(hots, axis=1), NT)
            acc[...] -= got[: CP * ROWS] + got[CP * ROWS :]

    def pair(step, carry):
        chunk(2 * step, 2)
        return carry

    tiles = (at + 127) >> 7
    lax.fori_loop(0, tiles >> 1, pair, 0)

    @pl.when((tiles & 1) == 1)
    def _():
        chunk(tiles - 1, 1)

    if first:
        lane = iota((ROWS, 128), 0)
        spread = hot(lane - 9 * ninth(lane) == iota((ROWS, 128), 1))
        damp = jnp.where(ninth(iota((GROUP, ROWS), 1)) == iota((GROUP, ROWS), 0), damp_ref[...], 0.0)
        damp = dot_exact(damp, spread)
        here = (group * GROUP + iota((GROUP, 128), 0)) * CP
        here = (iota((GROUP, 128), 1) == (here & 127)).astype(F32)
        sums = recv_ref[0, 96:104, :]
        for b in range(1, SHARDS):
            sums = sums + recv_ref[b, 96:104, :]
        for n, (e, f) in enumerate(PAIRS):
            term = sums[:, 2 * n : 2 * n + 1] + sums[:, 2 * n + 1 : 2 * n + 2]
            if e == f:
                term = term + damp[:, e : e + 1]
            term = term * here
            for row in {f * ROWS + e * GROUP: 0, e * ROWS + f * GROUP: 0}:
                own_s[row : row + GROUP, :] += term

    column = iota((ROWS, 128), 1)
    for s in range(3):
        parts = []
        for f in range(CP):
            rows = slice(f * ROWS, (f + 1) * ROWS)
            part = own_s[rows, :] if s == 0 else other_s[rows, (s - 1) * 128 : s * 128]
            parts.append(pltpu.roll(part, f, 1))
        for t in range(CP):
            entry = column + t * 128
            entry = entry - 9 * ninth(entry)
            got = parts[0]
            for f in range(1, CP):
                got = jnp.where(entry == f, parts[f], got)
            for e in range(CP):
                turn_s[t, pl.ds(e, GROUP, stride=CP), :] = got[e * GROUP : (e + 1) * GROUP]
            lanes = slice(s * WIDTH + t * 128, s * WIDTH + (t + 1) * 128)
            if first:
                slab_ref[:, lanes] = turn_s[t]
            else:
                slab_ref[:, lanes] = before_ref[:, lanes] + turn_s[t]


def times_rows(slab_ref, line):
    acc = jnp.zeros((ROWS, 128), F32)
    for s in range(3):
        for t in range(CP):
            lanes = slice(s * WIDTH + t * 128, s * WIDTH + (t + 1) * 128)
            acc = acc + slab_ref[:, lanes] * line(s, t)
    return jnp.sum(acc, axis=1, keepdims=True)


def image_kernel(partners_ref, slab_ref, pair_ref, z1_ref, z2_ref, z3_ref, msg_ref, lines_ref, most_ref):
    cluster = lax.axis_index("cams")
    most = pair_ref[20:21, :]
    for s, ref in enumerate((pair_ref, z1_ref, z2_ref, z3_ref)):
        chip = (cluster >> 1) + s & 3
        for h in range(2):
            lines_ref[2 * chip + (cluster + h & 1)] = ref[24 * h : 24 * h + 24, :]
            most = jnp.maximum(most, ref[24 * h + 20 : 24 * h + 21, :])
    blocks = [cluster, partners_ref[0, cluster], partners_ref[1, cluster]]
    start = [lines_ref[c, 0:CP, :] / lines_ref[c, CP : 2 * CP, :] for c in blocks]
    image = times_rows(slab_ref, lambda s, t: start[s][t : t + 1])
    image = total(image * (iota((ROWS, 128), 1) == iota((ROWS, 128), 0)).astype(F32))
    msg_ref[...] = jnp.broadcast_to(image, msg_ref.shape)
    most_ref[0] = jnp.max(most).astype(jnp.int32)


def step_kernel(partners_ref, all_ref, slab_ref, lines_ref, msg_ref, vec_ref, d_s):
    cluster = lax.axis_index("cams")
    mine = lax.axis_index("pts") * NCL + cluster
    column = iota((128, WIDTH), 1)
    spread = dot_exact(all_ref[...], hot(column - ROWS * ((column * 911) >> 16) == iota((128, WIDTH), 0)))
    owner = (iota((NCL, WIDTH), 1) * 911) >> 16
    image = jnp.zeros((NCL, WIDTH), F32)
    for j in range(SHARDS):
        image = jnp.where(owner == j, spread[j * NCL : (j + 1) * NCL], image)

    def whole(x):
        return jnp.sum(total(x), axis=1, keepdims=True)

    def line(row):
        return jnp.concatenate([lines_ref[:, row + t, :] for t in range(CP)], axis=1)

    residual, diag = line(0), line(CP)
    own_diag = lines_ref[cluster, 19:20, :]
    own_diag = jnp.where(iota((1, 128), 1) < ROWS, own_diag, 1.0)
    own_residual = lines_ref[cluster, 18:19, :]
    own_image = all_ref[pl.ds(mine, 1), :]
    direction = residual / diag
    own_direction = own_residual / own_diag
    norm = whole(residual * direction)
    alpha = norm / whole(direction * image)
    residual = residual - alpha * image
    own_residual = own_residual - alpha * own_image
    precond = residual / diag
    norm_next = whole(residual * precond)
    ratio = norm_next / norm
    d_s[...] = precond + ratio * direction
    own = own_residual / own_diag + ratio * own_direction
    blocks = [cluster, partners_ref[0, cluster], partners_ref[1, cluster]]
    lines = [d_s[pl.ds(c, 1), :] for c in blocks]
    acc = times_rows(slab_ref, lambda s, t: lines[s][:, t * 128 : (t + 1) * 128])
    acc = total(acc * (iota((ROWS, 128), 0) == iota((ROWS, 128), 1)).astype(F32))
    msg_ref[...] = jnp.broadcast_to(whole(own * acc), msg_ref.shape)
    vec_ref[0:1, :] = alpha * own_direction
    vec_ref[1:2, :] = own
    vec_ref[2:3, :] = own_residual
    vec_ref[3:4, :] = acc
    vec_ref[4:5, :] = jnp.broadcast_to(norm_next, (1, 128))
    vec_ref[5:8, :] = jnp.zeros((3, 128), F32)


def finish_kernel(all_ref, vec_ref, solution_ref, residual_ref):
    alpha = vec_ref[4:5, :] / total(all_ref[...])
    solution_ref[...] = (vec_ref[0:1, :] + alpha * vec_ref[1:2, :])[:, :ROWS]
    residual_ref[...] = (vec_ref[2:3, :] - alpha * vec_ref[3:4, :])[:, :ROWS]


SMEM = pl.BlockSpec(memory_space=pltpu.SMEM)
VMEM = pl.BlockSpec(memory_space=pltpu.VMEM)


def call(kernel, n_smem, args, outs, scratch=(), cost=None):
    return pl.pallas_call(
        kernel,
        out_shape=[jax.ShapeDtypeStruct(x, jnp.int32 if len(x) == 1 else F32) for x in outs],
        in_specs=[SMEM] * n_smem + [VMEM] * (len(args) - n_smem),
        out_specs=[SMEM if len(x) == 1 else VMEM for x in outs],
        scratch_shapes=[pltpu.VMEM(x, F32) for x in scratch],
        compiler_params=PARAMS,
        cost_estimate=cost,
    )(*args)


def exchange(x, axes):
    return lax.all_to_all(x, axes, 0, 0, tiled=True)


def form_rows(recv, other):
    first = other.shape == (1, ROWS)
    scratch = ((CP * ROWS, CAMS_CL), (CP * ROWS, 2 * CAMS_CL), (CP, ROWS, 128), (SHARDS + 2, SENT, 128))
    return call(
        functools.partial(rows_kernel, first),
        0,
        (recv, other),
        [(ROWS, 3 * WIDTH)],
        scratch,
        pl.CostEstimate(flops=8 * 10**9, bytes_accessed=4 * 10**6, transcendentals=0),
    )[0]


def share_vectors(own):
    other = lax.ppermute(own, "cams", [(i, i ^ 1) for i in range(NCL)])
    pair = jnp.concatenate([own, other], axis=0)
    moves = [[((i + 2 * s) % NCL, i) for i in range(NCL)] for s in range(1, 4)]
    return [pair] + [lax.ppermute(pair, "cams", move) for move in moves]


def body(cam_jac, pt_jac, resid, point_damping, obs_camera, members, partners, camera_damping):
    partners = partners.T
    points = (
        partners,
        jnp.transpose(cam_jac, (0, 2, 1, 3)),
        jnp.transpose(pt_jac, (0, 2, 1, 3)),
        resid,
        point_damping[None],
        obs_camera,
        members[0],
        camera_damping,
    )

    everywhere = ("pts", "cams")

    def send(turn):
        scratch = ((FEAT, P_SH), (FEAT, MEM), (128, MEM), (40, MEM), (40, 128))
        packed = call(pack_kernel, 2, (turn,) + points, [(SHARDS, PAYLOAD, 128)], scratch)[0]
        return exchange(packed, "pts")

    recv = send(jnp.zeros((1,), jnp.int32))
    vectors = share_vectors(call(sums_kernel, 0, (recv,), [(24, 128)])[0])
    slab = form_rows(recv, camera_damping)

    def first_images(slab):
        outs = [(SHARDS * NCL, 128), (NCL, 24, 128), (1,)]
        msg, lines, most = call(image_kernel, 1, (partners, slab, *vectors), outs)
        return exchange(msg, everywhere), lines, most[0]

    images, lines, most = first_images(slab)

    def more(slab, images):
        def again(state):
            turn, slab = state
            return (turn + 1, form_rows(send(turn[None]), slab))

        slab = lax.while_loop(lambda state: state[0] * SLOTS < most, again, (jnp.int32(1), slab))[1]
        return slab, first_images(slab)[0]

    slab, images = lax.cond(most > SLOTS, more, lambda *so_far: so_far, slab, images)
    outs = [(SHARDS * NCL, 128), (8, 128)]
    msg, vec = call(step_kernel, 1, (partners, images, slab, lines), outs, ((NCL, WIDTH),))
    outs = [(1, ROWS), (1, ROWS)]
    solution, residual = call(finish_kernel, 0, (exchange(msg, everywhere), vec), outs)
    return (slab[None], solution, residual)


def solution(mesh):
    in_specs = (
        P(None, None, None, "pts"),
        P(None, None, None, "pts"),
        P(None, None, "pts"),
        P("pts"),
        P(None, "pts"),
        P("pts", "cams", None),
        P(),
        P("cams", "pts"),
    )
    out_specs = (P("cams", "pts", None), P("cams", "pts"), P("cams", "pts"))
    return jax.shard_map(body, mesh=mesh, in_specs=in_specs, out_specs=out_specs, check_vma=False)
```

```python
import functools

import jax
import jax.numpy as jnp
from jax import lax
from jax.experimental import pallas as pl
from jax.experimental.pallas import tpu as pltpu
from jax.sharding import PartitionSpec as P

CP = 9
CAMS_CL = 128
NCL = 8
SHARDS = 16
P_SH = 2048
MEM = 512
ROWS = 72
GROUP = 8
WIDTH = CP * CAMS_CL
SLOTS = 96
SENT = 100
FEAT = 112
JROWS = 72
PAYLOAD = 104
CHUNK = 256
PAIRS = [(e, f) for e in range(CP) for f in range(e, CP)]

BF16 = jnp.bfloat16
F32 = jnp.float32
PARAMS = pltpu.CompilerParams(vmem_limit_bytes=48 * 1024 * 1024)
NN = (((1,), (0,)), ((), ()))
NT = (((1,), (1,)), ((), ()))


def iota(shape, axis):
    return lax.broadcasted_iota(jnp.int32, shape, axis)


def ninth(value):
    return (value * 7282) >> 16


def split2(value):
    high = value.astype(BF16).astype(F32)
    return jnp.concatenate([high, value - high], axis=0).astype(BF16)


def dot(a, b, dims):
    return lax.dot_general(a, b, dims, preferred_element_type=F32)


def dot_exact(a, onehot):
    high = a.astype(BF16)
    rest = a - high.astype(F32)
    middle = rest.astype(BF16)
    low = (rest - middle.astype(F32)).astype(BF16)
    return dot(high, onehot, NN) + dot(middle, onehot, NN) + dot(low, onehot, NN)


def hot(condition):
    return condition.astype(F32).astype(BF16)


def total(x):
    return jnp.sum(x, axis=0, keepdims=True)


def pack_kernel(
    round_ref, partners_ref, cam_ref, pt_ref, resid_ref, damp_ref, ids_ref, members_ref, cam_damp_ref,
    out_ref, x_s, y_s, f_s, g_s, t_s,
):
    cluster = lax.axis_index("cams")
    block = lax.axis_index("pts")
    first_partner = partners_ref[0, cluster]

    def chunk(step, carry):
        at = pl.ds(pl.multiple_of(step * CHUNK, CHUNK), CHUNK)
        p0, p1, p2 = (jnp.concatenate([pt_ref[0, i, :, at], pt_ref[1, i, :, at]], axis=0) for i in range(3))
        res = jnp.concatenate([resid_ref[0, :, at], resid_ref[1, :, at]], axis=0)
        damp = jnp.concatenate([damp_ref[pl.ds(2 * step + h, 1), :] for h in range(2)], axis=1)
        i00 = 1.0 / jnp.sqrt(total(p0 * p0) + damp)
        l10 = total(p0 * p1) * i00
        l20 = total(p0 * p2) * i00
        i11 = 1.0 / jnp.sqrt(total(p1 * p1) + damp - l10 * l10)
        l21 = (total(p1 * p2) - l20 * l10) * i11
        i22 = 1.0 / jnp.sqrt(total(p2 * p2) + damp - l20 * l20 - l21 * l21)
        b0 = p0 * i00
        b1 = (p1 - l10 * b0) * i11
        b2 = (p2 - l20 * b0 - l21 * b1) * i22
        ids = ids_ref[:, at]
        swap = jnp.broadcast_to(ids[0:1] >> 7, (4, CHUNK)) != cluster

        def turn(x):
            return jnp.where(swap, jnp.concatenate([x[2:4], x[0:2]], axis=0), x)

        for a in range(2):
            for e in range(CP):
                row = (a * CP + e) * 4
                x_s[row : row + 4, at] = turn(cam_ref[a, e, :, at])
        for i, b in enumerate((b0, b1, b2)):
            for a in range(2):
                row = 72 + (2 * i + a) * 4
                x_s[row : row + 4, at] = turn(b[4 * a : 4 * a + 4])
        ids = turn(ids)
        far = (iota((4, CHUNK), 0) >= 2) & ((ids >> 7) != first_partner)
        x_s[96:100, at] = ((ids & 127) + jnp.where(far, CAMS_CL, 0)).astype(F32)
        for a in range(2):
            x_s[100 + 4 * a : 104 + 4 * a, at] = turn(res[4 * a : 4 * a + 4])
        w = [total(b * res) for b in (b0, b1, b2)]
        x_s[108:112, at] = jnp.concatenate(w + [jnp.zeros((1, CHUNK), F32)], axis=0)
        return carry

    lax.fori_loop(0, P_SH // CHUNK, chunk, 0)

    y = dot(split2(x_s[...]), hot(iota((P_SH, MEM), 0) == members_ref[...]), NN)
    y_s[...] = y[:FEAT] + y[FEAT:]

    def pair(row):
        return y_s[row : row + 2, :]

    jac = [[pair((a * CP + e) * 4) for e in range(CP)] for a in range(2)]
    scaled = [[pair(72 + (2 * i + a) * 4) for a in range(2)] for i in range(3)]
    res = [pair(100 + 4 * a) for a in range(2)]
    w = [y_s[108 + i : 109 + i, :] for i in range(3)]
    same = (y_s[96:97, :] == y_s[97:98, :]).astype(F32)
    f_s[90:128, :] = jnp.zeros((38, MEM), F32)
    g_s[36:40, :] = jnp.zeros((4, MEM), F32)
    for e in range(CP):
        j0, j1 = jac[0][e], jac[1][e]
        red = [scaled[i][0] * j0 + scaled[i][1] * j1 for i in range(3)]
        both = sum(r[0:1] * r[1:2] for r in red) * same
        g_s[2 * e : 2 * e + 2, :] = j0 * res[0] + j1 * res[1] - sum(red[i] * w[i] for i in range(3))
        g_s[18 + 2 * e : 20 + 2 * e, :] = j0 * j0 + j1 * j1 - sum(r * r for r in red) - both
    for n, (e, f) in enumerate(PAIRS):
        f_s[2 * n : 2 * n + 2, :] = jac[0][e] * jac[0][f] + jac[1][e] * jac[1][f]
    feats = f_s[...]
    high = feats.astype(BF16)
    low = (feats - high.astype(F32)).astype(BF16)
    sums = split2(g_s[...])
    hots = [hot(iota((CAMS_CL, MEM), 0).astype(F32) == y_s[96 + q : 97 + q, :]) for q in range(2)]
    camsum = [dot(hots[q], high, NT) + dot(hots[q], low, NT) for q in range(2)]
    camsum = jnp.where((iota((CAMS_CL, 128), 1) & 1) == 0, camsum[0], camsum[1])
    sums = [dot(sums, hots[q], NT) for q in range(2)]
    sums = [x[:40] + x[40:] for x in sums]
    t_s[...] = jnp.where((iota((40, CAMS_CL), 0) & 1) == 0, sums[0], sums[1])
    part = t_s[pl.ds(0, 18, stride=2), :] + t_s[pl.ds(1, 18, stride=2), :]
    lane = iota((ROWS, CAMS_CL), 0)
    spread = hot(iota((ROWS, CAMS_CL), 1) == block * GROUP + ninth(lane))
    lane = iota((18, ROWS), 1)
    damp = jnp.where(iota((18, ROWS), 0) - 9 == lane - 9 * ninth(lane), cam_damp_ref[...], 0.0)
    part = part + dot_exact(damp, spread)

    offset = round_ref[0] * SLOTS
    groups = [y_s[96 + q : 97 + q, :].astype(jnp.int32) >> 3 for q in range(2)]
    lanes = iota((SHARDS, MEM), 0)
    wanted = (lanes == groups[0]) | (lanes == groups[1])
    count = dot(hot(wanted), hot(iota((MEM, MEM), 0) <= iota((MEM, MEM), 1)), NN).astype(jnp.int32)
    slot = count - (offset + 1)
    slot = jnp.where(wanted & (slot < SLOTS), slot, -1)
    most = jnp.max(count, axis=1, keepdims=True)
    here = jnp.minimum(jnp.maximum(most - offset, 0), SLOTS).astype(F32)
    most = jnp.broadcast_to(jnp.max(most, axis=0, keepdims=True).astype(F32), (1, 128))
    feats = split2(y_s[...])
    lane = iota((24, 128), 1)
    for j in range(0, SHARDS, 2):
        wants = jnp.concatenate(
            [jnp.broadcast_to(slot[j + h : j + h + 1], (128, MEM)) for h in range(2)], axis=0
        )
        sent = dot(feats, hot((iota((256, MEM), 0) & 127) == wants), NT)
        sent = sent[:FEAT] + sent[FEAT:]
        for h in range(2):
            to = j + h
            own = sent[:, h * 128 : (h + 1) * 128]
            scaled = own[JROWS : JROWS + 24]
            for third in range(3):
                rows = slice(24 * third, 24 * third + 24)
                out_ref[to, rows, :] = jnp.where(lane < SLOTS, own[rows], pltpu.roll(scaled, SLOTS - 32 * third, 1))
            out_ref[to, 72:76, :] = own[96:100]
            out_ref[to, 76:94, :] = part
            out_ref[to, 94:95, :] = most
            out_ref[to, 95:96, :] = jnp.broadcast_to(here[to : to + 1], (1, 128))
            out_ref[to, 96:104, :] = camsum[to * GROUP : (to + 1) * GROUP]


def sums_kernel(recv_ref, out_ref):
    group = lax.axis_index("pts")
    tot = recv_ref[0, 72:96, :]
    most = tot
    for b in range(1, SHARDS):
        one = recv_ref[b, 72:96, :]
        tot = tot + one
        most = jnp.maximum(most, one)
    tot, most = tot[4:22], most[22:23]
    column = iota((CAMS_CL, WIDTH), 1)
    spread = hot(ninth(column) == iota((CAMS_CL, WIDTH), 0))
    column = iota((CP, WIDTH), 1)
    entry = column - 9 * ninth(column) == iota((CP, WIDTH), 0)
    lines = dot_exact(tot, spread)
    lane = iota((CAMS_CL, 128), 1)
    share = hot((iota((CAMS_CL, 128), 0) == group * GROUP + ninth(lane)) & (lane < ROWS))
    lane = iota((CP, 128), 1)
    entry_share = lane - 9 * ninth(lane) == iota((CP, 128), 0)
    share = dot_exact(tot, share)
    for k in range(2):
        line = total(jnp.where(entry, lines[CP * k : CP * (k + 1)], 0.0))
        for t in range(CP):
            out_ref[CP * k + t : CP * k + t + 1, :] = line[:, t * 128 : (t + 1) * 128]
        out_ref[18 + k : 19 + k, :] = total(jnp.where(entry_share, share[CP * k : CP * (k + 1)], 0.0))
    out_ref[20:21, :] = most
    out_ref[21:24, :] = jnp.zeros((3, 128), F32)


def line_up_kernel(recv_ref, buf_s):
    counts = [recv_ref[b, 95, 0].astype(jnp.int32) for b in range(SHARDS)]
    lane = iota((1, 128), 1)
    third = iota((24, 128), 1) >> 5
    at = jnp.int32(0)
    for b in range(SHARDS):
        shift = at & 127
        tile = at >> 7
        jac = recv_ref[b, 0:JROWS, :]
        scaled = [pltpu.roll(jac[24 * h : 24 * h + 24], 128 - SLOTS + 32 * h, 1) for h in range(3)]
        scaled = jnp.where(third == 0, scaled[0], jnp.where(third == 1, scaled[1], scaled[2]))
        filled = ((lane < shift + (SLOTS - 128)) | ((lane >= shift) & (lane < shift + SLOTS))).astype(F32)
        for row, rows, values in ((0, JROWS, jac), (72, 24, scaled), (96, 4, recv_ref[b, JROWS : JROWS + 4, :])):
            moved = pltpu.roll(values, shift, 1)
            moved = moved * filled
            mask = iota((rows, 128), 1) >= shift
            pltpu.store(buf_s.at[tile, row : row + rows, :], moved, mask=mask)
            buf_s[tile + 1, row : row + rows, :] = jnp.where(mask, 0.0, moved)
        at = at + counts[b]
    buf_s[SHARDS + 2, 0:1, :] = jnp.broadcast_to(at.astype(F32), (1, 128))


def rows_kernel(first, recv_ref, buf_s, *refs):
    if first:
        damp_ref, slab_ref, own_s, other_s, turn_s = refs
    else:
        before_ref, slab_ref, own_s, other_s, turn_s = refs
    group = lax.axis_index("pts")
    own_s[...] = jnp.zeros(own_s.shape, F32)
    other_s[...] = jnp.zeros(other_s.shape, F32)

    at = buf_s[SHARDS + 2, 0, 0].astype(jnp.int32)

    def chunk(tile, tiles):
        lanes = 128 * tiles

        def load(row, count):
            return jnp.concatenate([buf_s[tile + h, row : row + count, :] for h in range(tiles)], axis=1)

        numbers = load(96, 4).astype(jnp.int32)
        spots = [numbers[q : q + 1] for q in range(4)]
        masks = [(iota((GROUP, lanes), 0) == spots[q] - group * GROUP).astype(F32) for q in range(2)]
        scaled = [[load(72 + (2 * i + a) * 4, 4) for a in range(2)] for i in range(3)]
        red = [[] for i in range(3)]
        for e in range(CP):
            j0, j1 = load(e * 4, 4), load((CP + e) * 4, 4)
            for i in range(3):
                red[i].append(scaled[i][0] * j0 + scaled[i][1] * j1)
        left = [
            jnp.concatenate([masks[0] * red[i][e][0:1] + masks[1] * red[i][e][1:2] for e in range(CP)], axis=0)
            for i in range(3)
        ]
        for base, size, acc in ((0, CAMS_CL, own_s), (2, 2 * CAMS_CL, other_s)):
            sides = []
            hots = []
            for q in (base, base + 1):
                terms = [sum(left[i] * red[i][e][q : q + 1] for i in range(3)) for e in range(CP)]
                sides.append(split2(jnp.concatenate(terms, axis=0)))
                spot = (spots[q] & 128) + ((spots[q] * CP) & 127)
                hots.append(hot(iota((size, lanes), 0) == spot))
            got = dot(jnp.concatenate(sides, axis=1), jnp.concatenate(hots, axis=1), NT)
            acc[...] -= got[: CP * ROWS] + got[CP * ROWS :]

    def pair(step, carry):
        chunk(2 * step, 2)
        return carry

    tiles = (at + 127) >> 7
    lax.fori_loop(0, tiles >> 1, pair, 0)

    @pl.when((tiles & 1) == 1)
    def _():
        chunk(tiles - 1, 1)

    if first:
        lane = iota((ROWS, 128), 0)
        spread = hot(lane - 9 * ninth(lane) == iota((ROWS, 128), 1))
        damp = jnp.where(ninth(iota((GROUP, ROWS), 1)) == iota((GROUP, ROWS), 0), damp_ref[...], 0.0)
        damp = dot_exact(damp, spread)
        here = (group * GROUP + iota((GROUP, 128), 0)) * CP
        here = (iota((GROUP, 128), 1) == (here & 127)).astype(F32)
        sums = recv_ref[0, 96:104, :]
        for b in range(1, SHARDS):
            sums = sums + recv_ref[b, 96:104, :]
        for n, (e, f) in enumerate(PAIRS):
            term = sums[:, 2 * n : 2 * n + 1] + sums[:, 2 * n + 1 : 2 * n + 2]
            if e == f:
                term = term + damp[:, e : e + 1]
            term = term * here
            for row in {f * ROWS + e * GROUP: 0, e * ROWS + f * GROUP: 0}:
                own_s[row : row + GROUP, :] += term

    column = iota((ROWS, 128), 1)
    for s in range(3):
        parts = []
        for f in range(CP):
            rows = slice(f * ROWS, (f + 1) * ROWS)
            part = own_s[rows, :] if s == 0 else other_s[rows, (s - 1) * 128 : s * 128]
            parts.append(pltpu.roll(part, f, 1))
        for t in range(CP):
            entry = column + t * 128
            entry = entry - 9 * ninth(entry)
            got = parts[0]
            for f in range(1, CP):
                got = jnp.where(entry == f, parts[f], got)
            for e in range(CP):
                turn_s[t, pl.ds(e, GROUP, stride=CP), :] = got[e * GROUP : (e + 1) * GROUP]
            lanes = slice(s * WIDTH + t * 128, s * WIDTH + (t + 1) * 128)
            if first:
                slab_ref[:, lanes] = turn_s[t]
            else:
                slab_ref[:, lanes] = before_ref[:, lanes] + turn_s[t]


def times_rows(slab_ref, line):
    acc = jnp.zeros((ROWS, 128), F32)
    for s in range(3):
        for t in range(CP):
            lanes = slice(s * WIDTH + t * 128, s * WIDTH + (t + 1) * 128)
            acc = acc + slab_ref[:, lanes] * line(s, t)
    return jnp.sum(acc, axis=1, keepdims=True)


def image_kernel(partners_ref, slab_ref, pair_ref, z1_ref, z2_ref, z3_ref, msg_ref, lines_ref, most_ref):
    cluster = lax.axis_index("cams")
    most = pair_ref[20:21, :]
    for s, ref in enumerate((pair_ref, z1_ref, z2_ref, z3_ref)):
        chip = (cluster >> 1) + s & 3
        for h in range(2):
            lines_ref[2 * chip + (cluster + h & 1)] = ref[24 * h : 24 * h + 24, :]
            most = jnp.maximum(most, ref[24 * h + 20 : 24 * h + 21, :])
    blocks = [cluster, partners_ref[0, cluster], partners_ref[1, cluster]]
    start = [lines_ref[c, 0:CP, :] / lines_ref[c, CP : 2 * CP, :] for c in blocks]
    image = times_rows(slab_ref, lambda s, t: start[s][t : t + 1])
    image = total(image * (iota((ROWS, 128), 1) == iota((ROWS, 128), 0)).astype(F32))
    msg_ref[...] = jnp.broadcast_to(image, msg_ref.shape)
    most_ref[0] = jnp.max(most).astype(jnp.int32)


def step_kernel(partners_ref, all_ref, slab_ref, lines_ref, msg_ref, vec_ref, d_s):
    cluster = lax.axis_index("cams")
    mine = lax.axis_index("pts") * NCL + cluster
    column = iota((128, WIDTH), 1)
    spread = dot_exact(all_ref[...], hot(column - ROWS * ((column * 911) >> 16) == iota((128, WIDTH), 0)))
    owner = (iota((NCL, WIDTH), 1) * 911) >> 16
    image = jnp.zeros((NCL, WIDTH), F32)
    for j in range(SHARDS):
        image = jnp.where(owner == j, spread[j * NCL : (j + 1) * NCL], image)

    def whole(x):
        return jnp.sum(total(x), axis=1, keepdims=True)

    def line(row):
        return jnp.concatenate([lines_ref[:, row + t, :] for t in range(CP)], axis=1)

    residual, diag = line(0), line(CP)
    own_diag = lines_ref[cluster, 19:20, :]
    own_diag = jnp.where(iota((1, 128), 1) < ROWS, own_diag, 1.0)
    own_residual = lines_ref[cluster, 18:19, :]
    own_image = all_ref[pl.ds(mine, 1), :]
    direction = residual / diag
    own_direction = own_residual / own_diag
    norm = whole(residual * direction)
    alpha = norm / whole(direction * image)
    residual = residual - alpha * image
    own_residual = own_residual - alpha * own_image
    precond = residual / diag
    norm_next = whole(residual * precond)
    ratio = norm_next / norm
    d_s[...] = precond + ratio * direction
    own = own_residual / own_diag + ratio * own_direction
    blocks = [cluster, partners_ref[0, cluster], partners_ref[1, cluster]]
    lines = [d_s[pl.ds(c, 1), :] for c in blocks]
    acc = times_rows(slab_ref, lambda s, t: lines[s][:, t * 128 : (t + 1) * 128])
    acc = total(acc * (iota((ROWS, 128), 0) == iota((ROWS, 128), 1)).astype(F32))
    msg_ref[...] = jnp.broadcast_to(whole(own * acc), msg_ref.shape)
    vec_ref[0:1, :] = alpha * own_direction
    vec_ref[1:2, :] = own
    vec_ref[2:3, :] = own_residual
    vec_ref[3:4, :] = acc
    vec_ref[4:5, :] = jnp.broadcast_to(norm_next, (1, 128))
    vec_ref[5:8, :] = jnp.zeros((3, 128), F32)


def finish_kernel(all_ref, vec_ref, solution_ref, residual_ref):
    alpha = vec_ref[4:5, :] / total(all_ref[...])
    solution_ref[...] = (vec_ref[0:1, :] + alpha * vec_ref[1:2, :])[:, :ROWS]
    residual_ref[...] = (vec_ref[2:3, :] - alpha * vec_ref[3:4, :])[:, :ROWS]


SMEM = pl.BlockSpec(memory_space=pltpu.SMEM)
VMEM = pl.BlockSpec(memory_space=pltpu.VMEM)


def call(kernel, n_smem, args, outs, scratch=(), cost=None):
    return pl.pallas_call(
        kernel,
        out_shape=[jax.ShapeDtypeStruct(x, jnp.int32 if len(x) == 1 else F32) for x in outs],
        in_specs=[SMEM] * n_smem + [VMEM] * (len(args) - n_smem),
        out_specs=[SMEM if len(x) == 1 else VMEM for x in outs],
        scratch_shapes=[pltpu.VMEM(x, F32) for x in scratch],
        compiler_params=PARAMS,
        cost_estimate=cost,
    )(*args)


def exchange(x, axes):
    return lax.all_to_all(x, axes, 0, 0, tiled=True)


def form_rows(recv, points, other):
    first = other.shape == (1, ROWS)
    scratch = ((CP * ROWS, CAMS_CL), (CP * ROWS, 2 * CAMS_CL), (CP, ROWS, 128))
    return call(
        functools.partial(rows_kernel, first),
        0,
        (recv, points, other),
        [(ROWS, 3 * WIDTH)],
        scratch,
        pl.CostEstimate(flops=8 * 10**9, bytes_accessed=4 * 10**6, transcendentals=0),
    )[0]


def line_up(recv):
    return call(line_up_kernel, 0, (recv,), [(SHARDS + 3, 104, 128)])[0]


def share_vectors(own):
    other = lax.ppermute(own, "cams", [(i, i ^ 1) for i in range(NCL)])
    pair = jnp.concatenate([own, other], axis=0)
    moves = [[((i + 2 * s) % NCL, i) for i in range(NCL)] for s in range(1, 4)]
    return [pair] + [lax.ppermute(pair, "cams", move) for move in moves]


def body(cam_jac, pt_jac, resid, point_damping, obs_camera, members, partners, camera_damping):
    partners = partners.T
    points = (
        partners,
        jnp.transpose(cam_jac, (0, 2, 1, 3)),
        jnp.transpose(pt_jac, (0, 2, 1, 3)),
        resid,
        point_damping.reshape(P_SH // 128, 128),
        obs_camera,
        members[0],
        camera_damping,
    )

    everywhere = ("pts", "cams")

    def send(turn):
        scratch = ((FEAT, P_SH), (FEAT, MEM), (128, MEM), (40, MEM), (40, 128))
        packed = call(pack_kernel, 2, (turn,) + points, [(SHARDS, PAYLOAD, 128)], scratch)[0]
        return exchange(packed, "pts")

    recv = send(jnp.zeros((1,), jnp.int32))
    vectors = share_vectors(call(sums_kernel, 0, (recv,), [(24, 128)])[0])
    slab = form_rows(recv, line_up(recv), camera_damping)

    def first_images(slab):
        outs = [(SHARDS * NCL, 128), (NCL, 24, 128), (1,)]
        msg, lines, most = call(image_kernel, 1, (partners, slab, *vectors), outs)
        return exchange(msg, everywhere), lines, most[0]

    images, lines, most = first_images(slab)

    def more(slab, images):
        def again(state):
            turn, slab = state
            recv = send(turn[None])
            return (turn + 1, form_rows(recv, line_up(recv), slab))

        slab = lax.while_loop(lambda state: state[0] * SLOTS < most, again, (jnp.int32(1), slab))[1]
        return slab, first_images(slab)[0]

    slab, images = lax.cond(most > SLOTS, more, lambda *so_far: so_far, slab, images)
    outs = [(SHARDS * NCL, 128), (8, 128)]
    msg, vec = call(step_kernel, 1, (partners, images, slab, lines), outs, ((NCL, WIDTH),))
    outs = [(1, ROWS), (1, ROWS)]
    solution, residual = call(finish_kernel, 0, (exchange(msg, everywhere), vec), outs)
    return (slab[None], solution, residual)


def solution(mesh):
    in_specs = (
        P(None, None, None, "pts"),
        P(None, None, None, "pts"),
        P(None, None, "pts"),
        P("pts"),
        P(None, "pts"),
        P("pts", "cams", None),
        P(),
        P("cams", "pts"),
    )
    out_specs = (P("cams", "pts", None), P("cams", "pts"), P("cams", "pts"))
    return jax.shard_map(body, mesh=mesh, in_specs=in_specs, out_specs=out_specs, check_vma=False)
```

```python
import functools

import jax
import jax.numpy as jnp
from jax import lax
from jax.experimental import pallas as pl
from jax.experimental.pallas import tpu as pltpu
from jax.sharding import PartitionSpec as P

CP = 9
CAMS_CL = 128
NCL = 8
SHARDS = 16
P_SH = 2048
MEM = 512
ROWS = 72
GROUP = 8
WIDTH = CP * CAMS_CL
SLOTS = 96
SENT = 100
FEAT = 112
JROWS = 72
PAYLOAD = 104
CHUNK = 256
PAIRS = [(e, f) for e in range(CP) for f in range(e, CP)]

BF16 = jnp.bfloat16
F32 = jnp.float32
PARAMS = pltpu.CompilerParams(vmem_limit_bytes=48 * 1024 * 1024)
NN = (((1,), (0,)), ((), ()))
NT = (((1,), (1,)), ((), ()))


def iota(shape, axis):
    return lax.broadcasted_iota(jnp.int32, shape, axis)


def ninth(value):
    return (value * 7282) >> 16


def split2(value):
    high = value.astype(BF16).astype(F32)
    return jnp.concatenate([high, value - high], axis=0).astype(BF16)


def dot(a, b, dims):
    return lax.dot_general(a, b, dims, preferred_element_type=F32)


def dot_exact(a, onehot):
    high = a.astype(BF16)
    rest = a - high.astype(F32)
    middle = rest.astype(BF16)
    low = (rest - middle.astype(F32)).astype(BF16)
    return dot(high, onehot, NN) + dot(middle, onehot, NN) + dot(low, onehot, NN)


def hot(condition):
    return condition.astype(F32).astype(BF16)


def total(x):
    return jnp.sum(x, axis=0, keepdims=True)


def partners_of(cluster, partners_ref):
    here = jnp.where(iota((2, NCL), 1) == cluster, partners_ref[...], 0)
    return jnp.sum(here.astype(F32), axis=1, keepdims=True)


def pack_kernel(later, *refs):
    offset = refs[0][0] * SLOTS if later else 0
    (partners_ref, cam_ref, pt_ref, resid_ref, damp_ref, ids_ref, members_ref, cam_damp_ref,
     out_ref, x_s, y_s, f_s, g_s, t_s) = refs[1:] if later else refs
    cluster = lax.axis_index("cams")
    block = lax.axis_index("pts")
    first_partner = partners_of(cluster, partners_ref)[0:1].astype(jnp.int32)

    def chunk(step, carry):
        at = pl.ds(pl.multiple_of(step * CHUNK, CHUNK), CHUNK)
        p0, p1, p2 = (jnp.concatenate([pt_ref[0, i, :, at], pt_ref[1, i, :, at]], axis=0) for i in range(3))
        res = jnp.concatenate([resid_ref[0, :, at], resid_ref[1, :, at]], axis=0)
        damp = jnp.concatenate([damp_ref[pl.ds(2 * step + h, 1), :] for h in range(2)], axis=1)
        i00 = 1.0 / jnp.sqrt(total(p0 * p0) + damp)
        l10 = total(p0 * p1) * i00
        l20 = total(p0 * p2) * i00
        i11 = 1.0 / jnp.sqrt(total(p1 * p1) + damp - l10 * l10)
        l21 = (total(p1 * p2) - l20 * l10) * i11
        i22 = 1.0 / jnp.sqrt(total(p2 * p2) + damp - l20 * l20 - l21 * l21)
        b0 = p0 * i00
        b1 = (p1 - l10 * b0) * i11
        b2 = (p2 - l20 * b0 - l21 * b1) * i22
        ids = ids_ref[:, at]
        swap = jnp.broadcast_to(ids[0:1] >> 7, (4, CHUNK)) != cluster

        def turn(x):
            return jnp.where(swap, jnp.concatenate([x[2:4], x[0:2]], axis=0), x)

        for a in range(2):
            for e in range(CP):
                row = (a * CP + e) * 4
                x_s[row : row + 4, at] = turn(cam_ref[a, e, :, at])
        for i, b in enumerate((b0, b1, b2)):
            for a in range(2):
                row = 72 + (2 * i + a) * 4
                x_s[row : row + 4, at] = turn(b[4 * a : 4 * a + 4])
        ids = turn(ids)
        far = (iota((4, CHUNK), 0) >= 2) & ((ids >> 7) != first_partner)
        x_s[96:100, at] = ((ids & 127) + jnp.where(far, CAMS_CL, 0)).astype(F32)
        for a in range(2):
            x_s[100 + 4 * a : 104 + 4 * a, at] = turn(res[4 * a : 4 * a + 4])
        w = [total(b * res) for b in (b0, b1, b2)]
        x_s[108:112, at] = jnp.concatenate(w + [jnp.zeros((1, CHUNK), F32)], axis=0)
        return carry

    lax.fori_loop(0, P_SH // CHUNK, chunk, 0)

    y = dot(split2(x_s[...]), hot(iota((P_SH, MEM), 0) == members_ref[...]), NN)
    y_s[...] = y[:FEAT] + y[FEAT:]

    def pair(row):
        return y_s[row : row + 2, :]

    jac = [[pair((a * CP + e) * 4) for e in range(CP)] for a in range(2)]
    scaled = [[pair(72 + (2 * i + a) * 4) for a in range(2)] for i in range(3)]
    res = [pair(100 + 4 * a) for a in range(2)]
    w = [y_s[108 + i : 109 + i, :] for i in range(3)]
    same = (y_s[96:97, :] == y_s[97:98, :]).astype(F32)
    f_s[90:128, :] = jnp.zeros((38, MEM), F32)
    g_s[36:40, :] = jnp.zeros((4, MEM), F32)
    for e in range(CP):
        j0, j1 = jac[0][e], jac[1][e]
        red = [scaled[i][0] * j0 + scaled[i][1] * j1 for i in range(3)]
        both = sum(r[0:1] * r[1:2] for r in red) * same
        g_s[2 * e : 2 * e + 2, :] = j0 * res[0] + j1 * res[1] - sum(red[i] * w[i] for i in range(3))
        g_s[18 + 2 * e : 20 + 2 * e, :] = j0 * j0 + j1 * j1 - sum(r * r for r in red) - both
    for n, (e, f) in enumerate(PAIRS):
        f_s[2 * n : 2 * n + 2, :] = jac[0][e] * jac[0][f] + jac[1][e] * jac[1][f]
    feats = f_s[...]
    high = feats.astype(BF16)
    low = (feats - high.astype(F32)).astype(BF16)
    sums = split2(g_s[...])
    hots = [hot(iota((CAMS_CL, MEM), 0).astype(F32) == y_s[96 + q : 97 + q, :]) for q in range(2)]
    camsum = [dot(hots[q], high, NT) + dot(hots[q], low, NT) for q in range(2)]
    camsum = jnp.where((iota((CAMS_CL, 128), 1) & 1) == 0, camsum[0], camsum[1])
    sums = [dot(sums, hots[q], NT) for q in range(2)]
    sums = [x[:40] + x[40:] for x in sums]
    t_s[...] = jnp.where((iota((40, CAMS_CL), 0) & 1) == 0, sums[0], sums[1])
    part = t_s[pl.ds(0, 18, stride=2), :] + t_s[pl.ds(1, 18, stride=2), :]
    lane = iota((ROWS, CAMS_CL), 0)
    spread = hot(iota((ROWS, CAMS_CL), 1) == block * GROUP + ninth(lane))
    lane = iota((18, ROWS), 1)
    damp = jnp.where(iota((18, ROWS), 0) - 9 == lane - 9 * ninth(lane), cam_damp_ref[...], 0.0)
    part = part + dot_exact(damp, spread)

    groups = [y_s[96 + q : 97 + q, :].astype(jnp.int32) >> 3 for q in range(2)]
    lanes = iota((SHARDS, MEM), 0)
    wanted = (lanes == groups[0]) | (lanes == groups[1])
    count = dot(hot(wanted), hot(iota((MEM, MEM), 0) <= iota((MEM, MEM), 1)), NN).astype(jnp.int32)
    slot = count - (offset + 1)
    slot = jnp.where(wanted & (slot < SLOTS), slot, -1)
    most = jnp.max(count, axis=1, keepdims=True)
    here = jnp.minimum(jnp.maximum(most - offset, 0), SLOTS).astype(F32)
    most = jnp.broadcast_to(jnp.max(most, axis=0, keepdims=True).astype(F32), (1, 128))
    feats = split2(y_s[...])
    lane = iota((24, 128), 1)
    for j in range(0, SHARDS, 2):
        wants = jnp.concatenate(
            [jnp.broadcast_to(slot[j + h : j + h + 1], (128, MEM)) for h in range(2)], axis=0
        )
        sent = dot(feats, hot((iota((256, MEM), 0) & 127) == wants), NT)
        sent = sent[:FEAT] + sent[FEAT:]
        for h in range(2):
            to = j + h
            own = sent[:, h * 128 : (h + 1) * 128]
            scaled = own[JROWS : JROWS + 24]
            for third in range(3):
                rows = slice(24 * third, 24 * third + 24)
                out_ref[to, rows, :] = jnp.where(lane < SLOTS, own[rows], pltpu.roll(scaled, SLOTS - 32 * third, 1))
            out_ref[to, 72:76, :] = own[96:100]
            out_ref[to, 76:94, :] = part
            out_ref[to, 94:95, :] = most
            out_ref[to, 95:96, :] = jnp.broadcast_to(here[to : to + 1], (1, 128))
            out_ref[to, 96:104, :] = camsum[to * GROUP : (to + 1) * GROUP]


def sums_kernel(partners_ref, recv_ref, out_ref):
    group = lax.axis_index("pts")
    tot = recv_ref[0, 72:96, :]
    most = tot
    for b in range(1, SHARDS):
        one = recv_ref[b, 72:96, :]
        tot = tot + one
        most = jnp.maximum(most, one)
    tot, most = tot[4:22], most[22:23]
    column = iota((CAMS_CL, WIDTH), 1)
    spread = hot(ninth(column) == iota((CAMS_CL, WIDTH), 0))
    column = iota((CP, WIDTH), 1)
    entry = column - 9 * ninth(column) == iota((CP, WIDTH), 0)
    lines = dot_exact(tot, spread)
    lane = iota((CAMS_CL, 128), 1)
    share = hot((iota((CAMS_CL, 128), 0) == group * GROUP + ninth(lane)) & (lane < ROWS))
    lane = iota((CP, 128), 1)
    entry_share = lane - 9 * ninth(lane) == iota((CP, 128), 0)
    share = dot_exact(tot, share)
    for k in range(2):
        line = total(jnp.where(entry, lines[CP * k : CP * (k + 1)], 0.0))
        for t in range(CP):
            out_ref[CP * k + t : CP * k + t + 1, :] = line[:, t * 128 : (t + 1) * 128]
        out_ref[18 + k : 19 + k, :] = total(jnp.where(entry_share, share[CP * k : CP * (k + 1)], 0.0))
    out_ref[20:21, :] = most
    partners = partners_of(lax.axis_index("cams"), partners_ref)
    out_ref[21:23, :] = jnp.broadcast_to(partners, (2, 128))
    out_ref[23:24, :] = jnp.zeros((1, 128), F32)


def line_up_kernel(recv_ref, buf_s):
    counts = [recv_ref[b, 95, 0].astype(jnp.int32) for b in range(SHARDS)]
    lane = iota((1, 128), 1)
    third = iota((24, 128), 1) >> 5
    at = jnp.int32(0)
    for b in range(SHARDS):
        shift = at & 127
        tile = at >> 7
        jac = recv_ref[b, 0:JROWS, :]
        scaled = [pltpu.roll(jac[24 * h : 24 * h + 24], 128 - SLOTS + 32 * h, 1) for h in range(3)]
        scaled = jnp.where(third == 0, scaled[0], jnp.where(third == 1, scaled[1], scaled[2]))
        filled = ((lane < shift + (SLOTS - 128)) | ((lane >= shift) & (lane < shift + SLOTS))).astype(F32)
        for row, rows, values in ((0, JROWS, jac), (72, 24, scaled), (96, 4, recv_ref[b, JROWS : JROWS + 4, :])):
            moved = pltpu.roll(values, shift, 1)
            moved = moved * filled
            mask = iota((rows, 128), 1) >= shift
            pltpu.store(buf_s.at[tile, row : row + rows, :], moved, mask=mask)
            buf_s[tile + 1, row : row + rows, :] = jnp.where(mask, 0.0, moved)
        at = at + counts[b]
    buf_s[SHARDS + 2, 0:1, :] = jnp.broadcast_to(at.astype(F32), (1, 128))


def rows_kernel(first, recv_ref, buf_s, *refs):
    if first:
        damp_ref, slab_ref, own_s, other_s, turn_s = refs
    else:
        before_ref, slab_ref, own_s, other_s, turn_s = refs
    group = lax.axis_index("pts")
    own_s[...] = jnp.zeros(own_s.shape, F32)
    other_s[...] = jnp.zeros(other_s.shape, F32)

    at = buf_s[SHARDS + 2, 0, 0].astype(jnp.int32)

    def chunk(tile, tiles):
        lanes = 128 * tiles

        def load(row, count):
            return jnp.concatenate([buf_s[tile + h, row : row + count, :] for h in range(tiles)], axis=1)

        numbers = load(96, 4).astype(jnp.int32)
        spots = [numbers[q : q + 1] for q in range(4)]
        masks = [(iota((GROUP, lanes), 0) == spots[q] - group * GROUP).astype(F32) for q in range(2)]
        scaled = [[load(72 + (2 * i + a) * 4, 4) for a in range(2)] for i in range(3)]
        red = [[] for i in range(3)]
        for e in range(CP):
            j0, j1 = load(e * 4, 4), load((CP + e) * 4, 4)
            for i in range(3):
                red[i].append(scaled[i][0] * j0 + scaled[i][1] * j1)
        left = [
            jnp.concatenate([masks[0] * red[i][e][0:1] + masks[1] * red[i][e][1:2] for e in range(CP)], axis=0)
            for i in range(3)
        ]
        for base, size, acc in ((0, CAMS_CL, own_s), (2, 2 * CAMS_CL, other_s)):
            sides = []
            hots = []
            for q in (base, base + 1):
                terms = [sum(left[i] * red[i][e][q : q + 1] for i in range(3)) for e in range(CP)]
                sides.append(split2(jnp.concatenate(terms, axis=0)))
                spot = (spots[q] & 128) + ((spots[q] * CP) & 127)
                hots.append(hot(iota((size, lanes), 0) == spot))
            got = dot(jnp.concatenate(sides, axis=1), jnp.concatenate(hots, axis=1), NT)
            acc[...] -= got[: CP * ROWS] + got[CP * ROWS :]

    def pair(step, carry):
        chunk(2 * step, 2)
        return carry

    tiles = (at + 127) >> 7
    lax.fori_loop(0, tiles >> 1, pair, 0)

    @pl.when((tiles & 1) == 1)
    def _():
        chunk(tiles - 1, 1)

    if first:
        lane = iota((ROWS, 128), 0)
        spread = hot(lane - 9 * ninth(lane) == iota((ROWS, 128), 1))
        damp = jnp.where(ninth(iota((GROUP, ROWS), 1)) == iota((GROUP, ROWS), 0), damp_ref[...], 0.0)
        damp = dot_exact(damp, spread)
        here = (group * GROUP + iota((GROUP, 128), 0)) * CP
        here = (iota((GROUP, 128), 1) == (here & 127)).astype(F32)
        sums = recv_ref[0, 96:104, :]
        for b in range(1, SHARDS):
            sums = sums + recv_ref[b, 96:104, :]
        for n, (e, f) in enumerate(PAIRS):
            term = sums[:, 2 * n : 2 * n + 1] + sums[:, 2 * n + 1 : 2 * n + 2]
            if e == f:
                term = term + damp[:, e : e + 1]
            term = term * here
            for row in {f * ROWS + e * GROUP: 0, e * ROWS + f * GROUP: 0}:
                own_s[row : row + GROUP, :] += term

    column = iota((ROWS, 128), 1)
    for s in range(3):
        parts = []
        for f in range(CP):
            rows = slice(f * ROWS, (f + 1) * ROWS)
            part = own_s[rows, :] if s == 0 else other_s[rows, (s - 1) * 128 : s * 128]
            parts.append(pltpu.roll(part, f, 1))
        for t in range(CP):
            entry = column + t * 128
            entry = entry - 9 * ninth(entry)
            got = parts[0]
            for f in range(1, CP):
                got = jnp.where(entry == f, parts[f], got)
            for e in range(CP):
                turn_s[t, pl.ds(e, GROUP, stride=CP), :] = got[e * GROUP : (e + 1) * GROUP]
            lanes = slice(s * WIDTH + t * 128, s * WIDTH + (t + 1) * 128)
            if first:
                slab_ref[:, lanes] = turn_s[t]
            else:
                slab_ref[:, lanes] = before_ref[:, lanes] + turn_s[t]


def times_rows(slab_ref, line):
    acc = jnp.zeros((ROWS, 128), F32)
    for s in range(3):
        for t in range(CP):
            lanes = slice(s * WIDTH + t * 128, s * WIDTH + (t + 1) * 128)
            acc = acc + slab_ref[:, lanes] * line(s, t)
    return jnp.sum(acc, axis=1, keepdims=True)


def image_kernel(slab_ref, pair_ref, z1_ref, z2_ref, z3_ref, msg_ref, lines_ref):
    cluster = lax.axis_index("cams")
    most = pair_ref[20:21, :]
    for s, ref in enumerate((pair_ref, z1_ref, z2_ref, z3_ref)):
        chip = (cluster >> 1) + s & 3
        for h in range(2):
            lines_ref[2 * chip + (cluster + h & 1)] = ref[24 * h : 24 * h + 24, :]
            most = jnp.maximum(most, ref[24 * h + 20 : 24 * h + 21, :])
    lines_ref[0, 23:24, :] = most
    blocks = [cluster] + [pair_ref[row, 0].astype(jnp.int32) for row in (21, 22)]
    start = [lines_ref[c, 0:CP, :] / lines_ref[c, CP : 2 * CP, :] for c in blocks]
    image = times_rows(slab_ref, lambda s, t: start[s][t : t + 1])
    image = total(image * (iota((ROWS, 128), 1) == iota((ROWS, 128), 0)).astype(F32))
    msg_ref[...] = jnp.broadcast_to(image, msg_ref.shape)


def step_kernel(all_ref, slab_ref, lines_ref, msg_ref, vec_ref, d_s):
    cluster = lax.axis_index("cams")
    mine = lax.axis_index("pts") * NCL + cluster
    column = iota((128, WIDTH), 1)
    spread = dot_exact(all_ref[...], hot(column - ROWS * ((column * 911) >> 16) == iota((128, WIDTH), 0)))
    owner = (iota((NCL, WIDTH), 1) * 911) >> 16
    image = jnp.zeros((NCL, WIDTH), F32)
    for j in range(SHARDS):
        image = jnp.where(owner == j, spread[j * NCL : (j + 1) * NCL], image)

    def whole(x):
        return jnp.sum(total(x), axis=1, keepdims=True)

    def line(row):
        return jnp.concatenate([lines_ref[:, row + t, :] for t in range(CP)], axis=1)

    residual, diag = line(0), line(CP)
    own_diag = lines_ref[cluster, 19:20, :]
    own_diag = jnp.where(iota((1, 128), 1) < ROWS, own_diag, 1.0)
    own_residual = lines_ref[cluster, 18:19, :]
    own_image = all_ref[pl.ds(mine, 1), :]
    direction = residual / diag
    own_direction = own_residual / own_diag
    norm = whole(residual * direction)
    alpha = norm / whole(direction * image)
    residual = residual - alpha * image
    own_residual = own_residual - alpha * own_image
    precond = residual / diag
    norm_next = whole(residual * precond)
    ratio = norm_next / norm
    d_s[...] = precond + ratio * direction
    own = own_residual / own_diag + ratio * own_direction
    blocks = [cluster] + [lines_ref[cluster, row, 0].astype(jnp.int32) for row in (21, 22)]
    lines = [d_s[pl.ds(c, 1), :] for c in blocks]
    acc = times_rows(slab_ref, lambda s, t: lines[s][:, t * 128 : (t + 1) * 128])
    acc = total(acc * (iota((ROWS, 128), 0) == iota((ROWS, 128), 1)).astype(F32))
    msg_ref[...] = jnp.broadcast_to(whole(own * acc), msg_ref.shape)
    vec_ref[0:1, :] = alpha * own_direction
    vec_ref[1:2, :] = own
    vec_ref[2:3, :] = own_residual
    vec_ref[3:4, :] = acc
    vec_ref[4:5, :] = jnp.broadcast_to(norm_next, (1, 128))
    vec_ref[5:8, :] = jnp.zeros((3, 128), F32)


def finish_kernel(all_ref, vec_ref, solution_ref, residual_ref):
    alpha = vec_ref[4:5, :] / total(all_ref[...])
    solution_ref[...] = (vec_ref[0:1, :] + alpha * vec_ref[1:2, :])[:, :ROWS]
    residual_ref[...] = (vec_ref[2:3, :] - alpha * vec_ref[3:4, :])[:, :ROWS]


SMEM = pl.BlockSpec(memory_space=pltpu.SMEM)
VMEM = pl.BlockSpec(memory_space=pltpu.VMEM)


def call(kernel, n_smem, args, outs, scratch=(), cost=None):
    return pl.pallas_call(
        kernel,
        out_shape=[jax.ShapeDtypeStruct(x, jnp.int32 if len(x) == 1 else F32) for x in outs],
        in_specs=[SMEM] * n_smem + [VMEM] * (len(args) - n_smem),
        out_specs=[SMEM if len(x) == 1 else VMEM for x in outs],
        scratch_shapes=[pltpu.VMEM(x, F32) for x in scratch],
        compiler_params=PARAMS,
        cost_estimate=cost,
    )(*args)


def exchange(x, axes):
    return lax.all_to_all(x, axes, 0, 0, tiled=True)


def form_rows(recv, points, other):
    first = other.shape == (1, ROWS)
    scratch = ((CP * ROWS, CAMS_CL), (CP * ROWS, 2 * CAMS_CL), (CP, ROWS, 128))
    return call(
        functools.partial(rows_kernel, first),
        0,
        (recv, points, other),
        [(ROWS, 3 * WIDTH)],
        scratch,
        pl.CostEstimate(flops=8 * 10**9, bytes_accessed=4 * 10**6, transcendentals=0),
    )[0]


def line_up(recv):
    return call(line_up_kernel, 0, (recv,), [(SHARDS + 3, 104, 128)])[0]


def share_vectors(own):
    other = lax.ppermute(own, "cams", [(i, i ^ 1) for i in range(NCL)])
    pair = jnp.concatenate([own, other], axis=0)
    moves = [[((i + 2 * s) % NCL, i) for i in range(NCL)] for s in range(1, 4)]
    return [pair] + [lax.ppermute(pair, "cams", move) for move in moves]


def body(cam_jac, pt_jac, resid, point_damping, obs_camera, members, partners, camera_damping):
    partners = partners.T
    points = (
        partners,
        jnp.transpose(cam_jac, (0, 2, 1, 3)),
        jnp.transpose(pt_jac, (0, 2, 1, 3)),
        resid,
        point_damping.reshape(P_SH // 128, 128),
        obs_camera,
        members[0],
        camera_damping,
    )

    everywhere = ("pts", "cams")

    def send(turn):
        scratch = ((FEAT, P_SH), (FEAT, MEM), (128, MEM), (40, MEM), (40, 128))
        kernel = functools.partial(pack_kernel, len(turn) > 0)
        packed = call(kernel, len(turn), turn + points, [(SHARDS, PAYLOAD, 128)], scratch)[0]
        return exchange(packed, "pts")

    recv = send(())
    vectors = share_vectors(call(sums_kernel, 0, (partners, recv), [(24, 128)])[0])
    slab = form_rows(recv, line_up(recv), camera_damping)

    def first_images(slab):
        outs = [(SHARDS * NCL, 128), (NCL, 24, 128)]
        msg, lines = call(image_kernel, 0, (slab, *vectors), outs)
        return exchange(msg, everywhere), lines

    images, lines = first_images(slab)
    most = lines[0, 23, 0].astype(jnp.int32)

    def more(slab, images):
        def again(state):
            turn, slab = state
            recv = send((turn[None],))
            return (turn + 1, form_rows(recv, line_up(recv), slab))

        slab = lax.while_loop(lambda state: state[0] * SLOTS < most, again, (jnp.int32(1), slab))[1]
        return slab, first_images(slab)[0]

    slab, images = lax.cond(most > SLOTS, more, lambda *so_far: so_far, slab, images)
    outs = [(SHARDS * NCL, 128), (8, 128)]
    msg, vec = call(step_kernel, 0, (images, slab, lines), outs, ((NCL, WIDTH),))
    outs = [(1, ROWS), (1, ROWS)]
    solution, residual = call(finish_kernel, 0, (exchange(msg, everywhere), vec), outs)
    return (slab[None], solution, residual)


def solution(mesh):
    in_specs = (
        P(None, None, None, "pts"),
        P(None, None, None, "pts"),
        P(None, None, "pts"),
        P("pts"),
        P(None, "pts"),
        P("pts", "cams", None),
        P(),
        P("cams", "pts"),
    )
    out_specs = (P("cams", "pts", None), P("cams", "pts"), P("cams", "pts"))
    return jax.shard_map(body, mesh=mesh, in_specs=in_specs, out_specs=out_specs, check_vma=False)
```

```python
import functools

import jax
import jax.numpy as jnp
from jax import lax
from jax.experimental import pallas as pl
from jax.experimental.pallas import tpu as pltpu
from jax.sharding import PartitionSpec as P

CP = 9
CAMS_CL = 128
NCL = 8
SHARDS = 16
P_SH = 2048
MEM = 512
ROWS = 72
GROUP = 8
WIDTH = CP * CAMS_CL
SLOTS = 96
SENT = 100
FEAT = 112
JROWS = 72
PAYLOAD = 104
CHUNK = 256
PAIRS = [(e, f) for e in range(CP) for f in range(e, CP)]

BF16 = jnp.bfloat16
F32 = jnp.float32
PARAMS = pltpu.CompilerParams(vmem_limit_bytes=48 * 1024 * 1024)
NN = (((1,), (0,)), ((), ()))
NT = (((1,), (1,)), ((), ()))


def iota(shape, axis):
    return lax.broadcasted_iota(jnp.int32, shape, axis)


def ninth(value):
    return (value * 7282) >> 16


def split2(value):
    high = value.astype(BF16).astype(F32)
    return jnp.concatenate([high, value - high], axis=0).astype(BF16)


def dot(a, b, dims):
    return lax.dot_general(a, b, dims, preferred_element_type=F32)


def dot_exact(a, onehot):
    high = a.astype(BF16)
    rest = a - high.astype(F32)
    middle = rest.astype(BF16)
    low = (rest - middle.astype(F32)).astype(BF16)
    return dot(high, onehot, NN) + dot(middle, onehot, NN) + dot(low, onehot, NN)


def hot(condition):
    return condition.astype(F32).astype(BF16)


def total(x):
    return jnp.sum(x, axis=0, keepdims=True)


def partners_of(cluster, partners_ref):
    here = jnp.where(iota((2, NCL), 1) == cluster, partners_ref[...], 0)
    return jnp.sum(here.astype(F32), axis=1, keepdims=True)


def pack_kernel(later, *refs):
    offset = refs[0][0] * SLOTS if later else 0
    (partners_ref, cam_ref, pt_ref, resid_ref, damp_ref, ids_ref, members_ref, cam_damp_ref,
     out_ref, x_s, y_s, f_s, g_s, t_s) = refs[1:] if later else refs
    cluster = lax.axis_index("cams")
    block = lax.axis_index("pts")
    first_partner = partners_of(cluster, partners_ref)[0:1].astype(jnp.int32)

    def chunk(step, carry):
        at = pl.ds(pl.multiple_of(step * CHUNK, CHUNK), CHUNK)
        p0, p1, p2 = (jnp.concatenate([pt_ref[0, i, :, at], pt_ref[1, i, :, at]], axis=0) for i in range(3))
        res = jnp.concatenate([resid_ref[0, :, at], resid_ref[1, :, at]], axis=0)
        damp = jnp.concatenate([damp_ref[pl.ds(2 * step + h, 1), :] for h in range(2)], axis=1)
        i00 = 1.0 / jnp.sqrt(total(p0 * p0) + damp)
        l10 = total(p0 * p1) * i00
        l20 = total(p0 * p2) * i00
        i11 = 1.0 / jnp.sqrt(total(p1 * p1) + damp - l10 * l10)
        l21 = (total(p1 * p2) - l20 * l10) * i11
        i22 = 1.0 / jnp.sqrt(total(p2 * p2) + damp - l20 * l20 - l21 * l21)
        b0 = p0 * i00
        b1 = (p1 - l10 * b0) * i11
        b2 = (p2 - l20 * b0 - l21 * b1) * i22
        ids = ids_ref[:, at]
        swap = jnp.broadcast_to(ids[0:1] >> 7, (4, CHUNK)) != cluster

        def turn(x):
            return jnp.where(swap, jnp.concatenate([x[2:4], x[0:2]], axis=0), x)

        for a in range(2):
            for e in range(CP):
                row = (a * CP + e) * 4
                x_s[row : row + 4, at] = turn(cam_ref[a, e, :, at])
        for i, b in enumerate((b0, b1, b2)):
            for a in range(2):
                row = 72 + (2 * i + a) * 4
                x_s[row : row + 4, at] = turn(b[4 * a : 4 * a + 4])
        ids = turn(ids)
        far = (iota((4, CHUNK), 0) >= 2) & ((ids >> 7) != first_partner)
        x_s[96:100, at] = ((ids & 127) + jnp.where(far, CAMS_CL, 0)).astype(F32)
        for a in range(2):
            x_s[100 + 4 * a : 104 + 4 * a, at] = turn(res[4 * a : 4 * a + 4])
        w = [total(b * res) for b in (b0, b1, b2)]
        x_s[108:112, at] = jnp.concatenate(w + [jnp.zeros((1, CHUNK), F32)], axis=0)
        return carry

    lax.fori_loop(0, P_SH // CHUNK, chunk, 0)

    y = dot(split2(x_s[...]), hot(iota((P_SH, MEM), 0) == members_ref[...]), NN)
    y_s[...] = y[:FEAT] + y[FEAT:]

    def pair(row):
        return y_s[row : row + 2, :]

    jac = [[pair((a * CP + e) * 4) for e in range(CP)] for a in range(2)]
    scaled = [[pair(72 + (2 * i + a) * 4) for a in range(2)] for i in range(3)]
    res = [pair(100 + 4 * a) for a in range(2)]
    w = [y_s[108 + i : 109 + i, :] for i in range(3)]
    same = (y_s[96:97, :] == y_s[97:98, :]).astype(F32)
    f_s[90:128, :] = jnp.zeros((38, MEM), F32)
    g_s[36:40, :] = jnp.zeros((4, MEM), F32)
    for e in range(CP):
        j0, j1 = jac[0][e], jac[1][e]
        red = [scaled[i][0] * j0 + scaled[i][1] * j1 for i in range(3)]
        both = sum(r[0:1] * r[1:2] for r in red) * same
        g_s[2 * e : 2 * e + 2, :] = j0 * res[0] + j1 * res[1] - sum(red[i] * w[i] for i in range(3))
        g_s[18 + 2 * e : 20 + 2 * e, :] = j0 * j0 + j1 * j1 - sum(r * r for r in red) - both
    for n, (e, f) in enumerate(PAIRS):
        f_s[2 * n : 2 * n + 2, :] = jac[0][e] * jac[0][f] + jac[1][e] * jac[1][f]
    feats = f_s[...]
    high = feats.astype(BF16)
    low = (feats - high.astype(F32)).astype(BF16)
    sums = split2(g_s[...])
    hots = [hot(iota((CAMS_CL, MEM), 0).astype(F32) == y_s[96 + q : 97 + q, :]) for q in range(2)]
    camsum = [dot(hots[q], high, NT) + dot(hots[q], low, NT) for q in range(2)]
    camsum = jnp.where((iota((CAMS_CL, 128), 1) & 1) == 0, camsum[0], camsum[1])
    sums = [dot(sums, hots[q], NT) for q in range(2)]
    sums = [x[:40] + x[40:] for x in sums]
    t_s[...] = jnp.where((iota((40, CAMS_CL), 0) & 1) == 0, sums[0], sums[1])
    part = t_s[pl.ds(0, 18, stride=2), :] + t_s[pl.ds(1, 18, stride=2), :]
    lane = iota((ROWS, CAMS_CL), 0)
    spread = hot(iota((ROWS, CAMS_CL), 1) == block * GROUP + ninth(lane))
    lane = iota((18, ROWS), 1)
    damp = jnp.where(iota((18, ROWS), 0) - 9 == lane - 9 * ninth(lane), cam_damp_ref[...], 0.0)
    part = part + dot_exact(damp, spread)

    groups = [y_s[96 + q : 97 + q, :].astype(jnp.int32) >> 3 for q in range(2)]
    lanes = iota((SHARDS, MEM), 0)
    wanted = (lanes == groups[0]) | (lanes == groups[1])
    count = dot(hot(wanted), hot(iota((MEM, MEM), 0) <= iota((MEM, MEM), 1)), NN).astype(jnp.int32)
    slot = count - (offset + 1)
    slot = jnp.where(wanted & (slot < SLOTS), slot, -1)
    most = jnp.max(count, axis=1, keepdims=True)
    here = jnp.minimum(jnp.maximum(most - offset, 0), SLOTS).astype(F32)
    most = jnp.broadcast_to(jnp.max(most, axis=0, keepdims=True).astype(F32), (1, 128))
    feats = split2(y_s[...])
    lane = iota((24, 128), 1)
    for j in range(0, SHARDS, 2):
        wants = jnp.concatenate(
            [jnp.broadcast_to(slot[j + h : j + h + 1], (128, MEM)) for h in range(2)], axis=0
        )
        sent = dot(feats, hot((iota((256, MEM), 0) & 127) == wants), NT)
        sent = sent[:FEAT] + sent[FEAT:]
        for h in range(2):
            to = j + h
            own = sent[:, h * 128 : (h + 1) * 128]
            scaled = own[JROWS : JROWS + 24]
            for third in range(3):
                rows = slice(24 * third, 24 * third + 24)
                out_ref[to, rows, :] = jnp.where(lane < SLOTS, own[rows], pltpu.roll(scaled, SLOTS - 32 * third, 1))
            out_ref[to, 72:76, :] = own[96:100]
            out_ref[to, 76:94, :] = part
            out_ref[to, 94:95, :] = most
            out_ref[to, 95:96, :] = jnp.broadcast_to(here[to : to + 1], (1, 128))
            out_ref[to, 96:104, :] = camsum[to * GROUP : (to + 1) * GROUP]


def sums_kernel(partners_ref, recv_ref, out_ref):
    group = lax.axis_index("pts")
    tot = recv_ref[0, 72:96, :]
    most = tot
    for b in range(1, SHARDS):
        one = recv_ref[b, 72:96, :]
        tot = tot + one
        most = jnp.maximum(most, one)
    tot, most = tot[4:22], most[22:23]
    column = iota((CAMS_CL, WIDTH), 1)
    spread = hot(ninth(column) == iota((CAMS_CL, WIDTH), 0))
    column = iota((CP, WIDTH), 1)
    entry = column - 9 * ninth(column) == iota((CP, WIDTH), 0)
    lines = dot_exact(tot, spread)
    lane = iota((CAMS_CL, 128), 1)
    share = hot((iota((CAMS_CL, 128), 0) == group * GROUP + ninth(lane)) & (lane < ROWS))
    lane = iota((CP, 128), 1)
    entry_share = lane - 9 * ninth(lane) == iota((CP, 128), 0)
    share = dot_exact(tot, share)
    for k in range(2):
        line = total(jnp.where(entry, lines[CP * k : CP * (k + 1)], 0.0))
        for t in range(CP):
            out_ref[CP * k + t : CP * k + t + 1, :] = line[:, t * 128 : (t + 1) * 128]
        out_ref[18 + k : 19 + k, :] = total(jnp.where(entry_share, share[CP * k : CP * (k + 1)], 0.0))
    out_ref[20:21, :] = most
    partners = partners_of(lax.axis_index("cams"), partners_ref)
    out_ref[21:23, :] = jnp.broadcast_to(partners, (2, 128))
    out_ref[23:24, :] = jnp.zeros((1, 128), F32)


def line_up_kernel(recv_ref, buf_s):
    counts = [recv_ref[b, 95, 0].astype(jnp.int32) for b in range(SHARDS)]
    lane = iota((1, 128), 1)
    third = iota((24, 128), 1) >> 5
    at = jnp.int32(0)
    for b in range(SHARDS):
        shift = at & 127
        tile = at >> 7
        jac = recv_ref[b, 0:JROWS, :]
        scaled = [pltpu.roll(jac[24 * h : 24 * h + 24], 128 - SLOTS + 32 * h, 1) for h in range(3)]
        scaled = jnp.where(third == 0, scaled[0], jnp.where(third == 1, scaled[1], scaled[2]))
        filled = ((lane < shift + (SLOTS - 128)) | ((lane >= shift) & (lane < shift + SLOTS))).astype(F32)
        for row, rows, values in ((0, JROWS, jac), (72, 24, scaled), (96, 4, recv_ref[b, JROWS : JROWS + 4, :])):
            moved = pltpu.roll(values, shift, 1)
            moved = moved * filled
            mask = iota((rows, 128), 1) >= shift
            pltpu.store(buf_s.at[tile, row : row + rows, :], moved, mask=mask)
            buf_s[tile + 1, row : row + rows, :] = jnp.where(mask, 0.0, moved)
        at = at + counts[b]
    buf_s[SHARDS + 2, 0:1, :] = jnp.broadcast_to(at.astype(F32), (1, 128))


def rows_kernel(first, recv_ref, buf_s, *refs):
    if first:
        damp_ref, slab_ref, own_s, other_s, turn_s = refs
    else:
        before_ref, slab_ref, own_s, other_s, turn_s = refs
    group = lax.axis_index("pts")
    own_s[...] = jnp.zeros(own_s.shape, F32)
    other_s[...] = jnp.zeros(other_s.shape, F32)

    at = buf_s[SHARDS + 2, 0, 0].astype(jnp.int32)

    def chunk(tile, tiles):
        lanes = 128 * tiles

        def load(row, count):
            return jnp.concatenate([buf_s[tile + h, row : row + count, :] for h in range(tiles)], axis=1)

        numbers = load(96, 4).astype(jnp.int32)
        spots = [numbers[q : q + 1] for q in range(4)]
        masks = [(iota((GROUP, lanes), 0) == spots[q] - group * GROUP).astype(F32) for q in range(2)]
        scaled = [[load(72 + (2 * i + a) * 4, 4) for a in range(2)] for i in range(3)]
        red = [[] for i in range(3)]
        for e in range(CP):
            j0, j1 = load(e * 4, 4), load((CP + e) * 4, 4)
            for i in range(3):
                red[i].append(scaled[i][0] * j0 + scaled[i][1] * j1)
        left = [
            jnp.concatenate([masks[0] * red[i][e][0:1] + masks[1] * red[i][e][1:2] for e in range(CP)], axis=0)
            for i in range(3)
        ]
        for base, size, acc in ((0, CAMS_CL, own_s), (2, 2 * CAMS_CL, other_s)):
            sides = []
            hots = []
            for q in (base, base + 1):
                terms = [sum(left[i] * red[i][e][q : q + 1] for i in range(3)) for e in range(CP)]
                sides.append(split2(jnp.concatenate(terms, axis=0)))
                spot = (spots[q] & 128) + ((spots[q] * CP) & 127)
                hots.append(hot(iota((size, lanes), 0) == spot))
            got = dot(jnp.concatenate(sides, axis=1), jnp.concatenate(hots, axis=1), NT)
            acc[...] -= got[: CP * ROWS] + got[CP * ROWS :]

    def pair(step, carry):
        chunk(2 * step, 2)
        return carry

    tiles = (at + 127) >> 7
    lax.fori_loop(0, tiles >> 1, pair, 0)

    @pl.when((tiles & 1) == 1)
    def _():
        chunk(tiles - 1, 1)

    if first:
        lane = iota((ROWS, 128), 0)
        spread = hot(lane - 9 * ninth(lane) == iota((ROWS, 128), 1))
        damp = jnp.where(ninth(iota((GROUP, ROWS), 1)) == iota((GROUP, ROWS), 0), damp_ref[...], 0.0)
        damp = dot_exact(damp, spread)
        here = (group * GROUP + iota((GROUP, 128), 0)) * CP
        here = (iota((GROUP, 128), 1) == (here & 127)).astype(F32)
        sums = recv_ref[0, 96:104, :]
        for b in range(1, SHARDS):
            sums = sums + recv_ref[b, 96:104, :]
        for n, (e, f) in enumerate(PAIRS):
            term = sums[:, 2 * n : 2 * n + 1] + sums[:, 2 * n + 1 : 2 * n + 2]
            if e == f:
                term = term + damp[:, e : e + 1]
            term = term * here
            for row in {f * ROWS + e * GROUP: 0, e * ROWS + f * GROUP: 0}:
                own_s[row : row + GROUP, :] += term

    column = iota((ROWS, 128), 1)
    for s in range(3):
        parts = []
        for f in range(CP):
            rows = slice(f * ROWS, (f + 1) * ROWS)
            part = own_s[rows, :] if s == 0 else other_s[rows, (s - 1) * 128 : s * 128]
            parts.append(pltpu.roll(part, f, 1))
        for t in range(CP):
            entry = column + t * 128
            entry = entry - 9 * ninth(entry)
            got = parts[0]
            for f in range(1, CP):
                got = jnp.where(entry == f, parts[f], got)
            for e in range(CP):
                turn_s[t, pl.ds(e, GROUP, stride=CP), :] = got[e * GROUP : (e + 1) * GROUP]
            lanes = slice(s * WIDTH + t * 128, s * WIDTH + (t + 1) * 128)
            if first:
                slab_ref[:, lanes] = turn_s[t, 0:ROWS, :]
            else:
                slab_ref[:, lanes] = before_ref[:, lanes] + turn_s[t, 0:ROWS, :]


def times_rows(slab_ref, line):
    acc = jnp.zeros((ROWS, 128), F32)
    for s in range(3):
        for t in range(CP):
            lanes = slice(s * WIDTH + t * 128, s * WIDTH + (t + 1) * 128)
            acc = acc + slab_ref[:, lanes] * line(s, t)
    return jnp.sum(acc, axis=1, keepdims=True)


def image_kernel(slab_ref, pair_ref, z1_ref, z2_ref, z3_ref, msg_ref, lines_ref):
    cluster = lax.axis_index("cams")
    most = pair_ref[20:21, :]
    for s, ref in enumerate((pair_ref, z1_ref, z2_ref, z3_ref)):
        chip = (cluster >> 1) + s & 3
        for h in range(2):
            lines_ref[2 * chip + (cluster + h & 1)] = ref[24 * h : 24 * h + 24, :]
            most = jnp.maximum(most, ref[24 * h + 20 : 24 * h + 21, :])
    lines_ref[0, 23:24, :] = most
    blocks = [cluster] + [pair_ref[row, 0].astype(jnp.int32) for row in (21, 22)]
    start = [lines_ref[c, 0:CP, :] / lines_ref[c, CP : 2 * CP, :] for c in blocks]
    image = times_rows(slab_ref, lambda s, t: start[s][t : t + 1])
    image = total(image * (iota((ROWS, 128), 1) == iota((ROWS, 128), 0)).astype(F32))
    msg_ref[...] = jnp.broadcast_to(image, msg_ref.shape)


def step_kernel(all_ref, slab_ref, lines_ref, msg_ref, vec_ref, d_s):
    cluster = lax.axis_index("cams")
    mine = lax.axis_index("pts") * NCL + cluster
    column = iota((128, WIDTH), 1)
    spread = dot_exact(all_ref[...], hot(column - ROWS * ((column * 911) >> 16) == iota((128, WIDTH), 0)))
    owner = (iota((NCL, WIDTH), 1) * 911) >> 16
    image = jnp.zeros((NCL, WIDTH), F32)
    for j in range(SHARDS):
        image = jnp.where(owner == j, spread[j * NCL : (j + 1) * NCL], image)

    def whole(x):
        return jnp.sum(total(x), axis=1, keepdims=True)

    def line(row):
        return jnp.concatenate([lines_ref[:, row + t, :] for t in range(CP)], axis=1)

    residual, diag = line(0), line(CP)
    own_diag = lines_ref[cluster, 19:20, :]
    own_diag = jnp.where(iota((1, 128), 1) < ROWS, own_diag, 1.0)
    own_residual = lines_ref[cluster, 18:19, :]
    own_image = all_ref[pl.ds(mine, 1), :]
    direction = residual / diag
    own_direction = own_residual / own_diag
    norm = whole(residual * direction)
    alpha = norm / whole(direction * image)
    residual = residual - alpha * image
    own_residual = own_residual - alpha * own_image
    precond = residual / diag
    norm_next = whole(residual * precond)
    ratio = norm_next / norm
    d_s[...] = precond + ratio * direction
    own = own_residual / own_diag + ratio * own_direction
    blocks = [cluster] + [lines_ref[cluster, row, 0].astype(jnp.int32) for row in (21, 22)]
    lines = [d_s[pl.ds(c, 1), :] for c in blocks]
    acc = times_rows(slab_ref, lambda s, t: lines[s][:, t * 128 : (t + 1) * 128])
    acc = total(acc * (iota((ROWS, 128), 0) == iota((ROWS, 128), 1)).astype(F32))
    msg_ref[...] = jnp.broadcast_to(whole(own * acc), msg_ref.shape)
    vec_ref[0:1, :] = alpha * own_direction
    vec_ref[1:2, :] = own
    vec_ref[2:3, :] = own_residual
    vec_ref[3:4, :] = acc
    vec_ref[4:5, :] = jnp.broadcast_to(norm_next, (1, 128))
    vec_ref[5:8, :] = jnp.zeros((3, 128), F32)


def finish_kernel(all_ref, vec_ref, solution_ref, residual_ref):
    alpha = vec_ref[4:5, :] / total(all_ref[...])
    solution_ref[...] = (vec_ref[0:1, :] + alpha * vec_ref[1:2, :])[:, :ROWS]
    residual_ref[...] = (vec_ref[2:3, :] - alpha * vec_ref[3:4, :])[:, :ROWS]


SMEM = pl.BlockSpec(memory_space=pltpu.SMEM)
VMEM = pl.BlockSpec(memory_space=pltpu.VMEM)


def call(kernel, n_smem, args, outs, scratch=(), cost=None):
    return pl.pallas_call(
        kernel,
        out_shape=[jax.ShapeDtypeStruct(x, jnp.int32 if len(x) == 1 else F32) for x in outs],
        in_specs=[SMEM] * n_smem + [VMEM] * (len(args) - n_smem),
        out_specs=[SMEM if len(x) == 1 else VMEM for x in outs],
        scratch_shapes=[pltpu.VMEM(x, F32) for x in scratch],
        compiler_params=PARAMS,
        cost_estimate=cost,
    )(*args)


def exchange(x, axes):
    return lax.all_to_all(x, axes, 0, 0, tiled=True)


def form_rows(recv, points, other):
    first = other.shape == (1, ROWS)
    scratch = ((CP * ROWS, CAMS_CL), (CP * ROWS, 2 * CAMS_CL), (CP, ROWS + 8, 128))
    return call(
        functools.partial(rows_kernel, first),
        0,
        (recv, points, other),
        [(ROWS, 3 * WIDTH)],
        scratch,
        pl.CostEstimate(flops=8 * 10**9, bytes_accessed=4 * 10**6, transcendentals=0),
    )[0]


def line_up(recv):
    return call(line_up_kernel, 0, (recv,), [(SHARDS + 3, 104, 128)])[0]


def share_vectors(own):
    other = lax.ppermute(own, "cams", [(i, i ^ 1) for i in range(NCL)])
    pair = jnp.concatenate([own, other], axis=0)
    moves = [[((i + 2 * s) % NCL, i) for i in range(NCL)] for s in range(1, 4)]
    return [pair] + [lax.ppermute(pair, "cams", move) for move in moves]


def body(cam_jac, pt_jac, resid, point_damping, obs_camera, members, partners, camera_damping):
    partners = partners.T
    points = (
        partners,
        jnp.transpose(cam_jac, (0, 2, 1, 3)),
        jnp.transpose(pt_jac, (0, 2, 1, 3)),
        resid,
        point_damping.reshape(P_SH // 128, 128),
        obs_camera,
        members[0],
        camera_damping,
    )

    everywhere = ("pts", "cams")

    def send(turn):
        scratch = ((FEAT, P_SH), (FEAT, MEM), (128, MEM), (40, MEM), (40, 128))
        kernel = functools.partial(pack_kernel, len(turn) > 0)
        packed = call(kernel, len(turn), turn + points, [(SHARDS, PAYLOAD, 128)], scratch)[0]
        return exchange(packed, "pts")

    recv = send(())
    vectors = share_vectors(call(sums_kernel, 0, (partners, recv), [(24, 128)])[0])
    slab = form_rows(recv, line_up(recv), camera_damping)

    def first_images(slab):
        outs = [(SHARDS * NCL, 128), (NCL, 24, 128)]
        msg, lines = call(image_kernel, 0, (slab, *vectors), outs)
        return exchange(msg, everywhere), lines

    images, lines = first_images(slab)
    most = lines[0, 23, 0].astype(jnp.int32)

    def more(slab, images):
        def again(state):
            turn, slab = state
            recv = send((turn[None],))
            return (turn + 1, form_rows(recv, line_up(recv), slab))

        slab = lax.while_loop(lambda state: state[0] * SLOTS < most, again, (jnp.int32(1), slab))[1]
        return slab, first_images(slab)[0]

    slab, images = lax.cond(most > SLOTS, more, lambda *so_far: so_far, slab, images)
    outs = [(SHARDS * NCL, 128), (8, 128)]
    msg, vec = call(step_kernel, 0, (images, slab, lines), outs, ((NCL, WIDTH),))
    outs = [(1, ROWS), (1, ROWS)]
    solution, residual = call(finish_kernel, 0, (exchange(msg, everywhere), vec), outs)
    return (slab[None], solution, residual)


def solution(mesh):
    in_specs = (
        P(None, None, None, "pts"),
        P(None, None, None, "pts"),
        P(None, None, "pts"),
        P("pts"),
        P(None, "pts"),
        P("pts", "cams", None),
        P(),
        P("cams", "pts"),
    )
    out_specs = (P("cams", "pts", None), P("cams", "pts"), P("cams", "pts"))
    return jax.shard_map(body, mesh=mesh, in_specs=in_specs, out_specs=out_specs, check_vma=False)
```

```python
import functools

import jax
import jax.numpy as jnp
from jax import lax
from jax.experimental import pallas as pl
from jax.experimental.pallas import tpu as pltpu
from jax.sharding import PartitionSpec as P

CP = 9
CAMS_CL = 128
NCL = 8
SHARDS = 16
P_SH = 2048
MEM = 512
ROWS = 72
GROUP = 8
WIDTH = CP * CAMS_CL
SLOTS = 96
SENT = 100
FEAT = 112
JROWS = 72
PAYLOAD = 96
CHUNK = 256
PAIRS = [(e, f) for e in range(CP) for f in range(e, CP)]

BF16 = jnp.bfloat16
F32 = jnp.float32
PARAMS = pltpu.CompilerParams(vmem_limit_bytes=48 * 1024 * 1024)
NN = (((1,), (0,)), ((), ()))
NT = (((1,), (1,)), ((), ()))


def iota(shape, axis):
    return lax.broadcasted_iota(jnp.int32, shape, axis)


def ninth(value):
    return (value * 7282) >> 16


def split2(value):
    high = value.astype(BF16).astype(F32)
    return jnp.concatenate([high, value - high], axis=0).astype(BF16)


def dot(a, b, dims):
    return lax.dot_general(a, b, dims, preferred_element_type=F32)


def dot_exact(a, onehot):
    high = a.astype(BF16)
    rest = a - high.astype(F32)
    middle = rest.astype(BF16)
    low = (rest - middle.astype(F32)).astype(BF16)
    return dot(high, onehot, NN) + dot(middle, onehot, NN) + dot(low, onehot, NN)


def hot(condition):
    return condition.astype(F32).astype(BF16)


def total(x):
    return jnp.sum(x, axis=0, keepdims=True)


def partners_of(cluster, partners_ref):
    here = jnp.where(iota((2, NCL), 1) == cluster, partners_ref[...], 0)
    return jnp.sum(here.astype(F32), axis=1, keepdims=True)


def pack_kernel(later, *refs):
    offset = refs[0][0] * SLOTS if later else 0
    (partners_ref, cam_ref, pt_ref, resid_ref, damp_ref, ids_ref, members_ref, cam_damp_ref,
     out_ref, x_s, y_s, f_s, g_s, t_s) = refs[1:] if later else refs
    cluster = lax.axis_index("cams")
    block = lax.axis_index("pts")
    first_partner = partners_of(cluster, partners_ref)[0:1].astype(jnp.int32)

    def chunk(step, carry):
        at = pl.ds(pl.multiple_of(step * CHUNK, CHUNK), CHUNK)
        p0, p1, p2 = (jnp.concatenate([pt_ref[0, i, :, at], pt_ref[1, i, :, at]], axis=0) for i in range(3))
        res = jnp.concatenate([resid_ref[0, :, at], resid_ref[1, :, at]], axis=0)
        damp = jnp.concatenate([damp_ref[pl.ds(2 * step + h, 1), :] for h in range(2)], axis=1)
        i00 = 1.0 / jnp.sqrt(total(p0 * p0) + damp)
        l10 = total(p0 * p1) * i00
        l20 = total(p0 * p2) * i00
        i11 = 1.0 / jnp.sqrt(total(p1 * p1) + damp - l10 * l10)
        l21 = (total(p1 * p2) - l20 * l10) * i11
        i22 = 1.0 / jnp.sqrt(total(p2 * p2) + damp - l20 * l20 - l21 * l21)
        b0 = p0 * i00
        b1 = (p1 - l10 * b0) * i11
        b2 = (p2 - l20 * b0 - l21 * b1) * i22
        ids = ids_ref[:, at]
        swap = jnp.broadcast_to(ids[0:1] >> 7, (4, CHUNK)) != cluster

        def turn(x):
            return jnp.where(swap, jnp.concatenate([x[2:4], x[0:2]], axis=0), x)

        for a in range(2):
            for e in range(CP):
                row = (a * CP + e) * 4
                x_s[row : row + 4, at] = turn(cam_ref[a, e, :, at])
        for i, b in enumerate((b0, b1, b2)):
            for a in range(2):
                row = 72 + (2 * i + a) * 4
                x_s[row : row + 4, at] = turn(b[4 * a : 4 * a + 4])
        ids = turn(ids)
        far = (iota((4, CHUNK), 0) >= 2) & ((ids >> 7) != first_partner)
        x_s[96:100, at] = ((ids & 127) + jnp.where(far, CAMS_CL, 0)).astype(F32)
        for a in range(2):
            x_s[100 + 4 * a : 104 + 4 * a, at] = turn(res[4 * a : 4 * a + 4])
        w = [total(b * res) for b in (b0, b1, b2)]
        x_s[108:112, at] = jnp.concatenate(w + [jnp.zeros((1, CHUNK), F32)], axis=0)
        return carry

    lax.fori_loop(0, P_SH // CHUNK, chunk, 0)

    y = dot(split2(x_s[...]), hot(iota((P_SH, MEM), 0) == members_ref[...]), NN)
    y_s[...] = y[:FEAT] + y[FEAT:]

    def pair(row):
        return y_s[row : row + 2, :]

    jac = [[pair((a * CP + e) * 4) for e in range(CP)] for a in range(2)]
    scaled = [[pair(72 + (2 * i + a) * 4) for a in range(2)] for i in range(3)]
    res = [pair(100 + 4 * a) for a in range(2)]
    w = [y_s[108 + i : 109 + i, :] for i in range(3)]
    same = (y_s[96:97, :] == y_s[97:98, :]).astype(F32)
    f_s[90:128, :] = jnp.zeros((38, MEM), F32)
    g_s[36:40, :] = jnp.zeros((4, MEM), F32)
    for e in range(CP):
        j0, j1 = jac[0][e], jac[1][e]
        red = [scaled[i][0] * j0 + scaled[i][1] * j1 for i in range(3)]
        both = sum(r[0:1] * r[1:2] for r in red) * same
        g_s[2 * e : 2 * e + 2, :] = j0 * res[0] + j1 * res[1] - sum(red[i] * w[i] for i in range(3))
        g_s[18 + 2 * e : 20 + 2 * e, :] = j0 * j0 + j1 * j1 - sum(r * r for r in red) - both
    for n, (e, f) in enumerate(PAIRS):
        f_s[2 * n : 2 * n + 2, :] = jac[0][e] * jac[0][f] + jac[1][e] * jac[1][f]
    feats = f_s[...]
    high = feats.astype(BF16)
    low = (feats - high.astype(F32)).astype(BF16)
    sums = split2(g_s[...])
    hots = [hot(iota((CAMS_CL, MEM), 0).astype(F32) == y_s[96 + q : 97 + q, :]) for q in range(2)]
    camsum = [dot(hots[q], high, NT) + dot(hots[q], low, NT) for q in range(2)]
    camsum = jnp.where((iota((CAMS_CL, 128), 1) & 1) == 0, camsum[0], camsum[1])
    sums = [dot(sums, hots[q], NT) for q in range(2)]
    sums = [x[:40] + x[40:] for x in sums]
    t_s[...] = jnp.where((iota((40, CAMS_CL), 0) & 1) == 0, sums[0], sums[1])
    part = t_s[pl.ds(0, 18, stride=2), :] + t_s[pl.ds(1, 18, stride=2), :]
    lane = iota((ROWS, CAMS_CL), 0)
    spread = hot(iota((ROWS, CAMS_CL), 1) == block * GROUP + ninth(lane))
    lane = iota((18, ROWS), 1)
    damp = jnp.where(iota((18, ROWS), 0) - 9 == lane - 9 * ninth(lane), cam_damp_ref[...], 0.0)
    part = part + dot_exact(damp, spread)

    groups = [y_s[96 + q : 97 + q, :].astype(jnp.int32) >> 3 for q in range(2)]
    lanes = iota((SHARDS, MEM), 0)
    wanted = (lanes == groups[0]) | (lanes == groups[1])
    count = dot(hot(wanted), hot(iota((MEM, MEM), 0) <= iota((MEM, MEM), 1)), NN).astype(jnp.int32)
    slot = count - (offset + 1)
    slot = jnp.where(wanted & (slot < SLOTS), slot, -1)
    most = jnp.max(count, axis=1, keepdims=True)
    here = jnp.minimum(jnp.maximum(most - offset, 0), SLOTS).astype(F32)
    most = jnp.broadcast_to(jnp.max(most, axis=0, keepdims=True).astype(F32), (1, 128))
    feats = split2(y_s[...])
    lane = iota((128, 384), 1)
    flat = dot_exact(camsum, hot((iota((128, 384), 0) >> 1) == (lane >> 3)))
    flat = jnp.where((lane & 7) == (iota((128, 384), 0) & 7), flat, 0.0)
    flat = jnp.sum(flat.reshape(SHARDS, GROUP, 384), axis=1)
    lane = iota((SHARDS, 128), 1)
    tail = jnp.where((lane >> 3) == 13, here, jnp.where((lane >> 3) == 14, most, flat[:, 256:384]))
    tails = [pltpu.roll(tail, SLOTS - 32 * q, 1) if q < 3 else tail for q in range(4)]
    lane = iota((24, 128), 1)
    for j in range(0, SHARDS, 2):
        wants = jnp.concatenate(
            [jnp.broadcast_to(slot[j + h : j + h + 1], (128, MEM)) for h in range(2)], axis=0
        )
        sent = dot(feats, hot((iota((256, MEM), 0) & 127) == wants), NT)
        sent = sent[:FEAT] + sent[FEAT:]
        for h in range(2):
            to = j + h
            own = sent[:, h * 128 : (h + 1) * 128]
            scaled = own[JROWS : JROWS + 24]
            for third in range(3):
                rows = slice(24 * third, 24 * third + 24)
                out_ref[to, rows, :] = jnp.where(lane < SLOTS, own[rows], pltpu.roll(scaled, SLOTS - 32 * third, 1))
            beside = jnp.concatenate([tails[q][to : to + 1] for q in range(4)], axis=0)
            out_ref[to, 72:76, :] = jnp.where(lane[0:4] < SLOTS, own[96:100], beside)
            out_ref[to, 76:94, :] = part
            out_ref[to, 94:95, :] = flat[to : to + 1, 0:128]
            out_ref[to, 95:96, :] = flat[to : to + 1, 128:256]


def sums_kernel(partners_ref, recv_ref, out_ref):
    group = lax.axis_index("pts")
    tot = recv_ref[0, 72:96, :]
    most = tot
    for b in range(1, SHARDS):
        one = recv_ref[b, 72:96, :]
        tot = tot + one
        most = jnp.maximum(most, one)
    tot, most = tot[4:22], jnp.broadcast_to(most[3:4, 112:113], (1, 128))
    column = iota((CAMS_CL, WIDTH), 1)
    spread = hot(ninth(column) == iota((CAMS_CL, WIDTH), 0))
    column = iota((CP, WIDTH), 1)
    entry = column - 9 * ninth(column) == iota((CP, WIDTH), 0)
    lines = dot_exact(tot, spread)
    lane = iota((CAMS_CL, 128), 1)
    share = hot((iota((CAMS_CL, 128), 0) == group * GROUP + ninth(lane)) & (lane < ROWS))
    lane = iota((CP, 128), 1)
    entry_share = lane - 9 * ninth(lane) == iota((CP, 128), 0)
    share = dot_exact(tot, share)
    for k in range(2):
        line = total(jnp.where(entry, lines[CP * k : CP * (k + 1)], 0.0))
        for t in range(CP):
            out_ref[CP * k + t : CP * k + t + 1, :] = line[:, t * 128 : (t + 1) * 128]
        out_ref[18 + k : 19 + k, :] = total(jnp.where(entry_share, share[CP * k : CP * (k + 1)], 0.0))
    out_ref[20:21, :] = most
    partners = partners_of(lax.axis_index("cams"), partners_ref)
    out_ref[21:23, :] = jnp.broadcast_to(partners, (2, 128))
    out_ref[23:24, :] = jnp.zeros((1, 128), F32)


def line_up_kernel(recv_ref, buf_s):
    counts = [recv_ref[b, 75, 104].astype(jnp.int32) for b in range(SHARDS)]
    lane = iota((1, 128), 1)
    third = iota((24, 128), 1) >> 5
    at = jnp.int32(0)
    for b in range(SHARDS):
        shift = at & 127
        tile = at >> 7
        jac = recv_ref[b, 0:JROWS, :]
        scaled = [pltpu.roll(jac[24 * h : 24 * h + 24], 128 - SLOTS + 32 * h, 1) for h in range(3)]
        scaled = jnp.where(third == 0, scaled[0], jnp.where(third == 1, scaled[1], scaled[2]))
        filled = ((lane < shift + (SLOTS - 128)) | ((lane >= shift) & (lane < shift + SLOTS))).astype(F32)
        for row, rows, values in ((0, JROWS, jac), (72, 24, scaled), (96, 4, recv_ref[b, JROWS : JROWS + 4, :])):
            moved = pltpu.roll(values, shift, 1)
            moved = moved * filled
            mask = iota((rows, 128), 1) >= shift
            pltpu.store(buf_s.at[tile, row : row + rows, :], moved, mask=mask)
            buf_s[tile + 1, row : row + rows, :] = jnp.where(mask, 0.0, moved)
        at = at + counts[b]
    buf_s[SHARDS + 2, 0:1, :] = jnp.broadcast_to(at.astype(F32), (1, 128))


def rows_kernel(first, recv_ref, buf_s, *refs):
    if first:
        damp_ref, slab_ref, own_s, other_s, turn_s = refs
    else:
        before_ref, slab_ref, own_s, other_s, turn_s = refs
    group = lax.axis_index("pts")
    own_s[...] = jnp.zeros(own_s.shape, F32)
    other_s[...] = jnp.zeros(other_s.shape, F32)

    at = buf_s[SHARDS + 2, 0, 0].astype(jnp.int32)

    def chunk(tile, tiles):
        lanes = 128 * tiles

        def load(row, count):
            return jnp.concatenate([buf_s[tile + h, row : row + count, :] for h in range(tiles)], axis=1)

        numbers = load(96, 4).astype(jnp.int32)
        spots = [numbers[q : q + 1] for q in range(4)]
        masks = [(iota((GROUP, lanes), 0) == spots[q] - group * GROUP).astype(F32) for q in range(2)]
        scaled = [[load(72 + (2 * i + a) * 4, 4) for a in range(2)] for i in range(3)]
        red = [[] for i in range(3)]
        for e in range(CP):
            j0, j1 = load(e * 4, 4), load((CP + e) * 4, 4)
            for i in range(3):
                red[i].append(scaled[i][0] * j0 + scaled[i][1] * j1)
        left = [
            jnp.concatenate([masks[0] * red[i][e][0:1] + masks[1] * red[i][e][1:2] for e in range(CP)], axis=0)
            for i in range(3)
        ]
        for base, size, acc in ((0, CAMS_CL, own_s), (2, 2 * CAMS_CL, other_s)):
            sides = []
            hots = []
            for q in (base, base + 1):
                terms = [sum(left[i] * red[i][e][q : q + 1] for i in range(3)) for e in range(CP)]
                sides.append(split2(jnp.concatenate(terms, axis=0)))
                spot = (spots[q] & 128) + ((spots[q] * CP) & 127)
                hots.append(hot(iota((size, lanes), 0) == spot))
            got = dot(jnp.concatenate(sides, axis=1), jnp.concatenate(hots, axis=1), NT)
            acc[...] -= got[: CP * ROWS] + got[CP * ROWS :]

    def pair(step, carry):
        chunk(2 * step, 2)
        return carry

    tiles = (at + 127) >> 7
    lax.fori_loop(0, tiles >> 1, pair, 0)

    @pl.when((tiles & 1) == 1)
    def _():
        chunk(tiles - 1, 1)

    if first:
        lane = iota((ROWS, 128), 0)
        spread = hot(lane - 9 * ninth(lane) == iota((ROWS, 128), 1))
        damp = jnp.where(ninth(iota((GROUP, ROWS), 1)) == iota((GROUP, ROWS), 0), damp_ref[...], 0.0)
        damp = dot_exact(damp, spread)
        here = (group * GROUP + iota((GROUP, 128), 0)) * CP
        here = (iota((GROUP, 128), 1) == (here & 127)).astype(F32)
        sums = recv_ref[0, 72:96, :]
        for b in range(1, SHARDS):
            sums = sums + recv_ref[b, 72:96, :]
        lane = iota((1, 128), 1) >> 5
        tail = sums[3:4]
        for q in range(3):
            tail = jnp.where(lane == q, pltpu.roll(sums[q : q + 1], 128 - SLOTS + 32 * q, 1), tail)
        flat = jnp.concatenate([sums[22:23], sums[23:24], tail], axis=1)
        flat = jnp.where((iota((GROUP, 384), 1) & 7) == iota((GROUP, 384), 0), flat, 0.0)
        lane = iota((384, 128), 1)
        sums = dot_exact(flat, hot(((iota((384, 128), 0) >> 3) == lane) & (lane < len(PAIRS))))
        for n, (e, f) in enumerate(PAIRS):
            term = sums[:, n : n + 1]
            if e == f:
                term = term + damp[:, e : e + 1]
            term = term * here
            for row in {f * ROWS + e * GROUP: 0, e * ROWS + f * GROUP: 0}:
                own_s[row : row + GROUP, :] += term

    column = iota((ROWS, 128), 1)
    for s in range(3):
        parts = []
        for f in range(CP):
            rows = slice(f * ROWS, (f + 1) * ROWS)
            part = own_s[rows, :] if s == 0 else other_s[rows, (s - 1) * 128 : s * 128]
            parts.append(pltpu.roll(part, f, 1))
        for t in range(CP):
            entry = column + t * 128
            entry = entry - 9 * ninth(entry)
            got = parts[0]
            for f in range(1, CP):
                got = jnp.where(entry == f, parts[f], got)
            for e in range(CP):
                turn_s[t, pl.ds(e, GROUP, stride=CP), :] = got[e * GROUP : (e + 1) * GROUP]
            lanes = slice(s * WIDTH + t * 128, s * WIDTH + (t + 1) * 128)
            if first:
                slab_ref[:, lanes] = turn_s[t, 0:ROWS, :]
            else:
                slab_ref[:, lanes] = before_ref[:, lanes] + turn_s[t, 0:ROWS, :]


def times_rows(slab_ref, line):
    acc = jnp.zeros((ROWS, 128), F32)
    for s in range(3):
        for t in range(CP):
            lanes = slice(s * WIDTH + t * 128, s * WIDTH + (t + 1) * 128)
            acc = acc + slab_ref[:, lanes] * line(s, t)
    return jnp.sum(acc, axis=1, keepdims=True)


def image_kernel(slab_ref, pair_ref, z1_ref, z2_ref, z3_ref, msg_ref, lines_ref):
    cluster = lax.axis_index("cams")
    most = pair_ref[20:21, :]
    for s, ref in enumerate((pair_ref, z1_ref, z2_ref, z3_ref)):
        chip = (cluster >> 1) + s & 3
        for h in range(2):
            lines_ref[2 * chip + (cluster + h & 1)] = ref[24 * h : 24 * h + 24, :]
            most = jnp.maximum(most, ref[24 * h + 20 : 24 * h + 21, :])
    lines_ref[0, 23:24, :] = most
    blocks = [cluster] + [pair_ref[row, 0].astype(jnp.int32) for row in (21, 22)]
    start = [lines_ref[c, 0:CP, :] / lines_ref[c, CP : 2 * CP, :] for c in blocks]
    image = times_rows(slab_ref, lambda s, t: start[s][t : t + 1])
    image = total(image * (iota((ROWS, 128), 1) == iota((ROWS, 128), 0)).astype(F32))
    msg_ref[...] = jnp.broadcast_to(image, msg_ref.shape)


def step_kernel(all_ref, slab_ref, lines_ref, msg_ref, vec_ref, d_s):
    cluster = lax.axis_index("cams")
    mine = lax.axis_index("pts") * NCL + cluster
    column = iota((128, WIDTH), 1)
    spread = dot_exact(all_ref[...], hot(column - ROWS * ((column * 911) >> 16) == iota((128, WIDTH), 0)))
    owner = (iota((NCL, WIDTH), 1) * 911) >> 16
    image = jnp.zeros((NCL, WIDTH), F32)
    for j in range(SHARDS):
        image = jnp.where(owner == j, spread[j * NCL : (j + 1) * NCL], image)

    def whole(x):
        return jnp.sum(total(x), axis=1, keepdims=True)

    def line(row):
        return jnp.concatenate([lines_ref[:, row + t, :] for t in range(CP)], axis=1)

    residual, diag = line(0), line(CP)
    own_diag = lines_ref[cluster, 19:20, :]
    own_diag = jnp.where(iota((1, 128), 1) < ROWS, own_diag, 1.0)
    own_residual = lines_ref[cluster, 18:19, :]
    own_image = all_ref[pl.ds(mine, 1), :]
    direction = residual / diag
    own_direction = own_residual / own_diag
    norm = whole(residual * direction)
    alpha = norm / whole(direction * image)
    residual = residual - alpha * image
    own_residual = own_residual - alpha * own_image
    precond = residual / diag
    norm_next = whole(residual * precond)
    ratio = norm_next / norm
    d_s[...] = precond + ratio * direction
    own = own_residual / own_diag + ratio * own_direction
    blocks = [cluster] + [lines_ref[cluster, row, 0].astype(jnp.int32) for row in (21, 22)]
    lines = [d_s[pl.ds(c, 1), :] for c in blocks]
    acc = times_rows(slab_ref, lambda s, t: lines[s][:, t * 128 : (t + 1) * 128])
    acc = total(acc * (iota((ROWS, 128), 0) == iota((ROWS, 128), 1)).astype(F32))
    msg_ref[...] = jnp.broadcast_to(whole(own * acc), msg_ref.shape)
    vec_ref[0:1, :] = alpha * own_direction
    vec_ref[1:2, :] = own
    vec_ref[2:3, :] = own_residual
    vec_ref[3:4, :] = acc
    vec_ref[4:5, :] = jnp.broadcast_to(norm_next, (1, 128))
    vec_ref[5:8, :] = jnp.zeros((3, 128), F32)


def finish_kernel(all_ref, vec_ref, solution_ref, residual_ref):
    alpha = vec_ref[4:5, :] / total(all_ref[...])
    solution_ref[...] = (vec_ref[0:1, :] + alpha * vec_ref[1:2, :])[:, :ROWS]
    residual_ref[...] = (vec_ref[2:3, :] - alpha * vec_ref[3:4, :])[:, :ROWS]


SMEM = pl.BlockSpec(memory_space=pltpu.SMEM)
VMEM = pl.BlockSpec(memory_space=pltpu.VMEM)


def call(kernel, n_smem, args, outs, scratch=(), cost=None):
    return pl.pallas_call(
        kernel,
        out_shape=[jax.ShapeDtypeStruct(x, jnp.int32 if len(x) == 1 else F32) for x in outs],
        in_specs=[SMEM] * n_smem + [VMEM] * (len(args) - n_smem),
        out_specs=[SMEM if len(x) == 1 else VMEM for x in outs],
        scratch_shapes=[pltpu.VMEM(x, F32) for x in scratch],
        compiler_params=PARAMS,
        cost_estimate=cost,
    )(*args)


def exchange(x, axes):
    return lax.all_to_all(x, axes, 0, 0, tiled=True)


def form_rows(recv, points, other):
    first = other.shape == (1, ROWS)
    scratch = ((CP * ROWS, CAMS_CL), (CP * ROWS, 2 * CAMS_CL), (CP, ROWS + 8, 128))
    return call(
        functools.partial(rows_kernel, first),
        0,
        (recv, points, other),
        [(ROWS, 3 * WIDTH)],
        scratch,
        pl.CostEstimate(flops=8 * 10**9, bytes_accessed=4 * 10**6, transcendentals=0),
    )[0]


def line_up(recv):
    return call(line_up_kernel, 0, (recv,), [(SHARDS + 3, 104, 128)])[0]


def share_vectors(own):
    other = lax.ppermute(own, "cams", [(i, i ^ 1) for i in range(NCL)])
    pair = jnp.concatenate([own, other], axis=0)
    moves = [[((i + 2 * s) % NCL, i) for i in range(NCL)] for s in range(1, 4)]
    return [pair] + [lax.ppermute(pair, "cams", move) for move in moves]


def body(cam_jac, pt_jac, resid, point_damping, obs_camera, members, partners, camera_damping):
    partners = partners.T
    points = (
        partners,
        jnp.transpose(cam_jac, (0, 2, 1, 3)),
        jnp.transpose(pt_jac, (0, 2, 1, 3)),
        resid,
        point_damping.reshape(P_SH // 128, 128),
        obs_camera,
        members[0],
        camera_damping,
    )

    everywhere = ("pts", "cams")

    def send(turn):
        scratch = ((FEAT, P_SH), (FEAT, MEM), (128, MEM), (40, MEM), (40, 128))
        kernel = functools.partial(pack_kernel, len(turn) > 0)
        packed = call(kernel, len(turn), turn + points, [(SHARDS, PAYLOAD, 128)], scratch)[0]
        return exchange(packed, "pts")

    recv = send(())
    vectors = share_vectors(call(sums_kernel, 0, (partners, recv), [(24, 128)])[0])
    slab = form_rows(recv, line_up(recv), camera_damping)

    def first_images(slab):
        outs = [(SHARDS * NCL, 128), (NCL, 24, 128)]
        msg, lines = call(image_kernel, 0, (slab, *vectors), outs)
        return exchange(msg, everywhere), lines

    images, lines = first_images(slab)
    most = lines[0, 23, 0].astype(jnp.int32)

    def more(slab, images):
        def again(state):
            turn, slab = state
            recv = send((turn[None],))
            return (turn + 1, form_rows(recv, line_up(recv), slab))

        slab = lax.while_loop(lambda state: state[0] * SLOTS < most, again, (jnp.int32(1), slab))[1]
        return slab, first_images(slab)[0]

    slab, images = lax.cond(most > SLOTS, more, lambda *so_far: so_far, slab, images)
    outs = [(SHARDS * NCL, 128), (8, 128)]
    msg, vec = call(step_kernel, 0, (images, slab, lines), outs, ((NCL, WIDTH),))
    outs = [(1, ROWS), (1, ROWS)]
    solution, residual = call(finish_kernel, 0, (exchange(msg, everywhere), vec), outs)
    return (slab[None], solution, residual)


def solution(mesh):
    in_specs = (
        P(None, None, None, "pts"),
        P(None, None, None, "pts"),
        P(None, None, "pts"),
        P("pts"),
        P(None, "pts"),
        P("pts", "cams", None),
        P(),
        P("cams", "pts"),
    )
    out_specs = (P("cams", "pts", None), P("cams", "pts"), P("cams", "pts"))
    return jax.shard_map(body, mesh=mesh, in_specs=in_specs, out_specs=out_specs, check_vma=False)
```

```python
import functools

import jax
import jax.numpy as jnp
from jax import lax
from jax.experimental import pallas as pl
from jax.experimental.pallas import tpu as pltpu
from jax.sharding import PartitionSpec as P

CP = 9
CAMS_CL = 128
NCL = 8
SHARDS = 16
P_SH = 2048
MEM = 512
ROWS = 72
GROUP = 8
WIDTH = CP * CAMS_CL
SLOTS = 96
SENT = 100
FEAT = 112
JROWS = 72
PAYLOAD = 96
CHUNK = 1024
PAIRS = [(e, f) for e in range(CP) for f in range(e, CP)]

BF16 = jnp.bfloat16
F32 = jnp.float32
PARAMS = pltpu.CompilerParams(vmem_limit_bytes=48 * 1024 * 1024)
NN = (((1,), (0,)), ((), ()))
NT = (((1,), (1,)), ((), ()))


def iota(shape, axis):
    return lax.broadcasted_iota(jnp.int32, shape, axis)


def ninth(value):
    return (value * 7282) >> 16


def split2(value):
    high = value.astype(BF16).astype(F32)
    return jnp.concatenate([high, value - high], axis=0).astype(BF16)


def dot(a, b, dims):
    return lax.dot_general(a, b, dims, preferred_element_type=F32)


def dot_exact(a, onehot):
    high = a.astype(BF16)
    rest = a - high.astype(F32)
    middle = rest.astype(BF16)
    low = (rest - middle.astype(F32)).astype(BF16)
    return dot(high, onehot, NN) + dot(middle, onehot, NN) + dot(low, onehot, NN)


def hot(condition):
    return condition.astype(F32).astype(BF16)


def total(x):
    return jnp.sum(x, axis=0, keepdims=True)


def partners_of(cluster, partners_ref):
    here = jnp.where(iota((2, NCL), 1) == cluster, partners_ref[...], 0)
    return jnp.sum(here.astype(F32), axis=1, keepdims=True)


def pack_kernel(later, *refs):
    offset = refs[0][0] * SLOTS if later else 0
    (partners_ref, cam_ref, pt_ref, resid_ref, damp_ref, ids_ref, members_ref, cam_damp_ref,
     out_ref, x_s, y_s, f_s, g_s, t_s) = refs[1:] if later else refs
    cluster = lax.axis_index("cams")
    block = lax.axis_index("pts")
    first_partner = partners_of(cluster, partners_ref)[0:1].astype(jnp.int32)

    def chunk(step, carry):
        at = pl.ds(pl.multiple_of(step * CHUNK, CHUNK), CHUNK)
        p0, p1, p2 = (jnp.concatenate([pt_ref[0, i, :, at], pt_ref[1, i, :, at]], axis=0) for i in range(3))
        res = jnp.concatenate([resid_ref[0, :, at], resid_ref[1, :, at]], axis=0)
        damp = jnp.concatenate([damp_ref[pl.ds(CHUNK // 128 * step + h, 1), :] for h in range(CHUNK // 128)], axis=1)
        i00 = 1.0 / jnp.sqrt(total(p0 * p0) + damp)
        l10 = total(p0 * p1) * i00
        l20 = total(p0 * p2) * i00
        i11 = 1.0 / jnp.sqrt(total(p1 * p1) + damp - l10 * l10)
        l21 = (total(p1 * p2) - l20 * l10) * i11
        i22 = 1.0 / jnp.sqrt(total(p2 * p2) + damp - l20 * l20 - l21 * l21)
        b0 = p0 * i00
        b1 = (p1 - l10 * b0) * i11
        b2 = (p2 - l20 * b0 - l21 * b1) * i22
        ids = ids_ref[:, at]
        swap = jnp.broadcast_to(ids[0:1] >> 7, (4, CHUNK)) != cluster

        def turn(x):
            return jnp.where(swap, jnp.concatenate([x[2:4], x[0:2]], axis=0), x)

        for a in range(2):
            for e in range(CP):
                row = (a * CP + e) * 4
                x_s[row : row + 4, at] = turn(cam_ref[a, e, :, at])
        for i, b in enumerate((b0, b1, b2)):
            for a in range(2):
                row = 72 + (2 * i + a) * 4
                x_s[row : row + 4, at] = turn(b[4 * a : 4 * a + 4])
        ids = turn(ids)
        far = (iota((4, CHUNK), 0) >= 2) & ((ids >> 7) != first_partner)
        x_s[96:100, at] = ((ids & 127) + jnp.where(far, CAMS_CL, 0)).astype(F32)
        for a in range(2):
            x_s[100 + 4 * a : 104 + 4 * a, at] = turn(res[4 * a : 4 * a + 4])
        w = [total(b * res) for b in (b0, b1, b2)]
        x_s[108:112, at] = jnp.concatenate(w + [jnp.zeros((1, CHUNK), F32)], axis=0)
        return carry

    lax.fori_loop(0, P_SH // CHUNK, chunk, 0)

    y = dot(split2(x_s[...]), hot(iota((P_SH, MEM), 0) == members_ref[...]), NN)
    y_s[...] = y[:FEAT] + y[FEAT:]

    def pair(row):
        return y_s[row : row + 2, :]

    jac = [[pair((a * CP + e) * 4) for e in range(CP)] for a in range(2)]
    scaled = [[pair(72 + (2 * i + a) * 4) for a in range(2)] for i in range(3)]
    res = [pair(100 + 4 * a) for a in range(2)]
    w = [y_s[108 + i : 109 + i, :] for i in range(3)]
    same = (y_s[96:97, :] == y_s[97:98, :]).astype(F32)
    f_s[90:128, :] = jnp.zeros((38, MEM), F32)
    g_s[36:40, :] = jnp.zeros((4, MEM), F32)
    for e in range(CP):
        j0, j1 = jac[0][e], jac[1][e]
        red = [scaled[i][0] * j0 + scaled[i][1] * j1 for i in range(3)]
        both = sum(r[0:1] * r[1:2] for r in red) * same
        g_s[2 * e : 2 * e + 2, :] = j0 * res[0] + j1 * res[1] - sum(red[i] * w[i] for i in range(3))
        g_s[18 + 2 * e : 20 + 2 * e, :] = j0 * j0 + j1 * j1 - sum(r * r for r in red) - both
    for n, (e, f) in enumerate(PAIRS):
        f_s[2 * n : 2 * n + 2, :] = jac[0][e] * jac[0][f] + jac[1][e] * jac[1][f]
    feats = f_s[...]
    high = feats.astype(BF16)
    low = (feats - high.astype(F32)).astype(BF16)
    sums = split2(g_s[...])
    hots = [hot(iota((CAMS_CL, MEM), 0).astype(F32) == y_s[96 + q : 97 + q, :]) for q in range(2)]
    camsum = [dot(hots[q], high, NT) + dot(hots[q], low, NT) for q in range(2)]
    camsum = jnp.where((iota((CAMS_CL, 128), 1) & 1) == 0, camsum[0], camsum[1])
    sums = [dot(sums, hots[q], NT) for q in range(2)]
    sums = [x[:40] + x[40:] for x in sums]
    t_s[...] = jnp.where((iota((40, CAMS_CL), 0) & 1) == 0, sums[0], sums[1])
    part = t_s[pl.ds(0, 18, stride=2), :] + t_s[pl.ds(1, 18, stride=2), :]
    lane = iota((ROWS, CAMS_CL), 0)
    spread = hot(iota((ROWS, CAMS_CL), 1) == block * GROUP + ninth(lane))
    lane = iota((18, ROWS), 1)
    damp = jnp.where(iota((18, ROWS), 0) - 9 == lane - 9 * ninth(lane), cam_damp_ref[...], 0.0)
    part = part + dot_exact(damp, spread)

    groups = [y_s[96 + q : 97 + q, :].astype(jnp.int32) >> 3 for q in range(2)]
    lanes = iota((SHARDS, MEM), 0)
    wanted = (lanes == groups[0]) | (lanes == groups[1])
    count = dot(hot(wanted), hot(iota((MEM, MEM), 0) <= iota((MEM, MEM), 1)), NN).astype(jnp.int32)
    slot = count - (offset + 1)
    slot = jnp.where(wanted & (slot < SLOTS), slot, -1)
    most = jnp.max(count, axis=1, keepdims=True)
    here = jnp.minimum(jnp.maximum(most - offset, 0), SLOTS).astype(F32)
    most = jnp.broadcast_to(jnp.max(most, axis=0, keepdims=True).astype(F32), (1, 128))
    feats = split2(y_s[...])
    lane = iota((128, 384), 1)
    flat = dot_exact(camsum, hot((iota((128, 384), 0) >> 1) == (lane >> 3)))
    flat = jnp.where((lane & 7) == (iota((128, 384), 0) & 7), flat, 0.0)
    flat = jnp.sum(flat.reshape(SHARDS, GROUP, 384), axis=1)
    lane = iota((SHARDS, 128), 1)
    tail = jnp.where((lane >> 3) == 13, here, jnp.where((lane >> 3) == 14, most, flat[:, 256:384]))
    tails = [pltpu.roll(tail, SLOTS - 32 * q, 1) if q < 3 else tail for q in range(4)]
    lane = iota((24, 128), 1)
    for j in range(0, SHARDS, 2):
        wants = jnp.concatenate(
            [jnp.broadcast_to(slot[j + h : j + h + 1], (128, MEM)) for h in range(2)], axis=0
        )
        sent = dot(feats, hot((iota((256, MEM), 0) & 127) == wants), NT)
        sent = sent[:FEAT] + sent[FEAT:]
        for h in range(2):
            to = j + h
            own = sent[:, h * 128 : (h + 1) * 128]
            scaled = own[JROWS : JROWS + 24]
            for third in range(3):
                rows = slice(24 * third, 24 * third + 24)
                out_ref[to, rows, :] = jnp.where(lane < SLOTS, own[rows], pltpu.roll(scaled, SLOTS - 32 * third, 1))
            beside = jnp.concatenate([tails[q][to : to + 1] for q in range(4)], axis=0)
            out_ref[to, 72:76, :] = jnp.where(lane[0:4] < SLOTS, own[96:100], beside)
            out_ref[to, 76:94, :] = part
            out_ref[to, 94:95, :] = flat[to : to + 1, 0:128]
            out_ref[to, 95:96, :] = flat[to : to + 1, 128:256]


def sums_kernel(partners_ref, recv_ref, out_ref):
    group = lax.axis_index("pts")
    tot = recv_ref[0, 72:96, :]
    most = tot
    for b in range(1, SHARDS):
        one = recv_ref[b, 72:96, :]
        tot = tot + one
        most = jnp.maximum(most, one)
    tot, most = tot[4:22], jnp.broadcast_to(most[3:4, 112:113], (1, 128))
    column = iota((CAMS_CL, WIDTH), 1)
    spread = hot(ninth(column) == iota((CAMS_CL, WIDTH), 0))
    column = iota((CP, WIDTH), 1)
    entry = column - 9 * ninth(column) == iota((CP, WIDTH), 0)
    lines = dot_exact(tot, spread)
    lane = iota((CAMS_CL, 128), 1)
    share = hot((iota((CAMS_CL, 128), 0) == group * GROUP + ninth(lane)) & (lane < ROWS))
    lane = iota((CP, 128), 1)
    entry_share = lane - 9 * ninth(lane) == iota((CP, 128), 0)
    share = dot_exact(tot, share)
    for k in range(2):
        line = total(jnp.where(entry, lines[CP * k : CP * (k + 1)], 0.0))
        for t in range(CP):
            out_ref[CP * k + t : CP * k + t + 1, :] = line[:, t * 128 : (t + 1) * 128]
        out_ref[18 + k : 19 + k, :] = total(jnp.where(entry_share, share[CP * k : CP * (k + 1)], 0.0))
    out_ref[20:21, :] = most
    partners = partners_of(lax.axis_index("cams"), partners_ref)
    out_ref[21:23, :] = jnp.broadcast_to(partners, (2, 128))
    out_ref[23:24, :] = jnp.zeros((1, 128), F32)


def line_up_kernel(recv_ref, buf_s):
    counts = [recv_ref[b, 75, 104].astype(jnp.int32) for b in range(SHARDS)]
    lane = iota((1, 128), 1)
    third = iota((24, 128), 1) >> 5
    at = jnp.int32(0)
    for b in range(SHARDS):
        shift = at & 127
        tile = at >> 7
        jac = recv_ref[b, 0:JROWS, :]
        scaled = [pltpu.roll(jac[24 * h : 24 * h + 24], 128 - SLOTS + 32 * h, 1) for h in range(3)]
        scaled = jnp.where(third == 0, scaled[0], jnp.where(third == 1, scaled[1], scaled[2]))
        filled = ((lane < shift + (SLOTS - 128)) | ((lane >= shift) & (lane < shift + SLOTS))).astype(F32)
        for row, rows, values in ((0, JROWS, jac), (72, 24, scaled), (96, 4, recv_ref[b, JROWS : JROWS + 4, :])):
            moved = pltpu.roll(values, shift, 1)
            moved = moved * filled
            mask = iota((rows, 128), 1) >= shift
            pltpu.store(buf_s.at[tile, row : row + rows, :], moved, mask=mask)
            buf_s[tile + 1, row : row + rows, :] = jnp.where(mask, 0.0, moved)
        at = at + counts[b]
    buf_s[SHARDS + 2, 0:1, :] = jnp.broadcast_to(at.astype(F32), (1, 128))


def rows_kernel(first, recv_ref, buf_s, *refs):
    if first:
        damp_ref, slab_ref, own_s, other_s, turn_s = refs
    else:
        before_ref, slab_ref, own_s, other_s, turn_s = refs
    group = lax.axis_index("pts")
    own_s[...] = jnp.zeros(own_s.shape, F32)
    other_s[...] = jnp.zeros(other_s.shape, F32)

    at = buf_s[SHARDS + 2, 0, 0].astype(jnp.int32)

    def chunk(tile, tiles):
        lanes = 128 * tiles

        def load(row, count):
            return jnp.concatenate([buf_s[tile + h, row : row + count, :] for h in range(tiles)], axis=1)

        numbers = load(96, 4).astype(jnp.int32)
        spots = [numbers[q : q + 1] for q in range(4)]
        masks = [(iota((GROUP, lanes), 0) == spots[q] - group * GROUP).astype(F32) for q in range(2)]
        scaled = [[load(72 + (2 * i + a) * 4, 4) for a in range(2)] for i in range(3)]
        red = [[] for i in range(3)]
        for e in range(CP):
            j0, j1 = load(e * 4, 4), load((CP + e) * 4, 4)
            for i in range(3):
                red[i].append(scaled[i][0] * j0 + scaled[i][1] * j1)
        left = [
            jnp.concatenate([masks[0] * red[i][e][0:1] + masks[1] * red[i][e][1:2] for e in range(CP)], axis=0)
            for i in range(3)
        ]
        for base, size, acc in ((0, CAMS_CL, own_s), (2, 2 * CAMS_CL, other_s)):
            sides = []
            hots = []
            for q in (base, base + 1):
                terms = [sum(left[i] * red[i][e][q : q + 1] for i in range(3)) for e in range(CP)]
                sides.append(split2(jnp.concatenate(terms, axis=0)))
                spot = (spots[q] & 128) + ((spots[q] * CP) & 127)
                hots.append(hot(iota((size, lanes), 0) == spot))
            got = dot(jnp.concatenate(sides, axis=1), jnp.concatenate(hots, axis=1), NT)
            acc[...] -= got[: CP * ROWS] + got[CP * ROWS :]

    def pair(step, carry):
        chunk(2 * step, 2)
        return carry

    tiles = (at + 127) >> 7
    lax.fori_loop(0, tiles >> 1, pair, 0)

    @pl.when((tiles & 1) == 1)
    def _():
        chunk(tiles - 1, 1)

    if first:
        lane = iota((ROWS, 128), 0)
        spread = hot(lane - 9 * ninth(lane) == iota((ROWS, 128), 1))
        damp = jnp.where(ninth(iota((GROUP, ROWS), 1)) == iota((GROUP, ROWS), 0), damp_ref[...], 0.0)
        damp = dot_exact(damp, spread)
        here = (group * GROUP + iota((GROUP, 128), 0)) * CP
        here = (iota((GROUP, 128), 1) == (here & 127)).astype(F32)
        sums = recv_ref[0, 72:96, :]
        for b in range(1, SHARDS):
            sums = sums + recv_ref[b, 72:96, :]
        lane = iota((1, 128), 1) >> 5
        tail = sums[3:4]
        for q in range(3):
            tail = jnp.where(lane == q, pltpu.roll(sums[q : q + 1], 128 - SLOTS + 32 * q, 1), tail)
        flat = jnp.concatenate([sums[22:23], sums[23:24], tail], axis=1)
        flat = jnp.where((iota((GROUP, 384), 1) & 7) == iota((GROUP, 384), 0), flat, 0.0)
        lane = iota((384, 128), 1)
        sums = dot_exact(flat, hot(((iota((384, 128), 0) >> 3) == lane) & (lane < len(PAIRS))))
        for n, (e, f) in enumerate(PAIRS):
            term = sums[:, n : n + 1]
            if e == f:
                term = term + damp[:, e : e + 1]
            term = term * here
            for row in {f * ROWS + e * GROUP: 0, e * ROWS + f * GROUP: 0}:
                own_s[row : row + GROUP, :] += term

    column = iota((ROWS, 128), 1)
    for s in range(3):
        parts = []
        for f in range(CP):
            rows = slice(f * ROWS, (f + 1) * ROWS)
            part = own_s[rows, :] if s == 0 else other_s[rows, (s - 1) * 128 : s * 128]
            parts.append(pltpu.roll(part, f, 1))
        for t in range(CP):
            entry = column + t * 128
            entry = entry - 9 * ninth(entry)
            got = parts[0]
            for f in range(1, CP):
                got = jnp.where(entry == f, parts[f], got)
            for e in range(CP):
                turn_s[t, pl.ds(e, GROUP, stride=CP), :] = got[e * GROUP : (e + 1) * GROUP]
            lanes = slice(s * WIDTH + t * 128, s * WIDTH + (t + 1) * 128)
            if first:
                slab_ref[:, lanes] = turn_s[t, 0:ROWS, :]
            else:
                slab_ref[:, lanes] = before_ref[:, lanes] + turn_s[t, 0:ROWS, :]


def times_rows(slab_ref, line):
    acc = jnp.zeros((ROWS, 128), F32)
    for s in range(3):
        for t in range(CP):
            lanes = slice(s * WIDTH + t * 128, s * WIDTH + (t + 1) * 128)
            acc = acc + slab_ref[:, lanes] * line(s, t)
    return jnp.sum(acc, axis=1, keepdims=True)


def image_kernel(slab_ref, pair_ref, z1_ref, z2_ref, z3_ref, msg_ref, lines_ref):
    cluster = lax.axis_index("cams")
    most = pair_ref[20:21, :]
    for s, ref in enumerate((pair_ref, z1_ref, z2_ref, z3_ref)):
        chip = (cluster >> 1) + s & 3
        for h in range(2):
            lines_ref[2 * chip + (cluster + h & 1)] = ref[24 * h : 24 * h + 24, :]
            most = jnp.maximum(most, ref[24 * h + 20 : 24 * h + 21, :])
    lines_ref[0, 23:24, :] = most
    blocks = [cluster] + [pair_ref[row, 0].astype(jnp.int32) for row in (21, 22)]
    start = [lines_ref[c, 0:CP, :] / lines_ref[c, CP : 2 * CP, :] for c in blocks]
    image = times_rows(slab_ref, lambda s, t: start[s][t : t + 1])
    image = total(image * (iota((ROWS, 128), 1) == iota((ROWS, 128), 0)).astype(F32))
    msg_ref[...] = jnp.broadcast_to(image, msg_ref.shape)


def step_kernel(all_ref, slab_ref, lines_ref, msg_ref, vec_ref, d_s):
    cluster = lax.axis_index("cams")
    mine = lax.axis_index("pts") * NCL + cluster
    column = iota((128, WIDTH), 1)
    spread = dot_exact(all_ref[...], hot(column - ROWS * ((column * 911) >> 16) == iota((128, WIDTH), 0)))
    owner = (iota((NCL, WIDTH), 1) * 911) >> 16
    image = jnp.zeros((NCL, WIDTH), F32)
    for j in range(SHARDS):
        image = jnp.where(owner == j, spread[j * NCL : (j + 1) * NCL], image)

    def whole(x):
        return jnp.sum(total(x), axis=1, keepdims=True)

    def line(row):
        return jnp.concatenate([lines_ref[:, row + t, :] for t in range(CP)], axis=1)

    residual, diag = line(0), line(CP)
    own_diag = lines_ref[cluster, 19:20, :]
    own_diag = jnp.where(iota((1, 128), 1) < ROWS, own_diag, 1.0)
    own_residual = lines_ref[cluster, 18:19, :]
    own_image = all_ref[pl.ds(mine, 1), :]
    direction = residual / diag
    own_direction = own_residual / own_diag
    norm = whole(residual * direction)
    alpha = norm / whole(direction * image)
    residual = residual - alpha * image
    own_residual = own_residual - alpha * own_image
    precond = residual / diag
    norm_next = whole(residual * precond)
    ratio = norm_next / norm
    d_s[...] = precond + ratio * direction
    own = own_residual / own_diag + ratio * own_direction
    blocks = [cluster] + [lines_ref[cluster, row, 0].astype(jnp.int32) for row in (21, 22)]
    lines = [d_s[pl.ds(c, 1), :] for c in blocks]
    acc = times_rows(slab_ref, lambda s, t: lines[s][:, t * 128 : (t + 1) * 128])
    acc = total(acc * (iota((ROWS, 128), 0) == iota((ROWS, 128), 1)).astype(F32))
    msg_ref[...] = jnp.broadcast_to(whole(own * acc), msg_ref.shape)
    vec_ref[0:1, :] = alpha * own_direction
    vec_ref[1:2, :] = own
    vec_ref[2:3, :] = own_residual
    vec_ref[3:4, :] = acc
    vec_ref[4:5, :] = jnp.broadcast_to(norm_next, (1, 128))
    vec_ref[5:8, :] = jnp.zeros((3, 128), F32)


def finish_kernel(all_ref, vec_ref, solution_ref, residual_ref):
    alpha = vec_ref[4:5, :] / total(all_ref[...])
    solution_ref[...] = (vec_ref[0:1, :] + alpha * vec_ref[1:2, :])[:, :ROWS]
    residual_ref[...] = (vec_ref[2:3, :] - alpha * vec_ref[3:4, :])[:, :ROWS]


SMEM = pl.BlockSpec(memory_space=pltpu.SMEM)
VMEM = pl.BlockSpec(memory_space=pltpu.VMEM)


def call(kernel, n_smem, args, outs, scratch=(), cost=None):
    return pl.pallas_call(
        kernel,
        out_shape=[jax.ShapeDtypeStruct(x, jnp.int32 if len(x) == 1 else F32) for x in outs],
        in_specs=[SMEM] * n_smem + [VMEM] * (len(args) - n_smem),
        out_specs=[SMEM if len(x) == 1 else VMEM for x in outs],
        scratch_shapes=[pltpu.VMEM(x, F32) for x in scratch],
        compiler_params=PARAMS,
        cost_estimate=cost,
    )(*args)


def exchange(x, axes):
    return lax.all_to_all(x, axes, 0, 0, tiled=True)


def form_rows(recv, points, other):
    first = other.shape == (1, ROWS)
    scratch = ((CP * ROWS, CAMS_CL), (CP * ROWS, 2 * CAMS_CL), (CP, ROWS + 8, 128))
    return call(
        functools.partial(rows_kernel, first),
        0,
        (recv, points, other),
        [(ROWS, 3 * WIDTH)],
        scratch,
        pl.CostEstimate(flops=8 * 10**9, bytes_accessed=4 * 10**6, transcendentals=0),
    )[0]


def line_up(recv):
    return call(line_up_kernel, 0, (recv,), [(SHARDS + 3, 104, 128)])[0]


def share_vectors(own):
    other = lax.ppermute(own, "cams", [(i, i ^ 1) for i in range(NCL)])
    pair = jnp.concatenate([own, other], axis=0)
    moves = [[((i + 2 * s) % NCL, i) for i in range(NCL)] for s in range(1, 4)]
    return [pair] + [lax.ppermute(pair, "cams", move) for move in moves]


def body(cam_jac, pt_jac, resid, point_damping, obs_camera, members, partners, camera_damping):
    partners = partners.T
    points = (
        partners,
        jnp.transpose(cam_jac, (0, 2, 1, 3)),
        jnp.transpose(pt_jac, (0, 2, 1, 3)),
        resid,
        point_damping.reshape(P_SH // 128, 128),
        obs_camera,
        members[0],
        camera_damping,
    )

    everywhere = ("pts", "cams")

    def send(turn):
        scratch = ((FEAT, P_SH), (FEAT, MEM), (128, MEM), (40, MEM), (40, 128))
        kernel = functools.partial(pack_kernel, len(turn) > 0)
        packed = call(kernel, len(turn), turn + points, [(SHARDS, PAYLOAD, 128)], scratch)[0]
        return exchange(packed, "pts")

    recv = send(())
    vectors = share_vectors(call(sums_kernel, 0, (partners, recv), [(24, 128)])[0])
    slab = form_rows(recv, line_up(recv), camera_damping)

    def first_images(slab):
        outs = [(SHARDS * NCL, 128), (NCL, 24, 128)]
        msg, lines = call(image_kernel, 0, (slab, *vectors), outs)
        return exchange(msg, everywhere), lines

    images, lines = first_images(slab)
    most = lines[0, 23, 0].astype(jnp.int32)

    def more(slab, images):
        def again(state):
            turn, slab = state
            recv = send((turn[None],))
            return (turn + 1, form_rows(recv, line_up(recv), slab))

        slab = lax.while_loop(lambda state: state[0] * SLOTS < most, again, (jnp.int32(1), slab))[1]
        return slab, first_images(slab)[0]

    slab, images = lax.cond(most > SLOTS, more, lambda *so_far: so_far, slab, images)
    outs = [(SHARDS * NCL, 128), (8, 128)]
    msg, vec = call(step_kernel, 0, (images, slab, lines), outs, ((NCL, WIDTH),))
    outs = [(1, ROWS), (1, ROWS)]
    solution, residual = call(finish_kernel, 0, (exchange(msg, everywhere), vec), outs)
    return (slab[None], solution, residual)


def solution(mesh):
    in_specs = (
        P(None, None, None, "pts"),
        P(None, None, None, "pts"),
        P(None, None, "pts"),
        P("pts"),
        P(None, "pts"),
        P("pts", "cams", None),
        P(),
        P("cams", "pts"),
    )
    out_specs = (P("cams", "pts", None), P("cams", "pts"), P("cams", "pts"))
    return jax.shard_map(body, mesh=mesh, in_specs=in_specs, out_specs=out_specs, check_vma=False)
```

```python
import functools

import jax
import jax.numpy as jnp
from jax import lax
from jax.experimental import pallas as pl
from jax.experimental.pallas import tpu as pltpu
from jax.sharding import PartitionSpec as P

CP = 9
CAMS_CL = 128
NCL = 8
SHARDS = 16
P_SH = 2048
MEM = 512
ROWS = 72
GROUP = 8
WIDTH = CP * CAMS_CL
SLOTS = 96
SENT = 100
FEAT = 112
JROWS = 72
PAYLOAD = 96
CHUNK = 256
PAIRS = [(e, f) for e in range(CP) for f in range(e, CP)]

BF16 = jnp.bfloat16
F32 = jnp.float32
PARAMS = pltpu.CompilerParams(vmem_limit_bytes=48 * 1024 * 1024)
NN = (((1,), (0,)), ((), ()))
NT = (((1,), (1,)), ((), ()))


def iota(shape, axis):
    return lax.broadcasted_iota(jnp.int32, shape, axis)


def ninth(value):
    return (value * 7282) >> 16


def split2(value):
    high = value.astype(BF16).astype(F32)
    return jnp.concatenate([high, value - high], axis=0).astype(BF16)


def dot(a, b, dims):
    return lax.dot_general(a, b, dims, preferred_element_type=F32)


def dot_exact(a, onehot):
    high = a.astype(BF16)
    rest = a - high.astype(F32)
    middle = rest.astype(BF16)
    low = (rest - middle.astype(F32)).astype(BF16)
    return dot(high, onehot, NN) + dot(middle, onehot, NN) + dot(low, onehot, NN)


def hot(condition):
    return condition.astype(F32).astype(BF16)


def total(x):
    return jnp.sum(x, axis=0, keepdims=True)


def partners_of(cluster, partners_ref):
    here = jnp.where(iota((2, NCL), 1) == cluster, partners_ref[...], 0)
    return jnp.sum(here.astype(F32), axis=1, keepdims=True)


def pack_kernel(later, *refs):
    offset = refs[0][0] * SLOTS if later else 0
    (partners_ref, cam_ref, pt_ref, resid_ref, damp_ref, ids_ref, members_ref, cam_damp_ref,
     out_ref, x_s, y_s, f_s, g_s, t_s) = refs[1:] if later else refs
    cluster = lax.axis_index("cams")
    block = lax.axis_index("pts")
    first_partner = partners_of(cluster, partners_ref)[0:1].astype(jnp.int32)

    def chunk(step, carry):
        at = pl.ds(pl.multiple_of(step * CHUNK, CHUNK), CHUNK)
        p0, p1, p2 = (jnp.concatenate([pt_ref[0, i, :, at], pt_ref[1, i, :, at]], axis=0) for i in range(3))
        res = jnp.concatenate([resid_ref[0, :, at], resid_ref[1, :, at]], axis=0)
        damp = jnp.concatenate([damp_ref[pl.ds(2 * step + h, 1), :] for h in range(2)], axis=1)
        i00 = 1.0 / jnp.sqrt(total(p0 * p0) + damp)
        l10 = total(p0 * p1) * i00
        l20 = total(p0 * p2) * i00
        i11 = 1.0 / jnp.sqrt(total(p1 * p1) + damp - l10 * l10)
        l21 = (total(p1 * p2) - l20 * l10) * i11
        i22 = 1.0 / jnp.sqrt(total(p2 * p2) + damp - l20 * l20 - l21 * l21)
        b0 = p0 * i00
        b1 = (p1 - l10 * b0) * i11
        b2 = (p2 - l20 * b0 - l21 * b1) * i22
        ids = ids_ref[:, at]
        swap = jnp.broadcast_to(ids[0:1] >> 7, (4, CHUNK)) != cluster

        def turn(x):
            return jnp.where(swap, jnp.concatenate([x[2:4], x[0:2]], axis=0), x)

        for a in range(2):
            for e in range(CP):
                row = (a * CP + e) * 4
                x_s[row : row + 4, at] = turn(cam_ref[a, e, :, at])
        for i, b in enumerate((b0, b1, b2)):
            for a in range(2):
                row = 72 + (2 * i + a) * 4
                x_s[row : row + 4, at] = turn(b[4 * a : 4 * a + 4])
        ids = turn(ids)
        far = (iota((4, CHUNK), 0) >= 2) & ((ids >> 7) != first_partner)
        x_s[96:100, at] = ((ids & 127) + jnp.where(far, CAMS_CL, 0)).astype(F32)
        for a in range(2):
            x_s[100 + 4 * a : 104 + 4 * a, at] = turn(res[4 * a : 4 * a + 4])
        w = [total(b * res) for b in (b0, b1, b2)]
        x_s[108:112, at] = jnp.concatenate(w + [jnp.zeros((1, CHUNK), F32)], axis=0)
        return carry

    lax.fori_loop(0, P_SH // CHUNK, chunk, 0)

    y = dot(split2(x_s[...]), hot(iota((P_SH, MEM), 0) == members_ref[...]), NN)
    y_s[...] = y[:FEAT] + y[FEAT:]

    def pair(row):
        return y_s[row : row + 2, :]

    jac = [[pair((a * CP + e) * 4) for e in range(CP)] for a in range(2)]
    scaled = [[pair(72 + (2 * i + a) * 4) for a in range(2)] for i in range(3)]
    res = [pair(100 + 4 * a) for a in range(2)]
    w = [y_s[108 + i : 109 + i, :] for i in range(3)]
    same = (y_s[96:97, :] == y_s[97:98, :]).astype(F32)
    f_s[90:128, :] = jnp.zeros((38, MEM), F32)
    g_s[36:40, :] = jnp.zeros((4, MEM), F32)
    for e in range(CP):
        j0, j1 = jac[0][e], jac[1][e]
        red = [scaled[i][0] * j0 + scaled[i][1] * j1 for i in range(3)]
        both = sum(r[0:1] * r[1:2] for r in red) * same
        g_s[2 * e : 2 * e + 2, :] = j0 * res[0] + j1 * res[1] - sum(red[i] * w[i] for i in range(3))
        g_s[18 + 2 * e : 20 + 2 * e, :] = j0 * j0 + j1 * j1 - sum(r * r for r in red) - both
    for n, (e, f) in enumerate(PAIRS):
        f_s[2 * n : 2 * n + 2, :] = jac[0][e] * jac[0][f] + jac[1][e] * jac[1][f]
    feats = f_s[...]
    high = feats.astype(BF16)
    low = (feats - high.astype(F32)).astype(BF16)
    sums = split2(g_s[...])
    hots = [hot(iota((CAMS_CL, MEM), 0).astype(F32) == y_s[96 + q : 97 + q, :]) for q in range(2)]
    camsum = [dot(hots[q], high, NT) + dot(hots[q], low, NT) for q in range(2)]
    camsum = jnp.where((iota((CAMS_CL, 128), 1) & 1) == 0, camsum[0], camsum[1])
    sums = [dot(sums, hots[q], NT) for q in range(2)]
    sums = [x[:40] + x[40:] for x in sums]
    t_s[...] = jnp.where((iota((40, CAMS_CL), 0) & 1) == 0, sums[0], sums[1])
    part = t_s[pl.ds(0, 18, stride=2), :] + t_s[pl.ds(1, 18, stride=2), :]
    lane = iota((ROWS, CAMS_CL), 0)
    spread = hot(iota((ROWS, CAMS_CL), 1) == block * GROUP + ninth(lane))
    lane = iota((18, ROWS), 1)
    damp = jnp.where(iota((18, ROWS), 0) - 9 == lane - 9 * ninth(lane), cam_damp_ref[...], 0.0)
    part = part + dot_exact(damp, spread)

    groups = [y_s[96 + q : 97 + q, :].astype(jnp.int32) >> 3 for q in range(2)]
    lanes = iota((SHARDS, MEM), 0)
    wanted = (lanes == groups[0]) | (lanes == groups[1])
    count = dot(hot(wanted), hot(iota((MEM, MEM), 0) <= iota((MEM, MEM), 1)), NN).astype(jnp.int32)
    slot = count - (offset + 1)
    slot = jnp.where(wanted & (slot < SLOTS), slot, -1)
    most = jnp.max(count, axis=1, keepdims=True)
    here = jnp.minimum(jnp.maximum(most - offset, 0), SLOTS).astype(F32)
    most = jnp.broadcast_to(jnp.max(most, axis=0, keepdims=True).astype(F32), (1, 128))
    feats = split2(y_s[...])
    lane = iota((128, 384), 1)
    flat = dot_exact(camsum, hot((iota((128, 384), 0) >> 1) == (lane >> 3)))
    flat = jnp.where((lane & 7) == (iota((128, 384), 0) & 7), flat, 0.0)
    flat = jnp.sum(flat.reshape(SHARDS, GROUP, 384), axis=1)
    lane = iota((SHARDS, 128), 1)
    tail = jnp.where((lane >> 3) == 13, here, jnp.where((lane >> 3) == 14, most, flat[:, 256:384]))
    tails = [pltpu.roll(tail, SLOTS - 32 * q, 1) if q < 3 else tail for q in range(4)]
    lane = iota((24, 128), 1)
    for j in range(0, SHARDS, 2):
        wants = jnp.concatenate(
            [jnp.broadcast_to(slot[j + h : j + h + 1], (128, MEM)) for h in range(2)], axis=0
        )
        sent = dot(feats, hot((iota((256, MEM), 0) & 127) == wants), NT)
        sent = sent[:FEAT] + sent[FEAT:]
        for h in range(2):
            to = j + h
            own = sent[:, h * 128 : (h + 1) * 128]
            scaled = own[JROWS : JROWS + 24]
            for third in range(3):
                rows = slice(24 * third, 24 * third + 24)
                out_ref[to, rows, :] = jnp.where(lane < SLOTS, own[rows], pltpu.roll(scaled, SLOTS - 32 * third, 1))
            beside = jnp.concatenate([tails[q][to : to + 1] for q in range(4)], axis=0)
            out_ref[to, 72:76, :] = jnp.where(lane[0:4] < SLOTS, own[96:100], beside)
            out_ref[to, 76:94, :] = part
            out_ref[to, 94:95, :] = flat[to : to + 1, 0:128]
            out_ref[to, 95:96, :] = flat[to : to + 1, 128:256]


def sums_kernel(partners_ref, recv_ref, out_ref):
    group = lax.axis_index("pts")
    tot = recv_ref[0, 72:96, :]
    most = tot
    for b in range(1, SHARDS):
        one = recv_ref[b, 72:96, :]
        tot = tot + one
        most = jnp.maximum(most, one)
    tot, most = tot[4:22], jnp.broadcast_to(most[3:4, 112:113], (1, 128))
    column = iota((CAMS_CL, WIDTH), 1)
    spread = hot(ninth(column) == iota((CAMS_CL, WIDTH), 0))
    column = iota((CP, WIDTH), 1)
    entry = column - 9 * ninth(column) == iota((CP, WIDTH), 0)
    lines = dot_exact(tot, spread)
    lane = iota((CAMS_CL, 128), 1)
    share = hot((iota((CAMS_CL, 128), 0) == group * GROUP + ninth(lane)) & (lane < ROWS))
    lane = iota((CP, 128), 1)
    entry_share = lane - 9 * ninth(lane) == iota((CP, 128), 0)
    share = dot_exact(tot, share)
    for k in range(2):
        line = total(jnp.where(entry, lines[CP * k : CP * (k + 1)], 0.0))
        for t in range(CP):
            out_ref[CP * k + t : CP * k + t + 1, :] = line[:, t * 128 : (t + 1) * 128]
        out_ref[18 + k : 19 + k, :] = total(jnp.where(entry_share, share[CP * k : CP * (k + 1)], 0.0))
    out_ref[20:21, :] = most
    partners = partners_of(lax.axis_index("cams"), partners_ref)
    out_ref[21:23, :] = jnp.broadcast_to(partners, (2, 128))
    out_ref[23:24, :] = jnp.zeros((1, 128), F32)


def line_up_kernel(recv_ref, buf_s):
    counts = [recv_ref[b, 75, 104].astype(jnp.int32) for b in range(SHARDS)]
    lane = iota((1, 128), 1)
    third = iota((24, 128), 1) >> 5
    at = jnp.int32(0)
    for b in range(SHARDS):
        shift = at & 127
        tile = at >> 7
        jac = recv_ref[b, 0:JROWS, :]
        scaled = [pltpu.roll(jac[24 * h : 24 * h + 24], 128 - SLOTS + 32 * h, 1) for h in range(3)]
        scaled = jnp.where(third == 0, scaled[0], jnp.where(third == 1, scaled[1], scaled[2]))
        filled = ((lane < shift + (SLOTS - 128)) | ((lane >= shift) & (lane < shift + SLOTS))).astype(F32)
        for row, rows, values in ((0, JROWS, jac), (72, 24, scaled), (96, 4, recv_ref[b, JROWS : JROWS + 4, :])):
            moved = pltpu.roll(values, shift, 1)
            moved = moved * filled
            mask = iota((rows, 128), 1) >= shift
            pltpu.store(buf_s.at[tile, row : row + rows, :], moved, mask=mask)
            buf_s[tile + 1, row : row + rows, :] = jnp.where(mask, 0.0, moved)
        at = at + counts[b]
    buf_s[SHARDS + 2, 0:1, :] = jnp.broadcast_to(at.astype(F32), (1, 128))


def rows_kernel(first, recv_ref, buf_s, *refs):
    if first:
        damp_ref, slab_ref, own_s, other_s, turn_s = refs
    else:
        before_ref, slab_ref, own_s, other_s, turn_s = refs
    group = lax.axis_index("pts")
    own_s[...] = jnp.zeros(own_s.shape, F32)
    other_s[...] = jnp.zeros(other_s.shape, F32)

    at = buf_s[SHARDS + 2, 0, 0].astype(jnp.int32)

    def chunk(tile, tiles):
        lanes = 128 * tiles

        def load(row, count):
            return jnp.concatenate([buf_s[tile + h, row : row + count, :] for h in range(tiles)], axis=1)

        numbers = load(96, 4).astype(jnp.int32)
        spots = [numbers[q : q + 1] for q in range(4)]
        masks = [(iota((GROUP, lanes), 0) == spots[q] - group * GROUP).astype(F32) for q in range(2)]
        scaled = [[load(72 + (2 * i + a) * 4, 4) for a in range(2)] for i in range(3)]
        red = [[] for i in range(3)]
        for e in range(CP):
            j0, j1 = load(e * 4, 4), load((CP + e) * 4, 4)
            for i in range(3):
                red[i].append(scaled[i][0] * j0 + scaled[i][1] * j1)
        left = [
            jnp.concatenate([masks[0] * red[i][e][0:1] + masks[1] * red[i][e][1:2] for e in range(CP)], axis=0)
            for i in range(3)
        ]
        for base, size, acc in ((0, CAMS_CL, own_s), (2, 2 * CAMS_CL, other_s)):
            sides = []
            hots = []
            for q in (base, base + 1):
                terms = [sum(left[i] * red[i][e][q : q + 1] for i in range(3)) for e in range(CP)]
                sides.append(split2(jnp.concatenate(terms, axis=0)))
                spot = (spots[q] & 128) + ((spots[q] * CP) & 127)
                hots.append(hot(iota((size, lanes), 0) == spot))
            got = dot(jnp.concatenate(sides, axis=1), jnp.concatenate(hots, axis=1), NT)
            acc[...] -= got[: CP * ROWS] + got[CP * ROWS :]

    def pair(step, carry):
        chunk(2 * step, 2)
        return carry

    tiles = (at + 127) >> 7
    lax.fori_loop(0, tiles >> 1, pair, 0)

    @pl.when((tiles & 1) == 1)
    def _():
        chunk(tiles - 1, 1)

    if first:
        lane = iota((ROWS, 128), 0)
        spread = hot(lane - 9 * ninth(lane) == iota((ROWS, 128), 1))
        damp = jnp.where(ninth(iota((GROUP, ROWS), 1)) == iota((GROUP, ROWS), 0), damp_ref[...], 0.0)
        damp = dot_exact(damp, spread)
        here = (group * GROUP + iota((GROUP, 128), 0)) * CP
        here = (iota((GROUP, 128), 1) == (here & 127)).astype(F32)
        sums = recv_ref[0, 72:96, :]
        for b in range(1, SHARDS):
            sums = sums + recv_ref[b, 72:96, :]
        lane = iota((1, 128), 1) >> 5
        tail = sums[3:4]
        for q in range(3):
            tail = jnp.where(lane == q, pltpu.roll(sums[q : q + 1], 128 - SLOTS + 32 * q, 1), tail)
        flat = jnp.concatenate([sums[22:23], sums[23:24], tail], axis=1)
        flat = jnp.where((iota((GROUP, 384), 1) & 7) == iota((GROUP, 384), 0), flat, 0.0)
        lane = iota((384, 128), 1)
        sums = dot_exact(flat, hot(((iota((384, 128), 0) >> 3) == lane) & (lane < len(PAIRS))))
        for n, (e, f) in enumerate(PAIRS):
            term = sums[:, n : n + 1]
            if e == f:
                term = term + damp[:, e : e + 1]
            term = term * here
            for row in {f * ROWS + e * GROUP: 0, e * ROWS + f * GROUP: 0}:
                own_s[row : row + GROUP, :] += term

    column = iota((ROWS, 128), 1)
    for s in range(3):
        parts = []
        for f in range(CP):
            rows = slice(f * ROWS, (f + 1) * ROWS)
            part = own_s[rows, :] if s == 0 else other_s[rows, (s - 1) * 128 : s * 128]
            parts.append(pltpu.roll(part, f, 1))
        for t in range(CP):
            entry = column + t * 128
            entry = entry - 9 * ninth(entry)
            got = parts[0]
            for f in range(1, CP):
                got = jnp.where(entry == f, parts[f], got)
            for e in range(CP):
                turn_s[t, pl.ds(e, GROUP, stride=CP), :] = got[e * GROUP : (e + 1) * GROUP]
            lanes = slice(s * WIDTH + t * 128, s * WIDTH + (t + 1) * 128)
            if first:
                slab_ref[:, lanes] = turn_s[t, 0:ROWS, :]
            else:
                slab_ref[:, lanes] = before_ref[:, lanes] + turn_s[t, 0:ROWS, :]


def times_rows(slab_ref, line):
    acc = jnp.zeros((ROWS, 128), F32)
    for s in range(3):
        for t in range(CP):
            lanes = slice(s * WIDTH + t * 128, s * WIDTH + (t + 1) * 128)
            acc = acc + slab_ref[:, lanes] * line(s, t)
    return jnp.sum(acc, axis=1, keepdims=True)


def image_kernel(slab_ref, pair_ref, z1_ref, z2_ref, z3_ref, msg_ref, lines_ref):
    cluster = lax.axis_index("cams")
    most = pair_ref[20:21, :]
    for s, ref in enumerate((pair_ref, z1_ref, z2_ref, z3_ref)):
        chip = (cluster >> 1) + s & 3
        for h in range(2):
            lines_ref[2 * chip + (cluster + h & 1)] = ref[24 * h : 24 * h + 24, :]
            most = jnp.maximum(most, ref[24 * h + 20 : 24 * h + 21, :])
    lines_ref[0, 23:24, :] = most
    blocks = [cluster] + [pair_ref[row, 0].astype(jnp.int32) for row in (21, 22)]
    start = [lines_ref[c, 0:CP, :] / lines_ref[c, CP : 2 * CP, :] for c in blocks]
    image = times_rows(slab_ref, lambda s, t: start[s][t : t + 1])
    image = total(image * (iota((ROWS, 128), 1) == iota((ROWS, 128), 0)).astype(F32))
    msg_ref[...] = jnp.broadcast_to(image, msg_ref.shape)


def step_kernel(all_ref, slab_ref, lines_ref, msg_ref, vec_ref, d_s):
    cluster = lax.axis_index("cams")
    mine = lax.axis_index("pts") * NCL + cluster
    column = iota((128, WIDTH), 1)
    spread = dot_exact(all_ref[...], hot(column - ROWS * ((column * 911) >> 16) == iota((128, WIDTH), 0)))
    owner = (iota((NCL, WIDTH), 1) * 911) >> 16
    image = jnp.zeros((NCL, WIDTH), F32)
    for j in range(SHARDS):
        image = jnp.where(owner == j, spread[j * NCL : (j + 1) * NCL], image)

    def whole(x):
        return jnp.sum(total(x), axis=1, keepdims=True)

    def line(row):
        return jnp.concatenate([lines_ref[:, row + t, :] for t in range(CP)], axis=1)

    residual, diag = line(0), line(CP)
    own_diag = lines_ref[cluster, 19:20, :]
    own_diag = jnp.where(iota((1, 128), 1) < ROWS, own_diag, 1.0)
    own_residual = lines_ref[cluster, 18:19, :]
    own_image = all_ref[pl.ds(mine, 1), :]
    direction = residual / diag
    own_direction = own_residual / own_diag
    norm = whole(residual * direction)
    alpha = norm / whole(direction * image)
    residual = residual - alpha * image
    own_residual = own_residual - alpha * own_image
    precond = residual / diag
    norm_next = whole(residual * precond)
    ratio = norm_next / norm
    d_s[...] = precond + ratio * direction
    own = own_residual / own_diag + ratio * own_direction
    blocks = [cluster] + [lines_ref[cluster, row, 0].astype(jnp.int32) for row in (21, 22)]
    lines = [d_s[pl.ds(c, 1), :] for c in blocks]
    acc = times_rows(slab_ref, lambda s, t: lines[s][:, t * 128 : (t + 1) * 128])
    acc = total(acc * (iota((ROWS, 128), 0) == iota((ROWS, 128), 1)).astype(F32))
    msg_ref[...] = jnp.broadcast_to(whole(own * acc), msg_ref.shape)
    vec_ref[0:1, :] = alpha * own_direction
    vec_ref[1:2, :] = own
    vec_ref[2:3, :] = own_residual
    vec_ref[3:4, :] = acc
    vec_ref[4:5, :] = jnp.broadcast_to(norm_next, (1, 128))
    vec_ref[5:8, :] = jnp.zeros((3, 128), F32)


def finish_kernel(all_ref, vec_ref, solution_ref, residual_ref):
    alpha = vec_ref[4:5, :] / total(all_ref[...])
    solution_ref[...] = (vec_ref[0:1, :] + alpha * vec_ref[1:2, :])[:, :ROWS]
    residual_ref[...] = (vec_ref[2:3, :] - alpha * vec_ref[3:4, :])[:, :ROWS]


SMEM = pl.BlockSpec(memory_space=pltpu.SMEM)
VMEM = pl.BlockSpec(memory_space=pltpu.VMEM)


def call(kernel, n_smem, args, outs, scratch=(), cost=None):
    return pl.pallas_call(
        kernel,
        out_shape=[jax.ShapeDtypeStruct(x, jnp.int32 if len(x) == 1 else F32) for x in outs],
        in_specs=[SMEM] * n_smem + [VMEM] * (len(args) - n_smem),
        out_specs=[SMEM if len(x) == 1 else VMEM for x in outs],
        scratch_shapes=[pltpu.VMEM(x, F32) for x in scratch],
        compiler_params=PARAMS,
        cost_estimate=cost,
    )(*args)


def exchange(x, axes):
    return lax.all_to_all(x, axes, 0, 0, tiled=True)


def form_rows(recv, points, other):
    first = other.shape == (1, ROWS)
    scratch = ((CP * ROWS, CAMS_CL), (CP * ROWS, 2 * CAMS_CL), (CP, ROWS + 8, 128))
    return call(
        functools.partial(rows_kernel, first),
        0,
        (recv, points, other),
        [(ROWS, 3 * WIDTH)],
        scratch,
        pl.CostEstimate(flops=8 * 10**9, bytes_accessed=4 * 10**6, transcendentals=0),
    )[0]


def line_up(recv):
    return call(line_up_kernel, 0, (recv,), [(SHARDS + 3, 104, 128)])[0]


def share_vectors(own):
    other = lax.ppermute(own, "cams", [(i, i ^ 1) for i in range(NCL)])
    pair = jnp.concatenate([own, other], axis=0)
    moves = {s: [((i + 2 * s) % NCL, i) for i in range(NCL)] for s in (2, 1, 3)}
    got = {s: lax.ppermute(pair, "cams", move) for s, move in moves.items()}
    return [pair, got[1], got[2], got[3]]


def body(cam_jac, pt_jac, resid, point_damping, obs_camera, members, partners, camera_damping):
    partners = partners.T
    points = (
        partners,
        jnp.transpose(cam_jac, (0, 2, 1, 3)),
        jnp.transpose(pt_jac, (0, 2, 1, 3)),
        resid,
        point_damping.reshape(P_SH // 128, 128),
        obs_camera,
        members[0],
        camera_damping,
    )

    everywhere = ("pts", "cams")

    def send(turn):
        scratch = ((FEAT, P_SH), (FEAT, MEM), (128, MEM), (40, MEM), (40, 128))
        kernel = functools.partial(pack_kernel, len(turn) > 0)
        packed = call(kernel, len(turn), turn + points, [(SHARDS, PAYLOAD, 128)], scratch)[0]
        return exchange(packed, "pts")

    recv = send(())
    vectors = share_vectors(call(sums_kernel, 0, (partners, recv), [(24, 128)])[0])
    slab = form_rows(recv, line_up(recv), camera_damping)

    def first_images(slab):
        outs = [(SHARDS * NCL, 128), (NCL, 24, 128)]
        msg, lines = call(image_kernel, 0, (slab, *vectors), outs)
        return exchange(msg, everywhere), lines

    images, lines = first_images(slab)
    most = lines[0, 23, 0].astype(jnp.int32)

    def more(slab, images):
        def again(state):
            turn, slab = state
            recv = send((turn[None],))
            return (turn + 1, form_rows(recv, line_up(recv), slab))

        slab = lax.while_loop(lambda state: state[0] * SLOTS < most, again, (jnp.int32(1), slab))[1]
        return slab, first_images(slab)[0]

    slab, images = lax.cond(most > SLOTS, more, lambda *so_far: so_far, slab, images)
    outs = [(SHARDS * NCL, 128), (8, 128)]
    msg, vec = call(step_kernel, 0, (images, slab, lines), outs, ((NCL, WIDTH),))
    outs = [(1, ROWS), (1, ROWS)]
    solution, residual = call(finish_kernel, 0, (exchange(msg, everywhere), vec), outs)
    return (slab[None], solution, residual)


def solution(mesh):
    in_specs = (
        P(None, None, None, "pts"),
        P(None, None, None, "pts"),
        P(None, None, "pts"),
        P("pts"),
        P(None, "pts"),
        P("pts", "cams", None),
        P(),
        P("cams", "pts"),
    )
    out_specs = (P("cams", "pts", None), P("cams", "pts"), P("cams", "pts"))
    return jax.shard_map(body, mesh=mesh, in_specs=in_specs, out_specs=out_specs, check_vma=False)
```
